32 devices in a mesh: order: 8 (over z, x), lat: 4 (over y, core).
Axes of the slice: x: 2, y: 2, z: 4, core: 2. Of those that a mesh axis runs over, the one named last changes fastest.
Arguments:
- position: float32 [16, 2, 64, 2160], P('order', None, None, 'lat'), may hold values from -6 to 6
- residual: float32 [16, 2, 64, 2160], P('order', None, None, 'lat'), as said below
- direction: float32 [16, 2, 64, 2160], P('order', None, None, 'lat'), as said below
- legendre: float32 [16, 2160, 256], P('order', None, 'lat'), may hold values from -0.125 to 0.125
- order_of: int32 [16], replicated, may hold values from 0 to 2025, as said below
- class_idx: int32 [256, 4320], P(('lat', 'order')), may hold values from 0 to 15
- land: int32 [256, 4320], P(('lat', 'order')), may hold values 0 or 1
- class_weight: float32 [16, 2], replicated, may hold values from 0.2 to 5
- damping: float32 [2160], P('lat'), may hold values from 0.05 to 0.5
Outputs:
- new_position: float32 [16, 2, 64, 2160], P('order', None, None, 'lat')
- new_residual: float32 [16, 2, 64, 2160], P('order', None, None, 'lat')
- new_direction: float32 [16, 2, 64, 2160], P('order', None, None, 'lat')
The draws below stay inside these ranges and needn't reach their ends.
Inputs may be any that keep to these rules, and one draw needn't show every extreme that they name: `order_of`: distinct multiples of 135: each of 0, 135, ..., 135 * (16 - 1) appears exactly once. `residual`: real-valued and not zero. `direction`: real-valued and not zero.
All inputs are finite; a program needn't handle non-finite values. No bound on the sum of `land` on one device may be relied on, other than what follows from the above.
Results may differ from the reference program's by a relative error of at most 0.000058.
Values sent between devices are 32-bit elements; how exact they have to be, the bound alone decides.
No kernel may reach another device: no remote copies, remote signals or barrier semaphores. Data moves between devices by JAX's collectives and lax.ppermute only.
A program may use at most 128 MiB of HBM per device.

```python
import math
import jax
import jax.numpy as jnp
from jax import lax

NDEG = 2160
NLON = 4320
CLASSES = 16
SAMPLES = 64
R_DEV = 8
ORDERS = 16
STRIDE = 135
NLAT = 256


def draw_order_of(key, part):
    shuffled = jax.random.permutation(jax.random.fold_in(key, 11), ORDERS).astype(jnp.int32)
    return (shuffled * STRIDE).astype(jnp.int32)


def coefficient_field(key):
    k_base, k_rows, k_cols = jax.random.split(key, 3)
    slot_pos = jnp.arange(ORDERS, dtype=jnp.float32) / max(ORDERS - 1, 1)
    degree_pos = jnp.arange(NDEG, dtype=jnp.float32) / (NDEG - 1)
    row_scale = 3.0 ** slot_pos * 10.0 ** jax.random.uniform(k_rows, (ORDERS,), dtype=jnp.float32)
    col_scale = 3.0 ** degree_pos * 10.0 ** jax.random.uniform(k_cols, (NDEG,), dtype=jnp.float32)
    full_shape = (ORDERS, 2, SAMPLES, NDEG)
    base_draw = jax.random.normal(k_base, full_shape, dtype=jnp.float32)
    return base_draw * row_scale[:, None, None, None] * col_scale[None, None, None, :] / 30.0


def draw_residual(key, part):
    return coefficient_field(jax.random.fold_in(key, 21))


def draw_direction(key, part):
    return coefficient_field(jax.random.fold_in(key, 37))


def place_ends(array, own_key, least, high):
    longest = array.shape.index(max(array.shape))
    spots = []
    for shift in (0, 1):
        where = [jax.random.randint(jax.random.fold_in(own_key, axis), (), 0, length) for axis, length in enumerate(array.shape)]
        where[longest] = (where[longest] + shift) % array.shape[longest]
        spots.append(tuple(where))
    return array.at[spots[0]].set(least).at[spots[1]].set(high)


def block_scale(own_key, extent, pieces, least, top_value):
    factor_of, own = 1.0, jax.random.fold_in(own_key, 6)
    for dim, blocks in pieces:
        steps = jnp.exp(jax.random.uniform(jax.random.fold_in(own, dim), (blocks,), jnp.float32, least / len(pieces), top_value / len(pieces)))
        factor_of = factor_of * jnp.repeat(steps, extent[dim] // blocks).reshape([-1 if axis == dim else 1 for axis in range(len(extent))])
    return factor_of


def centred(key, extent, scale, limit, shards=(), held_as=jnp.bfloat16):
    result = jax.random.normal(key, extent, jnp.float32) * scale
    if len(shards) > 0:
        result = block_scale(key, extent, shards, -0.22, 0.18) * result
    return jnp.clip(result, min=-limit, max=limit).astype(held_as)


def setup_inputs(seed: int = 0) -> dict:
    splits = jax.random.split(jax.random.key(seed), 10)
    return {
        "position": centred(splits[0], (ORDERS, 2, SAMPLES, NDEG), 1.0, 6.0, ((0, 8), (3, 4)), jnp.float32),
        "residual": draw_residual(jax.random.fold_in(splits[9], 71), 0),
        "direction": draw_direction(jax.random.fold_in(splits[9], 71), 0),
        "legendre": centred(splits[3], (ORDERS, NDEG, NLAT), NDEG ** -0.5, 0.125, ((0, 8), (2, 4)), jnp.float32),
        "order_of": draw_order_of(jax.random.fold_in(splits[9], 71), 0),
        "class_idx": place_ends(jax.random.randint(splits[5], (NLAT, NLON), 0, CLASSES), jax.random.fold_in(splits[5], 1), 0, CLASSES - 1).astype(jnp.int32),
        "land": place_ends((jax.random.randint(splits[6], (NLAT, NLON), 0, 10) < 3).astype(jnp.int32), jax.random.fold_in(splits[6], 1), 0, 1),
        "class_weight": jnp.clip(jnp.exp(jax.random.uniform(splits[7], (CLASSES, 2), jnp.float32, math.log(0.2), math.log(5.0))), 0.2, 5.0),
        "damping": jnp.clip(jnp.exp(math.log(0.5) - 2.3025851 * jax.random.uniform(splits[8], (NDEG,), jnp.float32) ** block_scale(splits[8], (NDEG,), ((0, 4),), -0.2, 0.2)), 0.05, 0.5),
    }


def tables(order_of, longitudes):
    longitude = jnp.arange(longitudes, dtype=jnp.int32)
    phases = (order_of[:, None] * longitude[None, :]) % longitudes
    angles = phases.astype(jnp.float32) * (2.0 * math.pi / longitudes)
    return jnp.stack([jnp.cos(angles), jnp.sin(angles)])


def sample_sums(product):
    return jnp.sum(product, axis=(0, 1, 3))


def reference(position, residual, direction, legendre, order_of, class_idx, land, class_weight, damping):
    highest = lax.Precision.HIGHEST
    degrees = jnp.arange(NDEG, dtype=jnp.int32)
    in_triangle = (degrees[None, :] >= order_of[:, None]).astype(jnp.float32)[:, None, None, :]
    pos_m = position * in_triangle
    res_m = residual * in_triangle
    dir_m = direction * in_triangle
    synthesis = jnp.einsum("mskd,mdt->tmsk", dir_m, legendre, precision=highest)
    harmonic = tables(order_of, NLON)
    by_class = class_weight[class_idx]
    weight_grid = jnp.where(land == 1, by_class[:, :, 1], by_class[:, :, 0])
    count_blocks = NLAT // R_DEV

    def per_block(operands):
        rows_in, weights_in = operands
        surface = jnp.einsum("rmsk,sml->rkl", rows_in, harmonic, precision=highest)
        weighted = surface * weights_in[:, None, :]
        return jnp.einsum("rkl,sml->rmsk", weighted, harmonic, precision=highest) * (2.0 / NLON)

    spectra = lax.map(per_block, (synthesis.reshape(count_blocks, R_DEV, ORDERS, 2, SAMPLES),
                                  weight_grid.reshape(count_blocks, R_DEV, NLON)))
    spectra = spectra.reshape(NLAT, ORDERS, 2, SAMPLES)
    summed = jnp.einsum("tmsk,mdt->mskd", spectra, legendre, precision=highest)
    applied = (summed + damping[None, None, None, :] * dir_m) * in_triangle
    norm_before = sample_sums(res_m * res_m)
    curvature = sample_sums(dir_m * applied)
    step_size = (norm_before / curvature)[None, None, :, None]
    new_position = pos_m + step_size * dir_m
    new_residual = res_m - step_size * applied
    norm_after = sample_sums(new_residual * new_residual)
    ratio_new = (norm_after / norm_before)[None, None, :, None]
    new_direction = new_residual + ratio_new * dir_m
    return (new_position, new_residual, new_direction)
```

```python
import functools
import math

import jax
import jax.numpy as jnp
import numpy as np
from jax import lax
from jax.experimental import pallas as pl
from jax.experimental.pallas import tpu as pltpu
from jax.sharding import Mesh
from jax.sharding import PartitionSpec as P

LANES = 128
HIGHEST = lax.Precision.HIGHEST
VMEM_LIMIT = 48 * 1024 * 1024
WHOLE = pl.BlockSpec(memory_space=pltpu.VMEM)
SCALARS = pl.BlockSpec(memory_space=pltpu.SMEM)
PARAMS = pltpu.CompilerParams(vmem_limit_bytes=VMEM_LIMIT)


def split_bf16(x):
    hi = x.astype(jnp.bfloat16)
    lo = (x - hi.astype(jnp.float32)).astype(jnp.bfloat16)
    return hi, lo


def dot3(a, b, dims):
    (ah, al), (bh, bl) = a, b
    dot = functools.partial(
        lax.dot_general, dimension_numbers=(dims, ((), ())), preferred_element_type=jnp.float32
    )
    return dot(ah, bh) + (dot(ah, bl) + dot(al, bh))


def call(kernel, out_shape, in_specs, flops, moved):
    return pl.pallas_call(
        kernel,
        out_shape=out_shape,
        in_specs=in_specs,
        out_specs=jax.tree.map(lambda _: WHOLE, out_shape),
        compiler_params=PARAMS,
        cost_estimate=pl.CostEstimate(flops=flops, bytes_accessed=moved, transcendentals=0),
    )


def place_direction(geo, scal, *refs):
    parts, (hi_ref, lo_ref) = refs[: geo.inner], refs[geo.inner :]
    m_local, sin_cos, samples, width = parts[0].shape
    window = hi_ref.shape[2]
    rows = sin_cos * samples
    degree = scal[geo.window_start] + lax.broadcasted_iota(jnp.int32, (rows, window), 1)
    for m in range(m_local):
        valid = degree >= scal[geo.orders + m]
        total = None
        for shift, part in enumerate(parts):
            block = part[m].reshape(rows, width)
            block = jnp.concatenate([block, jnp.zeros((rows, window - width), jnp.float32)], axis=1)
            block = pltpu.roll(block, scal[geo.places + shift], 1)
            total = block if total is None else total + block
        total = jnp.where(valid, total, 0.0)
        hi, lo = split_bf16(total)
        hi_ref[m] = hi
        lo_ref[m] = lo


def synthesise_own(leg_ref, hi_ref, lo_ref, out_ref):
    for m in range(leg_ref.shape[0]):
        leg = split_bf16(leg_ref[m])
        out_ref[m] = dot3(leg, (hi_ref[m], lo_ref[m]), ((1,), (1,)))


def synthesise_rest(geo, scal, own_ref, *refs):
    legs, (hi_ref, lo_ref, out_ref) = refs[:-3], refs[-3:]
    rows = out_ref.shape[3]
    for m in range(own_ref.shape[0]):
        for shift in range(geo.outer):
            if shift == 0:
                part = own_ref[m]
            else:
                leg = split_bf16(legs[shift - 1][m])
                part = dot3(leg, (hi_ref[m], lo_ref[m]), ((1,), (1,)))
            a = scal[geo.outer_of + shift]
            for o in range(out_ref.shape[0]):
                out_ref[o, a, m] = part[o * rows : (o + 1) * rows]


def weight_tables(longitudes, period, class_ref, land_ref, value_ref, basis_ref, out_ref):
    classes = class_ref[...]
    on_land = land_ref[...] == 1
    weight = jnp.zeros(classes.shape, jnp.float32)
    for c in range(value_ref.shape[0]):
        value = jnp.where(on_land, value_ref[c, 1], value_ref[c, 0])
        weight = jnp.where(classes == c, value, weight)
    rows = classes.shape[0]
    folded = jnp.zeros((rows, LANES), jnp.float32)
    for start in range(0, longitudes, LANES):
        piece = weight[:, start : min(start + LANES, longitudes)]
        if piece.shape[1] < LANES:
            piece = jnp.concatenate(
                [piece, jnp.zeros((rows, LANES - piece.shape[1]), jnp.float32)], axis=1
            )
        folded = folded + piece
    moments = lax.dot_general(
        folded,
        basis_ref[...],
        (((1,), (0,)), ((), ())),
        precision=HIGHEST,
        preferred_element_type=jnp.float32,
    )
    lane = lax.broadcasted_iota(jnp.int32, (rows, LANES), 1)
    sign = jnp.where(lane < LANES // 2, 1.0, -1.0)
    count = out_ref.shape[1]
    for n in range(count):
        even = jnp.broadcast_to(moments[:, n : n + 1], (rows, LANES))
        odd = jnp.broadcast_to(moments[:, count + n : count + n + 1], (rows, LANES))
        out_ref[0, n] = even
        out_ref[1, n] = sign * even
        out_ref[2, n] = odd
        out_ref[3, n] = sign * odd


def grid_rows(geo, slot, recv_ref, table_ref, out_ref, plain, swapped, done):
    orders = plain.shape[0]
    m_local = recv_ref.shape[1]
    for m in range(orders):
        o, i = divmod(m, m_local)
        total = recv_ref[o * geo.outer, i]
        for a in range(1, geo.outer):
            total = total + recv_ref[o * geo.outer + a, i]
        at = slot[m]
        plain[at] = total
        swapped[at] = pltpu.roll(total, LANES // 2, 1)
    for i in range(orders):
        total = None
        for j in range(orders):
            cos_part = table_ref[0, abs(i - j)] + table_ref[1, i + j]
            if i >= j:
                sin_part = table_ref[2, i + j] - table_ref[3, i - j]
            else:
                sin_part = table_ref[2, i + j] + table_ref[3, j - i]
            term = cos_part * plain[j] + sin_part * swapped[j]
            total = term if total is None else total + term
        done[i] = total
    copies = geo.outer * geo.inner
    for m in range(orders):
        o, i = divmod(m, m_local)
        value = done[slot[m]]
        for c in range(copies):
            out_ref[o * copies + c, i] = value


def split_block(geo, scal, *refs):
    here, (sib_ref, hi_ref, lo_ref) = refs[:-3], refs[-3:]
    width = hi_ref.shape[2]
    start = pl.multiple_of(scal[geo.block_start], LANES)
    for m in range(hi_ref.shape[0]):
        at = 0
        for b in range(geo.inner):
            for a in range(geo.outer):
                if b == 0:
                    block = here[a][m, :, pl.ds(start, width)]
                else:
                    block = sib_ref[b - 1, a, m]
                rows = block.shape[0]
                hi, lo = split_bf16(block)
                hi_ref[m, at : at + rows] = hi
                lo_ref[m, at : at + rows] = lo
                at += rows


def own_mask(geo, scal, m, rows, width):
    degree = scal[geo.own_start] + lax.broadcasted_iota(jnp.int32, (rows, width), 1)
    return degree >= scal[geo.orders + m]


def project(geo, scal, recv_ref, hi_ref, lo_ref, dir_ref, res_ref, damp_ref, app_ref, sums_ref):
    m_local, sin_cos, samples, width = dir_ref.shape
    window = hi_ref.shape[2]
    copies = geo.outer * geo.inner
    order_devices = recv_ref.shape[0] // copies
    damping = damp_ref[...]
    rows = sin_cos * samples
    back = window - scal[geo.block_offset]
    sums = [None] * 4
    for m in range(m_local):
        tiles = []
        for b in range(geo.inner):
            for a in range(geo.outer):
                band = scal[geo.outer_of + a] * geo.inner + scal[geo.inner_of + b]
                for o in range(order_devices):
                    tiles.append(recv_ref[o * copies + band, m])
        spectra = split_bf16(jnp.concatenate(tiles, axis=0))
        summed = dot3(spectra, (hi_ref[m], lo_ref[m]), ((0,), (0,)))
        summed = pltpu.roll(summed, back, 1)[:, :width]
        valid = own_mask(geo, scal, m, samples, width)
        for s in range(sin_cos):
            direction = jnp.where(valid, dir_ref[m, s], 0.0)
            residual = jnp.where(valid, res_ref[m, s], 0.0)
            part = summed[s * samples : (s + 1) * samples]
            applied = jnp.where(valid, part + damping * direction, 0.0)
            app_ref[m, s] = applied
            terms = (
                residual * residual,
                direction * applied,
                residual * applied,
                applied * applied,
            )
            sums = [t if old is None else old + t for old, t in zip(sums, terms)]
    stacked = jnp.concatenate(sums, axis=0)
    totals = jnp.sum(stacked, axis=1, keepdims=True)
    count = totals.shape[0]
    row = lax.broadcasted_iota(jnp.int32, (count, count), 0)
    column = lax.broadcasted_iota(jnp.int32, (count, count), 1)
    line = jnp.sum(jnp.where(row == column, totals, 0.0), axis=0, keepdims=True)
    for device in range(sums_ref.shape[0]):
        sums_ref[device] = line


def update(geo, scal, sums_ref, app_ref, pos_ref, dir_ref, res_ref, pos_out, res_out, dir_out):
    m_local, sin_cos, samples, width = dir_ref.shape
    totals = jnp.sum(sums_ref[...], axis=0)
    before, curvature, cross, square = [
        totals[:, i * samples : (i + 1) * samples] for i in range(4)
    ]
    step_row = before / curvature
    after = before - 2.0 * step_row * cross + step_row * step_row * square
    ratio_row = after / before
    row = lax.broadcasted_iota(jnp.int32, (samples, samples), 0)
    column = lax.broadcasted_iota(jnp.int32, (samples, samples), 1)
    diagonal = row == column
    step = jnp.sum(jnp.where(diagonal, step_row, 0.0), axis=1, keepdims=True)
    ratio = jnp.sum(jnp.where(diagonal, ratio_row, 0.0), axis=1, keepdims=True)
    for m in range(m_local):
        valid = own_mask(geo, scal, m, samples, width)
        for s in range(sin_cos):
            direction = jnp.where(valid, dir_ref[m, s], 0.0)
            residual = jnp.where(valid, res_ref[m, s], 0.0)
            position = jnp.where(valid, pos_ref[m, s], 0.0)
            new_residual = residual - step * app_ref[m, s]
            pos_out[m, s] = position + step * direction
            res_out[m, s] = new_residual
            dir_out[m, s] = new_residual + ratio * direction


class Geometry:
    def __init__(self, outer, inner, degrees, m_local):
        self.outer, self.inner = outer, inner
        bands = outer * inner
        block = degrees // bands
        pair = degrees // outer

        def down(x):
            return x // LANES * LANES

        def up(x):
            return -(-x // LANES) * LANES

        self.window_starts = [down(a * pair) for a in range(outer)]
        self.window = max(up((a + 1) * pair) - s for a, s in enumerate(self.window_starts))
        places = [
            [(a * inner + b) * block - self.window_starts[a] for b in range(inner)]
            for a in range(outer)
        ]
        starts = [[down(p) for p in row] for row in places]
        self.block_window = max(
            up(p + block) - s for prow, srow in zip(places, starts) for p, s in zip(prow, srow)
        )
        self.block_starts = [
            [min(s, self.window - self.block_window) for s in row] for row in starts
        ]
        self.window_start, self.block_start, self.block_offset, self.own_start = 0, 1, 2, 3
        self.places = 4
        self.outer_of = self.places + inner
        self.inner_of = self.outer_of + outer
        self.orders = self.inner_of + inner
        rows = []
        for a in range(outer):
            for b in range(inner):
                row = [
                    self.window_starts[a],
                    self.block_starts[a][b],
                    places[a][b] - self.block_starts[a][b],
                    (a * inner + b) * block,
                ]
                row += [places[a][(b - s) % inner] for s in range(inner)]
                row += [(a - s) % outer for s in range(outer)]
                row += [(b - s) % inner for s in range(inner)]
                rows.append(row)
        self.table = np.array(rows, np.int32)


def pick(index, choices):
    result = choices[-1]
    for i in range(len(choices) - 2, -1, -1):
        result = jnp.where(index == i, choices[i], result)
    return result


def rotate(x, axis, size, shift):
    return lax.ppermute(x, axis, [(i, (i + shift) % size) for i in range(size)])


def plain_grid(geo, grid_in, order_of, class_idx, land, class_weight, period):
    order_devices = grid_in.shape[0] // geo.outer
    m_local, rows, width = grid_in.shape[1:]
    orders = order_devices * m_local
    longitudes = class_idx.shape[1]
    stacked = grid_in.reshape(order_devices, geo.outer, m_local, rows, 2, width // 2)
    stacked = jnp.sum(stacked, axis=1).reshape(orders, rows, 2, width // 2)
    phases = order_of[:, None] * jnp.arange(period, dtype=jnp.int32)[None, :] % longitudes
    angles = phases.astype(jnp.float32) * (2.0 * math.pi / longitudes)
    harmonic = jnp.stack([jnp.cos(angles), jnp.sin(angles)])
    surface = jnp.einsum("mrsk,smp->rkp", stacked, harmonic, precision=HIGHEST)
    onehot = class_idx[:, :, None] == jnp.arange(class_weight.shape[0], dtype=jnp.int32)
    by_class = jnp.dot(onehot.astype(jnp.float32), class_weight, precision=HIGHEST)
    weight = jnp.where(land == 1, by_class[:, :, 1], by_class[:, :, 0])
    folded = jnp.sum(weight.reshape(rows, longitudes // period, period), axis=1)
    weighted = surface * folded[:, None, :]
    spectra = jnp.einsum("rkp,smp->mrsk", weighted, harmonic, precision=HIGHEST)
    spectra = (spectra * (2.0 / longitudes)).reshape(order_devices, 1, m_local, rows, width)
    copies = geo.outer * geo.inner
    spectra = jnp.broadcast_to(spectra, (order_devices, copies, m_local, rows, width))
    return spectra.reshape(order_devices * copies, m_local, rows, width)


def shards(
    outer,
    inner,
    position,
    residual,
    direction,
    legendre,
    order_of,
    class_idx,
    land,
    class_weight,
    damping,
):
    m_local, sin_cos, samples, deg_local = position.shape
    degrees, band_rows = legendre.shape[1:]
    rows_here, longitudes = class_idx.shape
    orders = order_of.shape[0]
    order_devices = orders // m_local
    devices = order_devices * outer * inner
    line = sin_cos * samples
    geo = Geometry(outer, inner, degrees, m_local)
    a = lax.axis_index("outer")
    b = lax.axis_index("inner")
    order_index = lax.axis_index("order")
    my_orders = lax.dynamic_slice_in_dim(order_of, order_index * m_local, m_local)
    where = lax.dynamic_index_in_dim(jnp.asarray(geo.table), a * inner + b, 0, keepdims=False)
    scal = jnp.concatenate([where, my_orders])

    by_row = jnp.transpose(legendre, (0, 2, 1))
    end = max(s + geo.window for s in geo.window_starts)
    by_row = jnp.pad(by_row, ((0, 0), (0, 0), (0, max(0, end - degrees))))
    windows = [by_row[:, :, s : s + geo.window] for s in geo.window_starts]
    received = [
        rotate(pick((a + s) % outer, windows), "outer", outer, s) for s in range(1, outer)
    ]
    siblings = [rotate(direction, "inner", inner, s) for s in range(1, inner)]
    own_window = pick(a, windows)

    pair = jax.ShapeDtypeStruct((m_local, line, geo.window), jnp.bfloat16)
    dir_hi, dir_lo = call(
        functools.partial(place_direction, geo),
        (pair, pair),
        [SCALARS] + [WHOLE] * inner,
        4 * m_local * line * geo.window,
        8 * m_local * line * geo.window,
    )(scal, direction, *siblings)
    own_flops = 6 * m_local * line * geo.window * band_rows
    own_rows = call(
        synthesise_own,
        jax.ShapeDtypeStruct((m_local, band_rows, line), jnp.float32),
        [WHOLE] * 3,
        own_flops,
        4 * m_local * (line + band_rows) * geo.window,
    )(own_window, dir_hi, dir_lo)

    stride = longitudes // (2 * orders)
    period = longitudes // stride if longitudes % stride == 0 else longitudes
    small = orders <= 32 and LANES % period == 0 and line == LANES and longitudes % period == 0
    if small:
        count = 2 * orders
        n = np.arange(count)[None, :]
        p = np.arange(LANES)[:, None]
        angle = 2.0 * math.pi * ((n * p) % period) / period
        basis = np.zeros((LANES, -(-2 * count // LANES) * LANES), np.float32)
        basis[:, :count] = np.cos(angle) / longitudes
        basis[:, count : 2 * count] = np.sin(angle) / longitudes
        tables = call(
            functools.partial(weight_tables, longitudes, period),
            jax.ShapeDtypeStruct((4, count, rows_here, LANES), jnp.float32),
            [WHOLE, WHOLE, SCALARS, WHOLE],
            100 * rows_here * longitudes,
            8 * rows_here * longitudes,
        )(class_idx, land, class_weight, jnp.asarray(basis))

    to_rows = call(
        functools.partial(synthesise_rest, geo),
        jax.ShapeDtypeStruct((order_devices, outer, m_local, rows_here, line), jnp.float32),
        [SCALARS] + [WHOLE] * (outer + 2),
        own_flops * (outer - 1),
        4 * m_local * (line + band_rows) * geo.window,
    )(scal, own_rows, *received, dir_hi, dir_lo)
    grid_in = lax.all_to_all(
        to_rows.reshape(order_devices * outer, m_local, rows_here, line),
        ("order", "outer"),
        split_axis=0,
        concat_axis=0,
        tiled=True,
    )

    def block_of(array, s):
        per_inner = [
            [array[..., t : t + geo.block_window] for t in (geo.block_starts[i][j] for i in range(outer))]
            for j in range(inner)
        ]
        target = (b + s) % inner
        choices = []
        for j in range(inner):
            starts = {geo.block_starts[i][j] for i in range(outer)}
            choices.append(per_inner[j][0] if len(starts) == 1 else pick(a, per_inner[j]))
        return pick(target, choices)

    here = [own_window] + received
    from_inner = [
        rotate(jnp.stack([block_of(x, s) for x in here]), "inner", inner, s)
        for s in range(1, inner)
    ]
    block = jax.ShapeDtypeStruct((m_local, inner * outer * band_rows, geo.block_window), jnp.bfloat16)
    leg_hi, leg_lo = call(
        functools.partial(split_block, geo),
        (block, block),
        [SCALARS] + [WHOLE] * (outer + 1),
        4 * m_local * inner * outer * band_rows * geo.block_window,
        8 * m_local * inner * outer * band_rows * geo.block_window,
    )(scal, *here, jnp.stack(from_inner))

    if small:
        to_orders = pl.pallas_call(
            functools.partial(grid_rows, geo),
            out_shape=jax.ShapeDtypeStruct((devices, m_local, rows_here, line), jnp.float32),
            in_specs=[SCALARS, WHOLE, WHOLE],
            out_specs=WHOLE,
            scratch_shapes=[pltpu.VMEM((orders, rows_here, line), jnp.float32)] * 3,
            compiler_params=PARAMS,
            cost_estimate=pl.CostEstimate(
                flops=6 * orders * orders * rows_here * line,
                bytes_accessed=8 * orders * rows_here * line,
                transcendentals=0,
            ),
        )(order_of // stride, grid_in, tables)
    else:
        to_orders = plain_grid(geo, grid_in, order_of, class_idx, land, class_weight, period)
    spectra = lax.all_to_all(
        to_orders, ("order", "outer", "inner"), split_axis=0, concat_axis=0, tiled=True
    )
    coefficients = jax.ShapeDtypeStruct(position.shape, jnp.float32)
    applied, sums = call(
        functools.partial(project, geo),
        (coefficients, jax.ShapeDtypeStruct((devices, 1, 4 * samples), jnp.float32)),
        [SCALARS] + [WHOLE] * 6,
        6 * m_local * line * geo.block_window * band_rows * outer * inner,
        16 * m_local * line * deg_local,
    )(scal, spectra, leg_hi, leg_lo, direction, residual, damping[None, :])
    sums = lax.all_to_all(
        sums, ("order", "outer", "inner"), split_axis=0, concat_axis=0, tiled=True
    )
    return call(
        functools.partial(update, geo),
        (coefficients,) * 3,
        [SCALARS] + [WHOLE] * 5,
        10 * m_local * line * deg_local,
        28 * m_local * line * deg_local,
    )(scal, sums, applied, position, direction, residual)


def solution(mesh):
    order_devices, bands = mesh.shape["order"], mesh.shape["lat"]
    outer = 2 if bands % 2 == 0 else 1
    inner = bands // outer
    split = Mesh(mesh.devices.reshape(order_devices, outer, inner), ("order", "outer", "inner"))
    lat = ("outer", "inner")
    coefficients = P("order", None, None, lat)
    grid = P(("outer", "inner", "order"), None)
    return jax.shard_map(
        functools.partial(shards, outer, inner),
        mesh=split,
        in_specs=(
            coefficients,
            coefficients,
            coefficients,
            P("order", None, lat),
            P(),
            grid,
            grid,
            P(),
            P(lat),
        ),
        out_specs=(coefficients,) * 3,
        check_vma=False,
    )
```

```python
import functools
import math

import jax
import jax.numpy as jnp
import numpy as np
from jax import lax
from jax.experimental import pallas as pl
from jax.experimental.pallas import tpu as pltpu
from jax.sharding import Mesh
from jax.sharding import PartitionSpec as P

LANES = 128
HIGHEST = lax.Precision.HIGHEST
VMEM_LEAST = 16 * 1024 * 1024
VMEM_MOST = 48 * 1024 * 1024
WHOLE = pl.BlockSpec(memory_space=pltpu.VMEM)
SCALARS = pl.BlockSpec(memory_space=pltpu.SMEM)
IN_HBM = pl.BlockSpec(memory_space=pltpu.HBM)


def split_bf16(x):
    hi = x.astype(jnp.bfloat16)
    lo = (x - hi.astype(jnp.float32)).astype(jnp.bfloat16)
    return hi, lo


def dot_pairs(a, b, dims, rows, columns):
    product = lax.dot_general(a, b, (dims, ((), ())), preferred_element_type=jnp.float32)
    low = product[:rows, columns:] + product[rows:, :columns]
    return product[:rows, :columns] + (low + product[rows:, columns:])


def params(moved):
    grant = min(VMEM_MOST, max(VMEM_LEAST, 3 * moved))
    return pltpu.CompilerParams(vmem_limit_bytes=grant)


def call(kernel, out_shape, in_specs, flops, moved, scratch=(), out_spec=WHOLE):
    return pl.pallas_call(
        kernel,
        out_shape=out_shape,
        in_specs=in_specs,
        out_specs=jax.tree.map(lambda _: out_spec, out_shape),
        scratch_shapes=scratch,
        compiler_params=params(moved),
        cost_estimate=pl.CostEstimate(flops=flops, bytes_accessed=moved, transcendentals=0),
    )


class Place:
    def __init__(self, geo, order_ref):
        self.geo = geo
        self.a, self.b = lax.axis_index("outer"), lax.axis_index("inner")
        self.first = lax.axis_index("order") * geo.m_local
        self.order_ref = order_ref

    def order(self, m):
        return self.order_ref[self.first + m]

    def outer(self, shift):
        return lax.rem(self.a + (self.geo.outer - shift), self.geo.outer)

    def inner(self, shift):
        return lax.rem(self.b + (self.geo.inner - shift), self.geo.inner)

    def among(self, table, b=None):
        index = self.a * self.geo.inner + (self.b if b is None else b)
        flat = [value for row in table for value in row]
        result = jnp.int32(flat[0])
        for i, value in enumerate(flat[1:], 1):
            result = jnp.where(index == i, jnp.int32(value), result)
        return result


def window_of(geo, leg_ref, m, block):
    start = geo.window_starts[block]
    width = min(geo.window, leg_ref.shape[2] - start)
    piece = leg_ref[m, :, start : start + width]
    if width < geo.window:
        fill = jnp.zeros((piece.shape[0], geo.window - width), jnp.float32)
        piece = jnp.concatenate([piece, fill], axis=1)
    return piece


def cut_windows(geo, leg_ref, *send_refs):
    a = lax.axis_index("outer")
    for shift, ref in enumerate(send_refs, 1):
        for block in range(geo.outer):

            @pl.when(lax.rem(a + shift, geo.outer) == block)
            def _(ref=ref, block=block):
                for m in range(ref.shape[0]):
                    ref[m] = window_of(geo, leg_ref, m, block)


def to_line(stacked):
    rows, width = stacked.shape
    folded = jnp.zeros((rows, LANES), jnp.float32)
    for start in range(0, width, LANES):
        piece = stacked[:, start : min(start + LANES, width)]
        if piece.shape[1] < LANES:
            fill = jnp.zeros((rows, LANES - piece.shape[1]), jnp.float32)
            piece = jnp.concatenate([piece, fill], axis=1)
        folded = folded + piece
    return jnp.sum(jnp.transpose(folded), axis=0, keepdims=True)


def residual_norm(geo, order_ref, res_ref, out_ref):
    place = Place(geo, order_ref)
    m_local, sin_cos, samples, width = res_ref.shape
    total = jnp.zeros((samples, width), jnp.float32)
    for m in range(m_local):
        valid = own_mask(place, m, samples, width)
        for s in range(sin_cos):
            residual = jnp.where(valid, res_ref[m, s], 0.0)
            total = total + residual * residual
    line = to_line(jnp.concatenate([total, jnp.zeros_like(total)], axis=0))
    line = line[:, : out_ref.shape[2]]
    for o in range(out_ref.shape[0]):
        out_ref[o] = jnp.broadcast_to(line, out_ref.shape[1:])


def prepare(geo, order_ref, leg_hbm, *refs):
    parts = refs[: geo.inner]
    out_ref, rows_ref, leg_ref, sem = refs[geo.inner :]
    fetch = pltpu.make_async_copy(leg_hbm, leg_ref, sem)
    fetch.start()
    place = Place(geo, order_ref)
    m_local, sin_cos, samples, width = parts[0].shape
    window = out_ref.shape[2]
    rows = sin_cos * samples
    start = place.among([[s] * geo.inner for s in geo.window_starts])
    degree = start + lax.broadcasted_iota(jnp.int32, (rows, window), 1)
    for m in range(m_local):
        valid = degree >= place.order(m)
        total = None
        for shift, part in enumerate(parts):
            block = part[m].reshape(rows, width)
            block = jnp.concatenate([block, jnp.zeros((rows, window - width), jnp.float32)], axis=1)
            block = pltpu.roll(block, place.among(geo.places, place.inner(shift)), 1)
            total = block if total is None else total + block
        total = jnp.where(valid, total, 0.0)
        hi, lo = split_bf16(total)
        out_ref[m, :rows] = hi
        out_ref[m, rows:] = lo
    fetch.wait()
    for block in range(geo.outer):

        @pl.when(place.a == block)
        def _(block=block):
            for m in range(m_local):
                rows_ref[m] = synthesis(window_of(geo, leg_ref, m, block), out_ref, m)


def synthesis(leg, dir_ref, m):
    rows, line = leg.shape[0], dir_ref.shape[1] // 2
    halves = jnp.concatenate(split_bf16(leg), axis=0)
    return dot_pairs(halves, dir_ref[m], ((1,), (1,)), rows, line)


def synthesise_rest(geo, own_ref, *refs):
    legs, (dir_ref, out_hbm, out_ref, sems) = refs[:-4], refs[-4:]
    place = Place(geo, None)
    rows = out_ref.shape[3]
    copies = []
    for m in range(own_ref.shape[0]):
        for shift in range(geo.outer):
            part = own_ref[m] if shift == 0 else synthesis(legs[shift - 1][m], dir_ref, m)
            a = place.outer(shift)
            for o in range(out_ref.shape[1]):
                out_ref[m, o, a] = part[o * rows : (o + 1) * rows]
        copy = pltpu.make_async_copy(out_ref.at[m], out_hbm.at[:, :, m], sems.at[m])
        copy.start()
        copies.append(copy)
    for copy in copies:
        copy.wait()


def weight_tables(longitudes, period, class_ref, land_ref, value_ref, basis_ref, out_ref):
    classes = class_ref[...]
    on_land = land_ref[...] == 1
    weight = jnp.zeros(classes.shape, jnp.float32)
    for c in range(value_ref.shape[0]):
        value = jnp.where(on_land, value_ref[c, 1], value_ref[c, 0])
        weight = jnp.where(classes == c, value, weight)
    rows = classes.shape[0]
    folded = jnp.zeros((rows, LANES), jnp.float32)
    for start in range(0, longitudes, LANES):
        piece = weight[:, start : min(start + LANES, longitudes)]
        if piece.shape[1] < LANES:
            piece = jnp.concatenate(
                [piece, jnp.zeros((rows, LANES - piece.shape[1]), jnp.float32)], axis=1
            )
        folded = folded + piece
    moments = lax.dot_general(
        folded,
        basis_ref[...],
        (((1,), (0,)), ((), ())),
        precision=HIGHEST,
        preferred_element_type=jnp.float32,
    )
    lane = lax.broadcasted_iota(jnp.int32, (rows, LANES), 1)
    sign = jnp.where(lane < LANES // 2, 1.0, -1.0)
    count = out_ref.shape[1]
    for n in range(count):
        even = jnp.broadcast_to(moments[:, n : n + 1], (rows, LANES))
        odd = jnp.broadcast_to(moments[:, count + n : count + n + 1], (rows, LANES))
        out_ref[0, n] = even
        out_ref[1, n] = sign * even
        out_ref[2, n] = odd
        out_ref[3, n] = sign * odd


def grid_rows(geo, stride, order_ref, recv_ref, table_ref, out_ref, plain, swapped, done):
    orders = plain.shape[0]
    m_local = recv_ref.shape[1]
    slot = [lax.div(order_ref[m], jnp.int32(stride)) for m in range(orders)]
    for m in range(orders):
        o, i = divmod(m, m_local)
        total = recv_ref[o * geo.outer, i]
        for a in range(1, geo.outer):
            total = total + recv_ref[o * geo.outer + a, i]
        at = slot[m]
        plain[at] = total
        swapped[at] = pltpu.roll(total, LANES // 2, 1)
    for i in range(orders):
        total = None
        for j in range(orders):
            cos_part = table_ref[0, abs(i - j)] + table_ref[1, i + j]
            if i >= j:
                sin_part = table_ref[2, i + j] - table_ref[3, i - j]
            else:
                sin_part = table_ref[2, i + j] + table_ref[3, j - i]
            term = cos_part * plain[j] + sin_part * swapped[j]
            total = term if total is None else total + term
        done[i] = total
    copies = geo.outer * geo.inner
    for m in range(orders):
        o, i = divmod(m, m_local)
        value = done[slot[m]]
        for c in range(copies):
            out_ref[o * copies + c, i] = value


def cut_blocks(geo, leg_hbm, *refs):
    legs, outs, (leg_ref, sem) = refs[: geo.outer - 1], refs[geo.outer - 1 : -2], refs[-2:]
    fetch = pltpu.make_async_copy(leg_hbm, leg_ref, sem)
    fetch.start()
    place = Place(geo, None)
    width = geo.block_window

    def each(own):
        for shift, ref in enumerate(outs):
            target = lax.rem(place.b + shift, geo.inner)
            for a in range(geo.outer):
                for b in range(geo.inner):

                    @pl.when((place.a == a) & (target == b))
                    def _(ref=ref, a=a, b=b):
                        start = geo.block_starts[a][b]
                        for m in range(leg_ref.shape[0]):
                            if own:
                                ref[0, m] = window_of(geo, leg_ref, m, a)[:, start : start + width]
                            else:
                                for i, leg in enumerate(legs):
                                    ref[i + 1, m] = leg[m, :, start : start + width]

    each(False)
    fetch.wait()
    each(True)


def own_mask(place, m, rows, width):
    geo = place.geo
    degree = place.among(geo.own_starts) + lax.broadcasted_iota(jnp.int32, (rows, width), 1)
    return degree >= place.order(m)


def project(geo, order_ref, recv_ref, *refs):
    legs = refs[: geo.inner]
    dir_hbm, res_hbm, damp_ref, norm_ref, app_ref, sums_ref, dir_ref, res_ref, sems = refs[geo.inner :]
    fetches = [
        pltpu.make_async_copy(src, dst, sems.at[i])
        for i, (src, dst) in enumerate(((dir_hbm, dir_ref), (res_hbm, res_ref)))
    ]
    for fetch in fetches:
        fetch.start()
    place = Place(geo, order_ref)
    m_local, sin_cos, samples, width = dir_ref.shape
    window = geo.block_window
    copies = geo.outer * geo.inner
    order_devices = recv_ref.shape[0] // copies
    damping = damp_ref[...]
    rows = sin_cos * samples
    offsets = [
        [p - s for p, s in zip(*pair)] for pair in zip(geo.places, geo.block_starts)
    ]
    back = window - place.among(offsets)
    totals = []
    for m in range(m_local):
        tiles, blocks = [], []
        for b in range(geo.inner):
            for a in range(geo.outer):
                band = place.outer(a) * geo.inner + place.inner(b)
                blocks.append(legs[b][a, m])
                for o in range(order_devices):
                    tiles.append(recv_ref[o * copies + band, m])
        hi, lo = split_bf16(jnp.concatenate(tiles, axis=0))
        high, low = split_bf16(jnp.concatenate(blocks, axis=0))
        dims = (((0,), (0,)), ((), ()))
        both = jnp.concatenate([hi, lo], axis=1)
        first = lax.dot_general(both, high, dims, preferred_element_type=jnp.float32)
        second = lax.dot_general(hi, low, dims, preferred_element_type=jnp.float32)
        summed = first[:rows] + (first[rows:] + second)
        totals.append(pltpu.roll(summed, back, 1)[:, :width])
    for fetch in fetches:
        fetch.wait()
    sums = [None] * 3
    for m in range(m_local):
        valid = own_mask(place, m, samples, width)
        for s in range(sin_cos):
            direction = jnp.where(valid, dir_ref[m, s], 0.0)
            residual = jnp.where(valid, res_ref[m, s], 0.0)
            part = totals[m][s * samples : (s + 1) * samples]
            applied = jnp.where(valid, part + damping * direction, 0.0)
            app_ref[m, s] = applied
            terms = (direction * applied, residual * applied, applied * applied)
            sums = [t if old is None else old + t for old, t in zip(sums, terms)]
    norm = jnp.sum(norm_ref[...], axis=0)[0:1, :samples]
    norm = jnp.where(lax.axis_index("order") == 0, norm, 0.0)
    line = to_line(jnp.concatenate(sums + [jnp.zeros_like(sums[0])], axis=0))
    line = jnp.concatenate([line[:, : 3 * samples], norm], axis=1)
    for device in range(sums_ref.shape[0]):
        sums_ref[device] = line


def update(geo, order_ref, sums_ref, app_ref, pos_ref, dir_ref, res_ref, *refs):
    outs, bufs, sems = refs[:3], refs[3:6], refs[6]
    place = Place(geo, order_ref)
    m_local, sin_cos, samples, width = dir_ref.shape
    totals = jnp.sum(sums_ref[...], axis=0)
    curvature, cross, square, before = [
        totals[:, i * samples : (i + 1) * samples] for i in range(4)
    ]
    step_row = before / curvature
    after = before - 2.0 * step_row * cross + step_row * step_row * square
    ratio_row = after / before
    row = lax.broadcasted_iota(jnp.int32, (samples, samples), 0)
    column = lax.broadcasted_iota(jnp.int32, (samples, samples), 1)
    diagonal = row == column
    step = jnp.sum(jnp.where(diagonal, step_row, 0.0), axis=1, keepdims=True)
    ratio = jnp.sum(jnp.where(diagonal, ratio_row, 0.0), axis=1, keepdims=True)
    copies = []
    for m in range(m_local):
        valid = own_mask(place, m, samples, width)
        for s in range(sin_cos):
            direction = jnp.where(valid, dir_ref[m, s], 0.0)
            residual = jnp.where(valid, res_ref[m, s], 0.0)
            position = jnp.where(valid, pos_ref[m, s], 0.0)
            new_residual = residual - step * app_ref[m, s]
            values = (position + step * direction, new_residual, new_residual + ratio * direction)
            for i in range(3):
                bufs[i][m, s] = values[i]
                copy = pltpu.make_async_copy(bufs[i].at[m, s], outs[i].at[m, s], sems.at[i, m, s])
                copy.start()
                copies.append(copy)
    for copy in copies:
        copy.wait()


class Geometry:
    def __init__(self, outer, inner, degrees, m_local):
        self.outer, self.inner, self.m_local = outer, inner, m_local
        block = degrees // (outer * inner)

        def down(x):
            return x // LANES * LANES

        def up(x):
            return -(-x // LANES) * LANES

        own = [[(a * inner + b) * block for b in range(inner)] for a in range(outer)]
        self.own_starts = own
        self.window_starts = [down(row[0]) for row in own]
        self.window = max(
            up(row[-1] + block) - start for row, start in zip(own, self.window_starts)
        )
        self.places = [
            [x - start for x in row] for row, start in zip(own, self.window_starts)
        ]
        self.block_window = max(up(p + block) - down(p) for row in self.places for p in row)
        self.block_starts = [
            [min(down(p), self.window - self.block_window) for p in row] for row in self.places
        ]


def far(x):
    return pltpu.with_memory_space_constraint(x, pltpu.HBM)


def rotate(x, axis, size, shift):
    return lax.ppermute(x, axis, [(i, (i + shift) % size) for i in range(size)])


def plain_grid(geo, grid_in, order_of, class_idx, land, class_weight, period):
    order_devices = grid_in.shape[0] // geo.outer
    m_local, rows, width = grid_in.shape[1:]
    orders = order_devices * m_local
    longitudes = class_idx.shape[1]
    stacked = grid_in.reshape(order_devices, geo.outer, m_local, rows, 2, width // 2)
    stacked = jnp.sum(stacked, axis=1).reshape(orders, rows, 2, width // 2)
    phases = order_of[:, None] * jnp.arange(period, dtype=jnp.int32)[None, :] % longitudes
    angles = phases.astype(jnp.float32) * (2.0 * math.pi / longitudes)
    harmonic = jnp.stack([jnp.cos(angles), jnp.sin(angles)])
    surface = jnp.einsum("mrsk,smp->rkp", stacked, harmonic, precision=HIGHEST)
    onehot = class_idx[:, :, None] == jnp.arange(class_weight.shape[0], dtype=jnp.int32)
    by_class = jnp.dot(onehot.astype(jnp.float32), class_weight, precision=HIGHEST)
    weight = jnp.where(land == 1, by_class[:, :, 1], by_class[:, :, 0])
    folded = jnp.sum(weight.reshape(rows, longitudes // period, period), axis=1)
    weighted = surface * folded[:, None, :]
    spectra = jnp.einsum("rkp,smp->mrsk", weighted, harmonic, precision=HIGHEST)
    spectra = (spectra * (2.0 / longitudes)).reshape(order_devices, 1, m_local, rows, width)
    copies = geo.outer * geo.inner
    spectra = jnp.broadcast_to(spectra, (order_devices, copies, m_local, rows, width))
    return spectra.reshape(order_devices * copies, m_local, rows, width)


def shards(
    outer,
    inner,
    position,
    residual,
    direction,
    legendre,
    order_of,
    class_idx,
    land,
    class_weight,
    damping,
):
    m_local, sin_cos, samples, deg_local = position.shape
    degrees, band_rows = legendre.shape[1:]
    rows_here, longitudes = class_idx.shape
    orders = order_of.shape[0]
    order_devices = orders // m_local
    devices = order_devices * outer * inner
    line = sin_cos * samples
    geo = Geometry(outer, inner, degrees, m_local)
    by_row = jnp.transpose(legendre, (0, 2, 1))
    cut = jax.ShapeDtypeStruct((m_local, band_rows, geo.window), jnp.float32)
    cuts = call(
        functools.partial(cut_windows, geo),
        (cut,) * (outer - 1),
        [WHOLE],
        m_local * band_rows * geo.window,
        8 * outer * m_local * band_rows * geo.window,
    )(by_row)
    received = [rotate(cuts[s - 1], "outer", outer, s) for s in range(1, outer)]
    siblings = [rotate(direction, "inner", inner, s) for s in range(1, inner)]

    norm_lanes = -(-samples // LANES) * LANES
    norm = call(
        functools.partial(residual_norm, geo),
        jax.ShapeDtypeStruct((order_devices, 8, norm_lanes), jnp.float32),
        [SCALARS, WHOLE],
        3 * m_local * line * deg_local,
        4 * m_local * line * deg_local,
    )(order_of, residual)
    norm = lax.all_to_all(norm, "order", split_axis=0, concat_axis=0, tiled=True)

    own_flops = 8 * m_local * line * geo.window * band_rows
    leg_moved = 4 * m_local * band_rows * degrees
    leg_scratch = [pltpu.VMEM(by_row.shape, jnp.float32), pltpu.SemaphoreType.DMA(())]
    dir_window, own_rows = call(
        functools.partial(prepare, geo),
        (
            jax.ShapeDtypeStruct((m_local, 2 * line, geo.window), jnp.bfloat16),
            jax.ShapeDtypeStruct((m_local, band_rows, line), jnp.float32),
        ),
        [SCALARS, IN_HBM] + [WHOLE] * inner,
        own_flops,
        8 * m_local * line * geo.window + leg_moved,
        leg_scratch,
    )(order_of, far(by_row), direction, *siblings)

    stride = longitudes // (2 * orders)
    period = longitudes // stride if longitudes % stride == 0 else longitudes
    small = orders <= 32 and LANES % period == 0 and line == LANES and longitudes % period == 0
    if small:
        count = 2 * orders
        n = np.arange(count)[None, :]
        p = np.arange(LANES)[:, None]
        angle = 2.0 * math.pi * ((n * p) % period) / period
        basis = np.zeros((LANES, -(-2 * count // LANES) * LANES), np.float32)
        basis[:, :count] = np.cos(angle) / longitudes
        basis[:, count : 2 * count] = np.sin(angle) / longitudes
        tables = call(
            functools.partial(weight_tables, longitudes, period),
            jax.ShapeDtypeStruct((4, count, rows_here, LANES), jnp.float32),
            [WHOLE, WHOLE, SCALARS, WHOLE],
            100 * rows_here * longitudes,
            8 * rows_here * longitudes,
        )(class_idx, land, class_weight, jnp.asarray(basis))

    *received, norm = lax.optimization_barrier((*received, norm))
    to_rows = call(
        functools.partial(synthesise_rest, geo),
        pltpu.HBM((order_devices, outer, m_local, rows_here, line), jnp.float32),
        [WHOLE] * (outer + 1),
        own_flops * (outer - 1),
        4 * m_local * (line + band_rows) * geo.window,
        [
            pltpu.VMEM((m_local, order_devices, outer, rows_here, line), jnp.float32),
            pltpu.SemaphoreType.DMA((m_local,)),
        ],
        IN_HBM,
    )(own_rows, *received, dir_window)
    grid_in = lax.all_to_all(
        to_rows.reshape(order_devices * outer, m_local, rows_here, line),
        ("order", "outer"),
        split_axis=0,
        concat_axis=0,
        tiled=True,
    )

    block = jax.ShapeDtypeStruct((outer, m_local, band_rows, geo.block_window), jnp.float32)
    own_block, *blocks = call(
        functools.partial(cut_blocks, geo),
        (block,) * inner,
        [IN_HBM] + [WHOLE] * (outer - 1),
        inner * outer * m_local * band_rows * geo.block_window,
        8 * inner * outer * m_local * band_rows * geo.block_window + leg_moved,
        leg_scratch,
    )(far(by_row), *received)
    from_inner = [rotate(blocks[s - 1], "inner", inner, s) for s in range(1, inner)]

    if small:
        to_orders = call(
            functools.partial(grid_rows, geo, stride),
            jax.ShapeDtypeStruct((devices, m_local, rows_here, line), jnp.float32),
            [SCALARS, WHOLE, WHOLE],
            6 * orders * orders * rows_here * line,
            8 * orders * rows_here * line,
            [pltpu.VMEM((orders, rows_here, line), jnp.float32)] * 3,
        )(order_of, grid_in, tables)
    else:
        to_orders = plain_grid(geo, grid_in, order_of, class_idx, land, class_weight, period)
    spectra = lax.all_to_all(
        to_orders, ("order", "outer", "inner"), split_axis=0, concat_axis=0, tiled=True
    )
    coefficients = jax.ShapeDtypeStruct(position.shape, jnp.float32)
    applied, sums = call(
        functools.partial(project, geo),
        (coefficients, jax.ShapeDtypeStruct((devices, 1, 4 * samples), jnp.float32)),
        [SCALARS] + [WHOLE] * (1 + inner) + [IN_HBM] * 2 + [WHOLE] * 2,
        6 * m_local * line * geo.block_window * band_rows * outer * inner,
        16 * m_local * line * deg_local,
        [pltpu.VMEM(position.shape, jnp.float32)] * 2 + [pltpu.SemaphoreType.DMA((2,))],
    )(order_of, spectra, own_block, *from_inner, far(direction), far(residual), damping[None, :], norm)
    sums = lax.all_to_all(
        sums, ("order", "outer", "inner"), split_axis=0, concat_axis=0, tiled=True
    )
    return call(
        functools.partial(update, geo),
        (coefficients,) * 3,
        [SCALARS] + [WHOLE] * 5,
        10 * m_local * line * deg_local,
        28 * m_local * line * deg_local,
        [pltpu.VMEM(position.shape, jnp.float32)] * 3
        + [pltpu.SemaphoreType.DMA((3, m_local, sin_cos))],
        IN_HBM,
    )(order_of, sums, applied, position, direction, residual)


def solution(mesh):
    order_devices, bands = mesh.shape["order"], mesh.shape["lat"]
    outer = 2 if bands % 2 == 0 else 1
    inner = bands // outer
    split = Mesh(mesh.devices.reshape(order_devices, outer, inner), ("order", "outer", "inner"))
    lat = ("outer", "inner")
    coefficients = P("order", None, None, lat)
    grid = P(("outer", "inner", "order"), None)
    return jax.shard_map(
        functools.partial(shards, outer, inner),
        mesh=split,
        in_specs=(
            coefficients,
            coefficients,
            coefficients,
            P("order", None, lat),
            P(),
            grid,
            grid,
            P(),
            P(lat),
        ),
        out_specs=(coefficients,) * 3,
        check_vma=False,
    )
```

```python
import functools
import math

import jax
import jax.numpy as jnp
import numpy as np
from jax import lax
from jax.experimental import pallas as pl
from jax.experimental.pallas import tpu as pltpu
from jax.sharding import Mesh
from jax.sharding import PartitionSpec as P

LANES = 128
HIGHEST = lax.Precision.HIGHEST
VMEM_LEAST = 16 * 1024 * 1024
VMEM_MOST = 48 * 1024 * 1024
WHOLE = pl.BlockSpec(memory_space=pltpu.VMEM)
SCALARS = pl.BlockSpec(memory_space=pltpu.SMEM)
IN_HBM = pl.BlockSpec(memory_space=pltpu.HBM)


def repeat(count, body):
    lax.fori_loop(0, count, lambda i, carry: (body(i), carry)[1], 0)


def split_bf16(x):
    hi = x.astype(jnp.bfloat16)
    lo = (x - hi.astype(jnp.float32)).astype(jnp.bfloat16)
    return hi, lo


def dot_pairs(a, b, dims, rows, columns):
    product = lax.dot_general(a, b, (dims, ((), ())), preferred_element_type=jnp.float32)
    low = product[:rows, columns:] + product[rows:, :columns]
    return product[:rows, :columns] + (low + product[rows:, columns:])


def params(moved):
    grant = min(VMEM_MOST, max(VMEM_LEAST, 3 * moved))
    return pltpu.CompilerParams(vmem_limit_bytes=grant)


def call(kernel, out_shape, in_specs, flops, moved, scratch=(), out_spec=WHOLE):
    return pl.pallas_call(
        kernel,
        out_shape=out_shape,
        in_specs=in_specs,
        out_specs=jax.tree.map(lambda _: out_spec, out_shape),
        scratch_shapes=scratch,
        compiler_params=params(moved),
        cost_estimate=pl.CostEstimate(flops=flops, bytes_accessed=moved, transcendentals=0),
    )


class Place:
    def __init__(self, geo, order_ref):
        self.geo = geo
        self.a, self.b = lax.axis_index("outer"), lax.axis_index("inner")
        self.first = lax.axis_index("order") * geo.m_local
        self.order_ref = order_ref

    def order(self, m):
        return self.order_ref[self.first + m]

    def outer(self, shift):
        return lax.rem(self.a + (self.geo.outer - shift), self.geo.outer)

    def inner(self, shift):
        return lax.rem(self.b + (self.geo.inner - shift), self.geo.inner)

    def among(self, table, b=None):
        index = self.a * self.geo.inner + (self.b if b is None else b)
        return choose(index, [value for row in table for value in row])


def choose(index, values):
    result = jnp.int32(values[0])
    for i, value in enumerate(values[1:], 1):
        result = jnp.where(index == i, jnp.int32(value), result)
    return result


def take(leg_ref, m, index, starts, width):
    degrees = leg_ref.shape[2]
    start = pl.multiple_of(choose(index, starts), LANES)
    last = None
    for i, first in enumerate(starts):
        first = first + width - LANES
        tile = leg_ref[m, :, first : min(first + LANES, degrees)]
        if tile.shape[1] < LANES:
            fill = jnp.zeros((tile.shape[0], LANES - tile.shape[1]), jnp.float32)
            tile = jnp.concatenate([tile, fill], axis=1)
        last = tile if last is None else jnp.where(index == i, tile, last)
    return jnp.concatenate([leg_ref[m, :, pl.ds(start, width - LANES)], last], axis=1)


def lane_start(place, table, b=None):
    return pl.multiple_of(place.among(table, b), LANES)


def cut_windows(geo, leg_hbm, *refs):
    send_refs, (leg_ref, sem) = refs[:-2], refs[-2:]
    fetch = pltpu.make_async_copy(leg_hbm, leg_ref, sem)
    fetch.start()
    a = lax.axis_index("outer")
    fetch.wait()
    for shift, ref in enumerate(send_refs, 1):
        block = lax.rem(a + shift, geo.outer)

        def one(m, ref=ref, block=block):
            ref[m] = take(leg_ref, m, block, geo.window_starts, geo.window)

        repeat(ref.shape[0], one)


def fold(x):
    rows, width = x.shape
    folded = None
    for start in range(0, width, LANES):
        piece = x[:, start : min(start + LANES, width)]
        if piece.shape[1] < LANES:
            fill = jnp.zeros((rows, LANES - piece.shape[1]), jnp.float32)
            piece = jnp.concatenate([piece, fill], axis=1)
        folded = piece if folded is None else folded + piece
    return folded


def to_line(folded):
    return jnp.sum(jnp.transpose(folded), axis=0, keepdims=True)


def prepare(geo, order_ref, leg_hbm, *refs):
    parts = refs[: geo.inner]
    out_ref, rows_ref, *cuts, leg_ref, sem = refs[geo.inner :]
    fetch = pltpu.make_async_copy(leg_hbm, leg_ref, sem)
    fetch.start()
    place = Place(geo, order_ref)
    m_local, sin_cos, samples, width = parts[0].shape
    window = out_ref.shape[2]
    line = sin_cos * samples
    start = place.among([[s] * geo.inner for s in geo.window_starts])
    piece = 16
    steps = samples // piece
    shifts = [place.among(geo.places, place.inner(shift)) for shift in range(geo.inner)]
    degree = start + lax.broadcasted_iota(jnp.int32, (piece, window), 1)

    def one(i):
        m, rest = lax.div(i, sin_cos * steps), lax.rem(i, sin_cos * steps)
        s, k = lax.div(rest, steps), lax.rem(rest, steps) * piece
        total = None
        for shift, part in zip(shifts, parts):
            block = part[m, s, pl.ds(pl.multiple_of(k, piece), piece), :]
            fill = jnp.zeros((piece, window - width), jnp.float32)
            block = pltpu.roll(jnp.concatenate([block, fill], axis=1), shift, 1)
            total = block if total is None else total + block
        total = jnp.where(degree >= place.order(m), total, 0.0)
        hi, lo = split_bf16(total)
        at = rest * piece
        out_ref[m, pl.ds(pl.multiple_of(at, piece), piece)] = hi
        out_ref[m, pl.ds(pl.multiple_of(line + at, piece), piece)] = lo

    repeat(m_local * sin_cos * steps, one)
    fetch.wait()

    def rows(m):
        leg = take(leg_ref, m, place.a, geo.window_starts, window)
        rows_ref[m] = synthesis(leg, out_ref, m)
        for shift, ref in enumerate(cuts):
            index = place.a * geo.inner + lax.rem(place.b + shift, geo.inner)
            ref[m] = take(leg_ref, m, index, geo.row_starts, geo.block_window)

    repeat(m_local, rows)


def synthesis(leg, dir_ref, m):
    rows, line = leg.shape[0], dir_ref.shape[1] // 2
    halves = jnp.concatenate(split_bf16(leg), axis=0)
    return dot_pairs(halves, dir_ref[m], ((1,), (1,)), rows, line)


def synthesise_rest(geo, own_ref, *refs):
    others = geo.outer - 1
    legs, (dir_ref, out_ref, *cuts) = refs[:others], refs[others:]
    place = Place(geo, None)
    rows = out_ref.shape[3]
    starts = [
        lane_start(place, geo.block_starts, lax.rem(place.b + shift, geo.inner))
        for shift in range(geo.inner)
    ]

    def put(m, shift, part):
        a = place.outer(shift)
        for o in range(out_ref.shape[0]):
            out_ref[o, a, m] = part[o * rows : (o + 1) * rows]

    def one(m):
        put(m, 0, own_ref[m])
        for shift in range(1, geo.outer):
            put(m, shift, synthesis(legs[shift - 1][m], dir_ref, m))
            for start, ref in zip(starts, cuts):
                ref[shift - 1, m] = legs[shift - 1][m, :, pl.ds(start, geo.block_window)]

    repeat(own_ref.shape[0], one)


def weight_tables(longitudes, period, class_ref, land_ref, value_ref, basis_ref, out_ref):
    classes = class_ref[...]
    on_land = land_ref[...] == 1
    weight = jnp.zeros(classes.shape, jnp.float32)
    for c in range(value_ref.shape[0]):
        value = jnp.where(on_land, value_ref[c, 1], value_ref[c, 0])
        weight = jnp.where(classes == c, value, weight)
    rows = classes.shape[0]
    folded = jnp.zeros((rows, LANES), jnp.float32)
    for start in range(0, longitudes, LANES):
        piece = weight[:, start : min(start + LANES, longitudes)]
        if piece.shape[1] < LANES:
            piece = jnp.concatenate(
                [piece, jnp.zeros((rows, LANES - piece.shape[1]), jnp.float32)], axis=1
            )
        folded = folded + piece
    moments = lax.dot_general(
        folded,
        basis_ref[...],
        (((1,), (0,)), ((), ())),
        precision=HIGHEST,
        preferred_element_type=jnp.float32,
    )
    lane = lax.broadcasted_iota(jnp.int32, (rows, LANES), 1)
    sign = jnp.where(lane < LANES // 2, 1.0, -1.0)
    count = out_ref.shape[1]
    for n in range(count):
        even = jnp.broadcast_to(moments[:, n : n + 1], (rows, LANES))
        odd = jnp.broadcast_to(moments[:, count + n : count + n + 1], (rows, LANES))
        out_ref[0, n] = even
        out_ref[1, n] = sign * even
        out_ref[2, n] = odd
        out_ref[3, n] = sign * odd


def grid_rows(geo, stride, order_ref, recv_ref, table_ref, out_ref, plain, swapped, done):
    orders = plain.shape[0]
    m_local, each = recv_ref.shape[1], out_ref.shape[1]
    slot = [lax.div(order_ref[m], jnp.int32(stride)) for m in range(orders)]
    for m in range(orders):
        o, i = divmod(m, m_local)
        total = recv_ref[o * geo.outer, i]
        for a in range(1, geo.outer):
            total = total + recv_ref[o * geo.outer + a, i]
        at = slot[m]
        plain[at] = total
        swapped[at] = pltpu.roll(total, LANES // 2, 1)
    for i in range(orders):
        total = None
        for j in range(orders):
            cos_part = table_ref[0, abs(i - j)] + table_ref[1, i + j]
            if i >= j:
                sin_part = table_ref[2, i + j] - table_ref[3, i - j]
            else:
                sin_part = table_ref[2, i + j] + table_ref[3, j - i]
            term = cos_part * plain[j] + sin_part * swapped[j]
            total = term if total is None else total + term
        done[i] = total
    for m in range(orders):
        o, i = divmod(m, m_local)
        b, i = divmod(i, each)
        value = done[slot[m]]
        for a in range(geo.outer):
            out_ref[(o * geo.outer + a) * geo.inner + b, i] = value


def own_mask(place, m, rows, width):
    geo = place.geo
    degree = place.among(geo.own_starts) + lax.broadcasted_iota(jnp.int32, (rows, width), 1)
    return degree >= place.order(m)


def project(geo, shift, order_ref, recv_ref, *refs):
    legs, refs = refs[: 2 * geo.inner], refs[2 * geo.inner :]
    dir_ref, res_ref, damp_ref = refs[:3]
    before_ref = refs[3] if shift else None
    app_ref, sums_ref = refs[-2:]
    place = Place(geo, order_ref)
    each, sin_cos, samples, width = app_ref.shape
    first = place.inner(shift) * each
    window = geo.block_window
    copies = geo.outer * geo.inner
    order_devices = recv_ref.shape[0] // copies
    damping = damp_ref[...]
    rows = sin_cos * samples
    offsets = [
        [p - s for p, s in zip(*pair)] for pair in zip(geo.places, geo.block_starts)
    ]
    back = window - place.among(offsets)

    def products(i):
        tiles, blocks = [], []
        for b in range(geo.inner):
            for a in range(geo.outer):
                band = place.outer(a) * geo.inner + place.inner(b)
                if a == 0:
                    blocks.append(legs[b][first + i])
                else:
                    blocks.append(legs[geo.inner + b][a - 1, first + i])
                for o in range(order_devices):
                    tiles.append(recv_ref[o * copies + band, i])
        hi, lo = split_bf16(jnp.concatenate(tiles, axis=0))
        high, low = split_bf16(jnp.concatenate(blocks, axis=0))
        dims = (((0,), (0,)), ((), ()))
        both = jnp.concatenate([hi, lo], axis=1)
        main = lax.dot_general(both, high, dims, preferred_element_type=jnp.float32)
        rest = lax.dot_general(hi, low, dims, preferred_element_type=jnp.float32)
        summed = main[:rows] + (main[rows:] + rest)
        summed = pltpu.roll(summed, back, 1)[:, :width]
        for s in range(sin_cos):
            app_ref[i, s] = summed[s * samples : (s + 1) * samples]

    repeat(each, products)

    def apply(at, sums):
        i, s = lax.div(at, sin_cos), lax.rem(at, sin_cos)
        valid = own_mask(place, first + i, samples, width)
        direction = jnp.where(valid, dir_ref[first + i, s], 0.0)
        residual = jnp.where(valid, res_ref[first + i, s], 0.0)
        applied = jnp.where(valid, app_ref[i, s] + damping * direction, 0.0)
        app_ref[i, s] = applied
        terms = (
            residual * residual,
            direction * applied,
            residual * applied,
            applied * applied,
        )
        return tuple(old + fold(t) for old, t in zip(sums, terms))

    if shift:
        start = tuple(before_ref[i * samples : (i + 1) * samples] for i in range(4))
    else:
        start = (jnp.zeros((samples, LANES), jnp.float32),) * 4
    sums = lax.fori_loop(0, each * sin_cos, apply, start)
    stacked = jnp.concatenate(sums, axis=0)
    if shift < geo.inner - 1:
        sums_ref[...] = stacked
    else:
        line = to_line(stacked)

        def give(device):
            sums_ref[device] = line

        repeat(sums_ref.shape[0], give)


def update(geo, order_ref, sums_ref, *refs):
    apps, refs = refs[: geo.inner], refs[geo.inner :]
    pos_ref, dir_ref, res_ref, *refs = refs
    outs, bufs, sems = refs[:3], refs[3:6], refs[6]
    place = Place(geo, order_ref)
    m_local, sin_cos, samples, width = dir_ref.shape
    totals = jnp.sum(sums_ref[...], axis=0)
    before, curvature, cross, square = [
        totals[:, i * samples : (i + 1) * samples] for i in range(4)
    ]
    step_row = before / curvature
    after = before - 2.0 * step_row * cross + step_row * step_row * square
    ratio_row = after / before
    row = lax.broadcasted_iota(jnp.int32, (samples, samples), 0)
    column = lax.broadcasted_iota(jnp.int32, (samples, samples), 1)
    diagonal = row == column
    step = jnp.sum(jnp.where(diagonal, step_row, 0.0), axis=1, keepdims=True)
    ratio = jnp.sum(jnp.where(diagonal, ratio_row, 0.0), axis=1, keepdims=True)

    def copy(i, m, s):
        return pltpu.make_async_copy(bufs[i].at[m, s], outs[i].at[m, s], sems.at[i, m, s])

    each = m_local // geo.inner
    for shift, app_ref in enumerate(apps):

        def one(at, shift=shift, app_ref=app_ref):
            i, s = lax.div(at, sin_cos), lax.rem(at, sin_cos)
            m = place.inner(shift) * each + i
            valid = own_mask(place, m, samples, width)
            direction = jnp.where(valid, dir_ref[m, s], 0.0)
            residual = jnp.where(valid, res_ref[m, s], 0.0)
            position = jnp.where(valid, pos_ref[m, s], 0.0)
            new_residual = residual - step * app_ref[i, s]
            values = (
                position + step * direction,
                new_residual,
                new_residual + ratio * direction,
            )
            for i in range(3):
                bufs[i][m, s] = values[i]
                copy(i, m, s).start()

        repeat(each * sin_cos, one)

    def end(at):
        for i in range(3):
            copy(i, lax.div(at, sin_cos), lax.rem(at, sin_cos)).wait()

    repeat(m_local * sin_cos, end)


class Geometry:
    def __init__(self, outer, inner, degrees, m_local):
        self.outer, self.inner, self.m_local = outer, inner, m_local
        block = degrees // (outer * inner)

        def down(x):
            return x // LANES * LANES

        def up(x):
            return -(-x // LANES) * LANES

        own = [[(a * inner + b) * block for b in range(inner)] for a in range(outer)]
        self.own_starts = own
        self.window_starts = [down(row[0]) for row in own]
        self.window = max(
            up(row[-1] + block) - start for row, start in zip(own, self.window_starts)
        )
        self.places = [
            [x - start for x in row] for row, start in zip(own, self.window_starts)
        ]
        self.block_window = max(up(p + block) - down(p) for row in self.places for p in row)
        self.block_starts = [
            [min(down(p), self.window - self.block_window) for p in row] for row in self.places
        ]
        self.row_starts = [
            w + s for w, row in zip(self.window_starts, self.block_starts) for s in row
        ]


def far(x):
    return pltpu.with_memory_space_constraint(x, pltpu.HBM)


def rotate(x, axis, size, shift):
    return lax.ppermute(x, axis, [(i, (i + shift) % size) for i in range(size)])


def plain_grid(geo, grid_in, order_of, class_idx, land, class_weight, period):
    order_devices = grid_in.shape[0] // geo.outer
    m_local, rows, width = grid_in.shape[1:]
    orders = order_devices * m_local
    longitudes = class_idx.shape[1]
    stacked = grid_in.reshape(order_devices, geo.outer, m_local, rows, 2, width // 2)
    stacked = jnp.sum(stacked, axis=1).reshape(orders, rows, 2, width // 2)
    phases = order_of[:, None] * jnp.arange(period, dtype=jnp.int32)[None, :] % longitudes
    angles = phases.astype(jnp.float32) * (2.0 * math.pi / longitudes)
    harmonic = jnp.stack([jnp.cos(angles), jnp.sin(angles)])
    surface = jnp.einsum("mrsk,smp->rkp", stacked, harmonic, precision=HIGHEST)
    onehot = class_idx[:, :, None] == jnp.arange(class_weight.shape[0], dtype=jnp.int32)
    by_class = jnp.dot(onehot.astype(jnp.float32), class_weight, precision=HIGHEST)
    weight = jnp.where(land == 1, by_class[:, :, 1], by_class[:, :, 0])
    folded = jnp.sum(weight.reshape(rows, longitudes // period, period), axis=1)
    weighted = surface * folded[:, None, :]
    spectra = jnp.einsum("rkp,smp->mrsk", weighted, harmonic, precision=HIGHEST)
    each = m_local // geo.inner
    spectra = spectra * (2.0 / longitudes)
    spectra = spectra.reshape(order_devices, 1, geo.inner, each, rows, width)
    spectra = jnp.broadcast_to(
        spectra, (order_devices, geo.outer, geo.inner, each, rows, width)
    )
    return spectra.reshape(order_devices * geo.outer * geo.inner, each, rows, width)


def shards(
    outer,
    inner,
    position,
    residual,
    direction,
    legendre,
    order_of,
    class_idx,
    land,
    class_weight,
    damping,
):
    m_local, sin_cos, samples, deg_local = position.shape
    degrees, band_rows = legendre.shape[1:]
    rows_here, longitudes = class_idx.shape
    orders = order_of.shape[0]
    order_devices = orders // m_local
    devices = order_devices * outer * inner
    each = m_local // inner
    line = sin_cos * samples
    geo = Geometry(outer, inner, degrees, m_local)
    by_row = jnp.transpose(legendre, (0, 2, 1))
    cut = pltpu.VMEM((m_local, band_rows, geo.window), jnp.float32)
    leg_moved = 4 * m_local * band_rows * degrees
    leg_scratch = [pltpu.VMEM(by_row.shape, jnp.float32), pltpu.SemaphoreType.DMA(())]
    cuts = call(
        functools.partial(cut_windows, geo),
        (cut,) * (outer - 1),
        [IN_HBM],
        m_local * band_rows * geo.window,
        8 * outer * m_local * band_rows * geo.window,
        leg_scratch,
    )(far(by_row))
    received = [rotate(cuts[s - 1], "outer", outer, s) for s in range(1, outer)]
    stride = longitudes // (2 * orders)
    period = longitudes // stride if longitudes % stride == 0 else longitudes
    small = orders <= 16 and LANES % period == 0 and line == LANES and longitudes % period == 0
    if small:
        count = 2 * orders
        n = np.arange(count)[None, :]
        p = np.arange(LANES)[:, None]
        angle = 2.0 * math.pi * ((n * p) % period) / period
        basis = np.zeros((LANES, -(-2 * count // LANES) * LANES), np.float32)
        basis[:, :count] = np.cos(angle) / longitudes
        basis[:, count : 2 * count] = np.sin(angle) / longitudes
        tables = call(
            functools.partial(weight_tables, longitudes, period),
            jax.ShapeDtypeStruct((4, count, rows_here, LANES), jnp.float32),
            [WHOLE, WHOLE, SCALARS, WHOLE],
            100 * rows_here * longitudes,
            8 * rows_here * longitudes,
        )(class_idx, land, class_weight, jnp.asarray(basis))

    siblings = [rotate(direction, "inner", inner, s) for s in range(1, inner)]
    if small:
        siblings, tables = lax.optimization_barrier((siblings, tables))
    own_flops = 8 * m_local * line * geo.window * band_rows
    dir_window, own_rows, *own_blocks = call(
        functools.partial(prepare, geo),
        (
            jax.ShapeDtypeStruct((m_local, 2 * line, geo.window), jnp.bfloat16),
            jax.ShapeDtypeStruct((m_local, band_rows, line), jnp.float32),
        )
        + (jax.ShapeDtypeStruct((m_local, band_rows, geo.block_window), jnp.float32),) * inner,
        [SCALARS, IN_HBM] + [WHOLE] * inner,
        own_flops,
        8 * m_local * line * geo.window + leg_moved,
        leg_scratch,
    )(order_of, far(by_row), direction, *siblings)
    first_legs = [own_blocks[0]]
    first_legs += [rotate(own_blocks[s], "inner", inner, s) for s in range(1, inner)]

    received, first_legs = lax.optimization_barrier((received, first_legs))
    block = jax.ShapeDtypeStruct((outer - 1, m_local, band_rows, geo.block_window), jnp.float32)
    to_rows, *blocks = call(
        functools.partial(synthesise_rest, geo),
        (jax.ShapeDtypeStruct((order_devices, outer, m_local, rows_here, line), jnp.float32),)
        + (block,) * inner,
        [WHOLE] * (outer + 1),
        own_flops * (outer - 1),
        4 * m_local * (line + band_rows) * geo.window,
    )(own_rows, *received, dir_window)
    rest_legs = [blocks[0]]
    rest_legs += [rotate(blocks[s], "inner", inner, s) for s in range(1, inner)]
    grid_in = lax.all_to_all(
        to_rows.reshape(order_devices * outer, m_local, rows_here, line),
        ("order", "outer"),
        split_axis=0,
        concat_axis=0,
        tiled=True,
    )

    grid_in, rest_legs = lax.optimization_barrier((grid_in, rest_legs))
    if small:
        to_orders = call(
            functools.partial(grid_rows, geo, stride),
            jax.ShapeDtypeStruct((devices, each, rows_here, line), jnp.float32),
            [SCALARS, WHOLE, WHOLE],
            6 * orders * orders * rows_here * line,
            8 * orders * rows_here * line,
            [pltpu.VMEM((orders, rows_here, line), jnp.float32)] * 3,
        )(order_of, grid_in, tables)
    else:
        to_orders = plain_grid(geo, grid_in, order_of, class_idx, land, class_weight, period)
    spectra = lax.all_to_all(
        to_orders, ("order", "outer", "inner"), split_axis=0, concat_axis=0, tiled=True
    )
    shares = [spectra] + [rotate(spectra, "inner", inner, s) for s in range(1, inner)]
    coefficients = jax.ShapeDtypeStruct(position.shape, jnp.float32)
    part = (each,) + position.shape[1:]
    sums = ()
    applied = []
    for shift, share in enumerate(shares):
        if shift < inner - 1:
            sums_out = jax.ShapeDtypeStruct((4 * samples, LANES), jnp.float32)
        else:
            sums_out = jax.ShapeDtypeStruct((devices, 1, 4 * samples), jnp.float32)
        result, sums = call(
            functools.partial(project, geo, shift),
            (jax.ShapeDtypeStruct(part, jnp.float32), sums_out),
            [SCALARS] + [WHOLE] * (4 + 2 * inner + (shift > 0)),
            6 * each * line * geo.block_window * band_rows * outer * inner,
            16 * each * line * deg_local,
        )(
            order_of,
            share,
            *first_legs,
            *rest_legs,
            direction,
            residual,
            damping[None, :],
            *((sums,) if shift else ()),
        )
        applied.append(result)
    sums = lax.all_to_all(
        sums, ("order", "outer", "inner"), split_axis=0, concat_axis=0, tiled=True
    )
    return call(
        functools.partial(update, geo),
        (coefficients,) * 3,
        [SCALARS] + [WHOLE] * (4 + inner),
        10 * m_local * line * deg_local,
        28 * m_local * line * deg_local,
        [pltpu.VMEM(position.shape, jnp.float32)] * 3
        + [pltpu.SemaphoreType.DMA((3, m_local, sin_cos))],
        IN_HBM,
    )(order_of, sums, *applied, position, direction, residual)


def solution(mesh):
    order_devices, bands = mesh.shape["order"], mesh.shape["lat"]
    outer = 2 if bands % 2 == 0 else 1
    inner = bands // outer
    split = Mesh(mesh.devices.reshape(order_devices, outer, inner), ("order", "outer", "inner"))
    lat = ("outer", "inner")
    coefficients = P("order", None, None, lat)
    grid = P(("outer", "inner", "order"), None)
    return jax.shard_map(
        functools.partial(shards, outer, inner),
        mesh=split,
        in_specs=(
            coefficients,
            coefficients,
            coefficients,
            P("order", None, lat),
            P(),
            grid,
            grid,
            P(),
            P(lat),
        ),
        out_specs=(coefficients,) * 3,
        check_vma=False,
    )
```

```python
import functools
import math

import jax
import jax.numpy as jnp
import numpy as np
from jax import lax
from jax.experimental import pallas as pl
from jax.experimental.pallas import tpu as pltpu
from jax.sharding import Mesh
from jax.sharding import PartitionSpec as P

LANES = 128
HIGHEST = lax.Precision.HIGHEST
VMEM_LEAST = 16 * 1024 * 1024
VMEM_MOST = 48 * 1024 * 1024
WHOLE = pl.BlockSpec(memory_space=pltpu.VMEM)
SCALARS = pl.BlockSpec(memory_space=pltpu.SMEM)
IN_HBM = pl.BlockSpec(memory_space=pltpu.HBM)


def repeat(count, body):
    lax.fori_loop(0, count, lambda i, carry: (body(i), carry)[1], 0)


def split_bf16(x):
    hi = x.astype(jnp.bfloat16)
    lo = (x - hi.astype(jnp.float32)).astype(jnp.bfloat16)
    return hi, lo


def dot_pairs(a, b, dims, rows, columns):
    product = lax.dot_general(a, b, (dims, ((), ())), preferred_element_type=jnp.float32)
    low = product[:rows, columns:] + product[rows:, :columns]
    return product[:rows, :columns] + (low + product[rows:, columns:])


def params(moved):
    grant = min(VMEM_MOST, max(VMEM_LEAST, 3 * moved))
    return pltpu.CompilerParams(vmem_limit_bytes=grant)


def call(kernel, out_shape, in_specs, flops, moved, scratch=(), out_spec=WHOLE):
    return pl.pallas_call(
        kernel,
        out_shape=out_shape,
        in_specs=in_specs,
        out_specs=jax.tree.map(lambda _: out_spec, out_shape),
        scratch_shapes=scratch,
        compiler_params=params(moved),
        cost_estimate=pl.CostEstimate(flops=flops, bytes_accessed=moved, transcendentals=0),
    )


class Place:
    def __init__(self, geo, order_ref):
        self.geo = geo
        self.a, self.b = lax.axis_index("outer"), lax.axis_index("inner")
        self.first = lax.axis_index("order") * geo.m_local
        self.order_ref = order_ref

    def order(self, m):
        return self.order_ref[self.first + m]

    def outer(self, shift):
        return lax.rem(self.a + (self.geo.outer - shift), self.geo.outer)

    def inner(self, shift):
        return lax.rem(self.b + (self.geo.inner - shift), self.geo.inner)

    def among(self, table, b=None):
        index = self.a * self.geo.inner + (self.b if b is None else b)
        return choose(index, [value for row in table for value in row])


def choose(index, values):
    result = jnp.int32(values[0])
    for i, value in enumerate(values[1:], 1):
        result = jnp.where(index == i, jnp.int32(value), result)
    return result


def take(leg_ref, m, index, starts, width):
    degrees = leg_ref.shape[2]
    start = pl.multiple_of(choose(index, starts), LANES)
    last = None
    for i, first in enumerate(starts):
        first = first + width - LANES
        tile = leg_ref[m, :, first : min(first + LANES, degrees)]
        if tile.shape[1] < LANES:
            fill = jnp.zeros((tile.shape[0], LANES - tile.shape[1]), jnp.float32)
            tile = jnp.concatenate([tile, fill], axis=1)
        last = tile if last is None else jnp.where(index == i, tile, last)
    return jnp.concatenate([leg_ref[m, :, pl.ds(start, width - LANES)], last], axis=1)


def exact_window(geo, leg_ref, m, block):
    wide = take(leg_ref, m, block, geo.window_starts, geo.take_width)
    back = lax.rem(geo.take_width - choose(block, geo.window_shifts), geo.take_width)
    return pltpu.roll(wide, back, 1)[:, : geo.window]


def inner_block(geo, window, target):
    result = None
    for b, start in enumerate(geo.block_starts):
        piece = window[:, start : start + geo.block_window]
        result = piece if result is None else jnp.where(target == b, piece, result)
    return result


def cut_windows(geo, leg_hbm, *refs):
    send_refs, (leg_ref, sem) = refs[:-2], refs[-2:]
    fetch = pltpu.make_async_copy(leg_hbm, leg_ref, sem)
    fetch.start()
    a = lax.axis_index("outer")
    fetch.wait()
    m_local, rows = leg_ref.shape[:2]
    lane = lax.broadcasted_iota(jnp.int32, (rows, LANES), 1)
    for shift, ref in enumerate(send_refs, 1):
        block = lax.rem(a + shift, geo.outer)
        tiles = [None] * geo.rest_tiles
        for m in range(m_local):
            window = exact_window(geo, leg_ref, m, block)
            ref[:, m * geo.main : (m + 1) * geo.main] = window[:, : geo.main]
            if geo.rest:
                at, place = divmod(m, geo.rest_each)
                tile = jnp.where(lane < geo.rest, window[:, geo.main :], 0.0)
                if place:
                    tile = pltpu.roll(tile, place * geo.rest, 1)
                tiles[at] = tile if tiles[at] is None else tiles[at] + tile
        for i, tile in enumerate(tiles):
            start = m_local * geo.main + i * LANES
            ref[:, start : start + LANES] = tile


def unpack_window(geo, ref, m):
    window = ref[:, m * geo.main : (m + 1) * geo.main]
    if geo.rest:
        at, place = divmod(m, geo.rest_each)
        start = geo.m_local * geo.main + at * LANES
        tile = ref[:, start : start + LANES]
        if place:
            tile = pltpu.roll(tile, LANES - place * geo.rest, 1)
        window = jnp.concatenate([window, tile], axis=1)
    return window


def fold(x):
    rows, width = x.shape
    folded = None
    for start in range(0, width, LANES):
        piece = x[:, start : min(start + LANES, width)]
        if piece.shape[1] < LANES:
            fill = jnp.zeros((rows, LANES - piece.shape[1]), jnp.float32)
            piece = jnp.concatenate([piece, fill], axis=1)
        folded = piece if folded is None else folded + piece
    return folded


def to_line(folded):
    return jnp.sum(jnp.transpose(folded), axis=0, keepdims=True)


def prepare(geo, order_ref, leg_hbm, *refs):
    parts = refs[: geo.inner]
    out_ref, rows_ref, *cuts, leg_ref, sem = refs[geo.inner :]
    fetch = pltpu.make_async_copy(leg_hbm, leg_ref, sem)
    fetch.start()
    place = Place(geo, order_ref)
    m_local, sin_cos, samples, width = parts[0].shape
    window = out_ref.shape[2]
    line = sin_cos * samples
    start = place.a * geo.pair
    piece = 16
    steps = samples // piece
    shifts = [choose(place.inner(shift), geo.places) for shift in range(geo.inner)]
    degree = start + lax.broadcasted_iota(jnp.int32, (piece, window), 1)

    def one(i):
        m, rest = lax.div(i, sin_cos * steps), lax.rem(i, sin_cos * steps)
        s, k = lax.div(rest, steps), lax.rem(rest, steps) * piece
        total = None
        for shift, part in zip(shifts, parts):
            block = part[m, s, pl.ds(pl.multiple_of(k, piece), piece), :]
            fill = jnp.zeros((piece, window - width), jnp.float32)
            block = pltpu.roll(jnp.concatenate([block, fill], axis=1), shift, 1)
            total = block if total is None else total + block
        total = jnp.where(degree >= place.order(m), total, 0.0)
        hi, lo = split_bf16(total)
        at = rest * piece
        out_ref[m, pl.ds(pl.multiple_of(at, piece), piece)] = hi
        out_ref[m, pl.ds(pl.multiple_of(line + at, piece), piece)] = lo

    repeat(m_local * sin_cos * steps, one)
    fetch.wait()

    def rows(m):
        leg = exact_window(geo, leg_ref, m, place.a)
        rows_ref[m] = synthesis(leg, out_ref, m)
        for shift, ref in enumerate(cuts):
            ref[m] = inner_block(geo, leg, lax.rem(place.b + shift, geo.inner))

    repeat(m_local, rows)


def synthesis(leg, dir_ref, m):
    rows, line = leg.shape[0], dir_ref.shape[1] // 2
    halves = jnp.concatenate(split_bf16(leg), axis=0)
    return dot_pairs(halves, dir_ref[m], ((1,), (1,)), rows, line)


def synthesise_rest(geo, own_ref, *refs):
    others = geo.outer - 1
    legs, (dir_ref, out_ref, *cuts) = refs[:others], refs[others:]
    place = Place(geo, None)
    rows = out_ref.shape[3]

    def put(m, shift, part):
        a = place.outer(shift)
        for o in range(out_ref.shape[0]):
            out_ref[o, a, m] = part[o * rows : (o + 1) * rows]

    for m in range(own_ref.shape[0]):
        put(m, 0, own_ref[m])
        for shift in range(1, geo.outer):
            leg = unpack_window(geo, legs[shift - 1], m)
            put(m, shift, synthesis(leg, dir_ref, m))
            for ahead, ref in enumerate(cuts):
                ref[shift - 1, m] = inner_block(geo, leg, lax.rem(place.b + ahead, geo.inner))


def weight_tables(longitudes, period, class_ref, land_ref, value_ref, basis_ref, out_ref):
    classes = class_ref[...]
    on_land = land_ref[...] == 1
    weight = jnp.zeros(classes.shape, jnp.float32)
    for c in range(value_ref.shape[0]):
        value = jnp.where(on_land, value_ref[c, 1], value_ref[c, 0])
        weight = jnp.where(classes == c, value, weight)
    rows = classes.shape[0]
    folded = jnp.zeros((rows, LANES), jnp.float32)
    for start in range(0, longitudes, LANES):
        piece = weight[:, start : min(start + LANES, longitudes)]
        if piece.shape[1] < LANES:
            piece = jnp.concatenate(
                [piece, jnp.zeros((rows, LANES - piece.shape[1]), jnp.float32)], axis=1
            )
        folded = folded + piece
    moments = lax.dot_general(
        folded,
        basis_ref[...],
        (((1,), (0,)), ((), ())),
        precision=HIGHEST,
        preferred_element_type=jnp.float32,
    )
    lane = lax.broadcasted_iota(jnp.int32, (rows, LANES), 1)
    sign = jnp.where(lane < LANES // 2, 1.0, -1.0)
    count = out_ref.shape[1]
    for n in range(count):
        even = jnp.broadcast_to(moments[:, n : n + 1], (rows, LANES))
        odd = jnp.broadcast_to(moments[:, count + n : count + n + 1], (rows, LANES))
        out_ref[0, n] = even
        out_ref[1, n] = sign * even
        out_ref[2, n] = odd
        out_ref[3, n] = sign * odd


def grid_rows(geo, stride, order_ref, recv_ref, table_ref, out_ref, plain, swapped, done):
    orders = plain.shape[0]
    m_local, each = recv_ref.shape[1], out_ref.shape[1]
    slot = [lax.div(order_ref[m], jnp.int32(stride)) for m in range(orders)]
    for m in range(orders):
        o, i = divmod(m, m_local)
        total = recv_ref[o * geo.outer, i]
        for a in range(1, geo.outer):
            total = total + recv_ref[o * geo.outer + a, i]
        at = slot[m]
        plain[at] = total
        swapped[at] = pltpu.roll(total, LANES // 2, 1)
    for i in range(orders):
        total = None
        for j in range(orders):
            cos_part = table_ref[0, abs(i - j)] + table_ref[1, i + j]
            if i >= j:
                sin_part = table_ref[2, i + j] - table_ref[3, i - j]
            else:
                sin_part = table_ref[2, i + j] + table_ref[3, j - i]
            term = cos_part * plain[j] + sin_part * swapped[j]
            total = term if total is None else total + term
        done[i] = total
    for m in range(orders):
        o, i = divmod(m, m_local)
        b, i = divmod(i, each)
        value = done[slot[m]]
        for a in range(geo.outer):
            out_ref[(o * geo.outer + a) * geo.inner + b, i] = value


def own_mask(place, m, rows, width):
    geo = place.geo
    degree = place.among(geo.own_starts) + lax.broadcasted_iota(jnp.int32, (rows, width), 1)
    return degree >= place.order(m)


def project(geo, shift, order_ref, recv_ref, *refs):
    legs, refs = refs[: 2 * geo.inner], refs[2 * geo.inner :]
    dir_ref, res_ref, damp_ref = refs[:3]
    before_ref = refs[3] if shift else None
    app_ref, sums_ref = refs[-2:]
    place = Place(geo, order_ref)
    each, sin_cos, samples, width = app_ref.shape
    first = place.inner(shift) * each
    window = geo.block_window
    copies = geo.outer * geo.inner
    order_devices = recv_ref.shape[0] // copies
    damping = damp_ref[...]
    rows = sin_cos * samples
    offsets = [p - s for p, s in zip(geo.places, geo.block_starts)]
    back = window - choose(place.b, offsets)

    def products(i):
        tiles, blocks = [], []
        for b in range(geo.inner):
            for a in range(geo.outer):
                band = place.outer(a) * geo.inner + place.inner(b)
                if a == 0:
                    blocks.append(legs[b][first + i])
                else:
                    blocks.append(legs[geo.inner + b][a - 1, first + i])
                for o in range(order_devices):
                    tiles.append(recv_ref[o * copies + band, i])
        hi, lo = split_bf16(jnp.concatenate(tiles, axis=0))
        high, low = split_bf16(jnp.concatenate(blocks, axis=0))
        dims = (((0,), (0,)), ((), ()))
        both = jnp.concatenate([hi, lo], axis=1)
        main = lax.dot_general(both, high, dims, preferred_element_type=jnp.float32)
        rest = lax.dot_general(hi, low, dims, preferred_element_type=jnp.float32)
        summed = main[:rows] + (main[rows:] + rest)
        summed = pltpu.roll(summed, back, 1)[:, :width]
        for s in range(sin_cos):
            app_ref[i, s] = summed[s * samples : (s + 1) * samples]

    repeat(each, products)

    def apply(at, sums):
        i, s = lax.div(at, sin_cos), lax.rem(at, sin_cos)
        valid = own_mask(place, first + i, samples, width)
        direction = jnp.where(valid, dir_ref[first + i, s], 0.0)
        residual = jnp.where(valid, res_ref[first + i, s], 0.0)
        applied = jnp.where(valid, app_ref[i, s] + damping * direction, 0.0)
        app_ref[i, s] = applied
        terms = (
            residual * residual,
            direction * applied,
            residual * applied,
            applied * applied,
        )
        return tuple(old + fold(t) for old, t in zip(sums, terms))

    if shift:
        start = tuple(before_ref[i * samples : (i + 1) * samples] for i in range(4))
    else:
        start = (jnp.zeros((samples, LANES), jnp.float32),) * 4
    sums = lax.fori_loop(0, each * sin_cos, apply, start)
    stacked = jnp.concatenate(sums, axis=0)
    if shift < geo.inner - 1:
        sums_ref[...] = stacked
    else:
        line = to_line(stacked)

        def give(device):
            sums_ref[device] = line

        repeat(sums_ref.shape[0], give)


def update(geo, order_ref, sums_ref, *refs):
    apps, refs = refs[: geo.inner], refs[geo.inner :]
    pos_ref, dir_ref, res_ref, *refs = refs
    outs, bufs, sems = refs[:3], refs[3:6], refs[6]
    place = Place(geo, order_ref)
    m_local, sin_cos, samples, width = dir_ref.shape
    totals = jnp.sum(sums_ref[...], axis=0)
    before, curvature, cross, square = [
        totals[:, i * samples : (i + 1) * samples] for i in range(4)
    ]
    step_row = before / curvature
    after = before - 2.0 * step_row * cross + step_row * step_row * square
    ratio_row = after / before
    row = lax.broadcasted_iota(jnp.int32, (samples, samples), 0)
    column = lax.broadcasted_iota(jnp.int32, (samples, samples), 1)
    diagonal = row == column
    step = jnp.sum(jnp.where(diagonal, step_row, 0.0), axis=1, keepdims=True)
    ratio = jnp.sum(jnp.where(diagonal, ratio_row, 0.0), axis=1, keepdims=True)

    def copy(i, m, s):
        return pltpu.make_async_copy(bufs[i].at[m, s], outs[i].at[m, s], sems.at[i, m, s])

    each = m_local // geo.inner
    for shift, app_ref in enumerate(apps):

        def one(at, shift=shift, app_ref=app_ref):
            i, s = lax.div(at, sin_cos), lax.rem(at, sin_cos)
            m = place.inner(shift) * each + i
            valid = own_mask(place, m, samples, width)
            direction = jnp.where(valid, dir_ref[m, s], 0.0)
            residual = jnp.where(valid, res_ref[m, s], 0.0)
            position = jnp.where(valid, pos_ref[m, s], 0.0)
            new_residual = residual - step * app_ref[i, s]
            values = (
                position + step * direction,
                new_residual,
                new_residual + ratio * direction,
            )
            for i in range(3):
                bufs[i][m, s] = values[i]
                copy(i, m, s).start()

        repeat(each * sin_cos, one)

    def end(at):
        for i in range(3):
            copy(i, lax.div(at, sin_cos), lax.rem(at, sin_cos)).wait()

    repeat(m_local * sin_cos, end)


class Geometry:
    def __init__(self, outer, inner, degrees, m_local):
        self.outer, self.inner, self.m_local = outer, inner, m_local
        block = degrees // (outer * inner)

        def down(x):
            return x // LANES * LANES

        def up(x):
            return -(-x // LANES) * LANES

        pair = degrees // outer
        self.pair = pair
        self.own_starts = [[(a * inner + b) * block for b in range(inner)] for a in range(outer)]
        self.window_starts = [down(a * pair) for a in range(outer)]
        self.window_shifts = [a * pair - s for a, s in enumerate(self.window_starts)]
        self.take_width = max(up(s + pair) for s in self.window_shifts)
        self.window = up(pair)
        self.places = [b * block for b in range(inner)]
        self.block_window = max(up(p + block) - down(p) for p in self.places)
        self.block_starts = [min(down(p), self.window - self.block_window) for p in self.places]
        self.main = down(pair)
        self.rest = pair - self.main
        self.rest_each = LANES // self.rest if self.rest else 1
        self.rest_tiles = -(-m_local // self.rest_each) if self.rest else 0
        self.packed = m_local * self.main + self.rest_tiles * LANES


def far(x):
    return pltpu.with_memory_space_constraint(x, pltpu.HBM)


def rotate(x, axis, size, shift):
    return lax.ppermute(x, axis, [(i, (i + shift) % size) for i in range(size)])


def plain_grid(geo, grid_in, order_of, class_idx, land, class_weight, period):
    order_devices = grid_in.shape[0] // geo.outer
    m_local, rows, width = grid_in.shape[1:]
    orders = order_devices * m_local
    longitudes = class_idx.shape[1]
    stacked = grid_in.reshape(order_devices, geo.outer, m_local, rows, 2, width // 2)
    stacked = jnp.sum(stacked, axis=1).reshape(orders, rows, 2, width // 2)
    phases = order_of[:, None] * jnp.arange(period, dtype=jnp.int32)[None, :] % longitudes
    angles = phases.astype(jnp.float32) * (2.0 * math.pi / longitudes)
    harmonic = jnp.stack([jnp.cos(angles), jnp.sin(angles)])
    surface = jnp.einsum("mrsk,smp->rkp", stacked, harmonic, precision=HIGHEST)
    onehot = class_idx[:, :, None] == jnp.arange(class_weight.shape[0], dtype=jnp.int32)
    by_class = jnp.dot(onehot.astype(jnp.float32), class_weight, precision=HIGHEST)
    weight = jnp.where(land == 1, by_class[:, :, 1], by_class[:, :, 0])
    folded = jnp.sum(weight.reshape(rows, longitudes // period, period), axis=1)
    weighted = surface * folded[:, None, :]
    spectra = jnp.einsum("rkp,smp->mrsk", weighted, harmonic, precision=HIGHEST)
    each = m_local // geo.inner
    spectra = spectra * (2.0 / longitudes)
    spectra = spectra.reshape(order_devices, 1, geo.inner, each, rows, width)
    spectra = jnp.broadcast_to(
        spectra, (order_devices, geo.outer, geo.inner, each, rows, width)
    )
    return spectra.reshape(order_devices * geo.outer * geo.inner, each, rows, width)


def shards(
    outer,
    inner,
    position,
    residual,
    direction,
    legendre,
    order_of,
    class_idx,
    land,
    class_weight,
    damping,
):
    m_local, sin_cos, samples, deg_local = position.shape
    degrees, band_rows = legendre.shape[1:]
    rows_here, longitudes = class_idx.shape
    orders = order_of.shape[0]
    order_devices = orders // m_local
    devices = order_devices * outer * inner
    each = m_local // inner
    line = sin_cos * samples
    geo = Geometry(outer, inner, degrees, m_local)
    by_row = jnp.transpose(legendre, (0, 2, 1))
    cut = pltpu.VMEM((band_rows, geo.packed), jnp.float32)
    leg_moved = 4 * m_local * band_rows * degrees
    leg_scratch = [pltpu.VMEM(by_row.shape, jnp.float32), pltpu.SemaphoreType.DMA(())]
    cuts = call(
        functools.partial(cut_windows, geo),
        (cut,) * (outer - 1),
        [IN_HBM],
        m_local * band_rows * geo.window,
        8 * outer * m_local * band_rows * geo.window,
        leg_scratch,
    )(far(by_row))
    received = [rotate(cuts[s - 1], "outer", outer, s) for s in range(1, outer)]
    stride = longitudes // (2 * orders)
    period = longitudes // stride if longitudes % stride == 0 else longitudes
    small = orders <= 16 and LANES % period == 0 and line == LANES and longitudes % period == 0
    if small:
        count = 2 * orders
        n = np.arange(count)[None, :]
        p = np.arange(LANES)[:, None]
        angle = 2.0 * math.pi * ((n * p) % period) / period
        basis = np.zeros((LANES, -(-2 * count // LANES) * LANES), np.float32)
        basis[:, :count] = np.cos(angle) / longitudes
        basis[:, count : 2 * count] = np.sin(angle) / longitudes
        tables = call(
            functools.partial(weight_tables, longitudes, period),
            jax.ShapeDtypeStruct((4, count, rows_here, LANES), jnp.float32),
            [WHOLE, WHOLE, SCALARS, WHOLE],
            100 * rows_here * longitudes,
            8 * rows_here * longitudes,
        )(class_idx, land, class_weight, jnp.asarray(basis))

    siblings = [rotate(direction, "inner", inner, s) for s in range(1, inner)]
    if small:
        siblings, tables = lax.optimization_barrier((siblings, tables))
    own_flops = 8 * m_local * line * geo.window * band_rows
    dir_window, own_rows, *own_blocks = call(
        functools.partial(prepare, geo),
        (
            jax.ShapeDtypeStruct((m_local, 2 * line, geo.window), jnp.bfloat16),
            jax.ShapeDtypeStruct((m_local, band_rows, line), jnp.float32),
        )
        + (jax.ShapeDtypeStruct((m_local, band_rows, geo.block_window), jnp.float32),) * inner,
        [SCALARS, IN_HBM] + [WHOLE] * inner,
        own_flops,
        8 * m_local * line * geo.window + leg_moved,
        leg_scratch,
    )(order_of, far(by_row), direction, *siblings)
    first_legs = [own_blocks[0]]
    first_legs += [rotate(own_blocks[s], "inner", inner, s) for s in range(1, inner)]

    received, first_legs = lax.optimization_barrier((received, first_legs))
    block = jax.ShapeDtypeStruct((outer - 1, m_local, band_rows, geo.block_window), jnp.float32)
    to_rows, *blocks = call(
        functools.partial(synthesise_rest, geo),
        (jax.ShapeDtypeStruct((order_devices, outer, m_local, rows_here, line), jnp.float32),)
        + (block,) * inner,
        [WHOLE] * (outer + 1),
        own_flops * (outer - 1),
        4 * m_local * (line + band_rows) * geo.window,
    )(own_rows, *received, dir_window)
    rest_legs = [blocks[0]]
    rest_legs += [rotate(blocks[s], "inner", inner, s) for s in range(1, inner)]
    grid_in = lax.all_to_all(
        to_rows.reshape(order_devices * outer, m_local, rows_here, line),
        ("order", "outer"),
        split_axis=0,
        concat_axis=0,
        tiled=True,
    )

    grid_in, rest_legs = lax.optimization_barrier((grid_in, rest_legs))
    if small:
        to_orders = call(
            functools.partial(grid_rows, geo, stride),
            jax.ShapeDtypeStruct((devices, each, rows_here, line), jnp.float32),
            [SCALARS, WHOLE, WHOLE],
            6 * orders * orders * rows_here * line,
            8 * orders * rows_here * line,
            [pltpu.VMEM((orders, rows_here, line), jnp.float32)] * 3,
        )(order_of, grid_in, tables)
    else:
        to_orders = plain_grid(geo, grid_in, order_of, class_idx, land, class_weight, period)
    spectra = lax.all_to_all(
        to_orders, ("order", "outer", "inner"), split_axis=0, concat_axis=0, tiled=True
    )
    shares = [spectra] + [rotate(spectra, "inner", inner, s) for s in range(1, inner)]
    coefficients = jax.ShapeDtypeStruct(position.shape, jnp.float32)
    part = (each,) + position.shape[1:]
    sums = ()
    applied = []
    for shift, share in enumerate(shares):
        if shift < inner - 1:
            sums_out = jax.ShapeDtypeStruct((4 * samples, LANES), jnp.float32)
        else:
            sums_out = jax.ShapeDtypeStruct((devices, 1, 4 * samples), jnp.float32)
        result, sums = call(
            functools.partial(project, geo, shift),
            (jax.ShapeDtypeStruct(part, jnp.float32), sums_out),
            [SCALARS] + [WHOLE] * (4 + 2 * inner + (shift > 0)),
            6 * each * line * geo.block_window * band_rows * outer * inner,
            16 * each * line * deg_local,
        )(
            order_of,
            share,
            *first_legs,
            *rest_legs,
            direction,
            residual,
            damping[None, :],
            *((sums,) if shift else ()),
        )
        applied.append(result)
    sums = lax.all_to_all(
        sums, ("order", "outer", "inner"), split_axis=0, concat_axis=0, tiled=True
    )
    return call(
        functools.partial(update, geo),
        (coefficients,) * 3,
        [SCALARS] + [WHOLE] * (4 + inner),
        10 * m_local * line * deg_local,
        28 * m_local * line * deg_local,
        [pltpu.VMEM(position.shape, jnp.float32)] * 3
        + [pltpu.SemaphoreType.DMA((3, m_local, sin_cos))],
        IN_HBM,
    )(order_of, sums, *applied, position, direction, residual)


def solution(mesh):
    order_devices, bands = mesh.shape["order"], mesh.shape["lat"]
    outer = 2 if bands % 2 == 0 else 1
    inner = bands // outer
    split = Mesh(mesh.devices.reshape(order_devices, outer, inner), ("order", "outer", "inner"))
    lat = ("outer", "inner")
    coefficients = P("order", None, None, lat)
    grid = P(("outer", "inner", "order"), None)
    return jax.shard_map(
        functools.partial(shards, outer, inner),
        mesh=split,
        in_specs=(
            coefficients,
            coefficients,
            coefficients,
            P("order", None, lat),
            P(),
            grid,
            grid,
            P(),
            P(lat),
        ),
        out_specs=(coefficients,) * 3,
        check_vma=False,
    )
```

```python
import functools
import math

import jax
import jax.numpy as jnp
import numpy as np
from jax import lax
from jax.experimental import pallas as pl
from jax.experimental.pallas import tpu as pltpu
from jax.sharding import Mesh
from jax.sharding import PartitionSpec as P

LANES = 128
HIGHEST = lax.Precision.HIGHEST
VMEM_LEAST = 16 * 1024 * 1024
VMEM_MOST = 48 * 1024 * 1024
WHOLE = pl.BlockSpec(memory_space=pltpu.VMEM)
SCALARS = pl.BlockSpec(memory_space=pltpu.SMEM)
IN_HBM = pl.BlockSpec(memory_space=pltpu.HBM)


def repeat(count, body):
    lax.fori_loop(0, count, lambda i, carry: (body(i), carry)[1], 0)


def split_bf16(x):
    hi = x.astype(jnp.bfloat16)
    lo = (x - hi.astype(jnp.float32)).astype(jnp.bfloat16)
    return hi, lo


def dot_pairs(a, b, dims, rows, columns):
    product = lax.dot_general(a, b, (dims, ((), ())), preferred_element_type=jnp.float32)
    low = product[:rows, columns:] + product[rows:, :columns]
    return product[:rows, :columns] + (low + product[rows:, columns:])


def params(moved):
    grant = min(VMEM_MOST, max(VMEM_LEAST, 3 * moved))
    return pltpu.CompilerParams(vmem_limit_bytes=grant)


def call(kernel, out_shape, in_specs, flops, moved, scratch=(), out_spec=WHOLE):
    return pl.pallas_call(
        kernel,
        out_shape=out_shape,
        in_specs=in_specs,
        out_specs=jax.tree.map(lambda _: out_spec, out_shape),
        scratch_shapes=scratch,
        compiler_params=params(moved),
        cost_estimate=pl.CostEstimate(flops=flops, bytes_accessed=moved, transcendentals=0),
    )


class Place:
    def __init__(self, geo, order_ref):
        self.geo = geo
        self.a, self.b = lax.axis_index("outer"), lax.axis_index("inner")
        self.first = lax.axis_index("order") * geo.m_local
        self.order_ref = order_ref

    def order(self, m):
        return self.order_ref[self.first + m]

    def outer(self, shift):
        return lax.rem(self.a + (self.geo.outer - shift), self.geo.outer)

    def inner(self, shift):
        return lax.rem(self.b + (self.geo.inner - shift), self.geo.inner)

    def among(self, table, b=None):
        index = self.a * self.geo.inner + (self.b if b is None else b)
        return choose(index, [value for row in table for value in row])


def choose(index, values):
    result = jnp.int32(values[0])
    for i, value in enumerate(values[1:], 1):
        result = jnp.where(index == i, jnp.int32(value), result)
    return result


def take(leg_ref, m, index, starts, width):
    degrees = leg_ref.shape[2]
    start = pl.multiple_of(choose(index, starts), LANES)
    last = None
    for i, first in enumerate(starts):
        first = first + width - LANES
        tile = leg_ref[m, :, first : min(first + LANES, degrees)]
        if tile.shape[1] < LANES:
            fill = jnp.zeros((tile.shape[0], LANES - tile.shape[1]), jnp.float32)
            tile = jnp.concatenate([tile, fill], axis=1)
        last = tile if last is None else jnp.where(index == i, tile, last)
    return jnp.concatenate([leg_ref[m, :, pl.ds(start, width - LANES)], last], axis=1)


def exact_window(geo, leg_ref, m, block):
    wide = take(leg_ref, m, block, geo.window_starts, geo.take_width)
    back = lax.rem(geo.take_width - choose(block, geo.window_shifts), geo.take_width)
    return pltpu.roll(wide, back, 1)[:, : geo.window]


def inner_block(geo, window, target):
    result = None
    for b, start in enumerate(geo.block_starts):
        piece = window[:, start : start + geo.block_window]
        result = piece if result is None else jnp.where(target == b, piece, result)
    return result


def cut_windows(geo, leg_hbm, *refs):
    send_refs, (leg_ref, sem) = refs[:-2], refs[-2:]
    fetch = pltpu.make_async_copy(leg_hbm, leg_ref, sem)
    fetch.start()
    a = lax.axis_index("outer")
    fetch.wait()
    m_local, rows = leg_ref.shape[:2]
    lane = lax.broadcasted_iota(jnp.int32, (rows, LANES), 1)
    for shift, ref in enumerate(send_refs, 1):
        block = lax.rem(a + shift, geo.outer)
        tiles = [None] * geo.rest_tiles
        for m in range(m_local):
            window = exact_window(geo, leg_ref, m, block)
            ref[:, m * geo.main : (m + 1) * geo.main] = window[:, : geo.main]
            if geo.rest:
                at, place = divmod(m, geo.rest_each)
                tile = jnp.where(lane < geo.rest, window[:, geo.main :], 0.0)
                if place:
                    tile = pltpu.roll(tile, place * geo.rest, 1)
                tiles[at] = tile if tiles[at] is None else tiles[at] + tile
        for i, tile in enumerate(tiles):
            start = m_local * geo.main + i * LANES
            ref[:, start : start + LANES] = tile


def unpack_window(geo, ref, m):
    window = ref[:, m * geo.main : (m + 1) * geo.main]
    if geo.rest:
        at, place = divmod(m, geo.rest_each)
        start = geo.m_local * geo.main + at * LANES
        tile = ref[:, start : start + LANES]
        if place:
            tile = pltpu.roll(tile, LANES - place * geo.rest, 1)
        window = jnp.concatenate([window, tile], axis=1)
    return window


def fold(x):
    rows, width = x.shape
    folded = None
    for start in range(0, width, LANES):
        piece = x[:, start : min(start + LANES, width)]
        if piece.shape[1] < LANES:
            fill = jnp.zeros((rows, LANES - piece.shape[1]), jnp.float32)
            piece = jnp.concatenate([piece, fill], axis=1)
        folded = piece if folded is None else folded + piece
    return folded


def to_line(folded):
    return jnp.sum(jnp.transpose(folded), axis=0, keepdims=True)


def prepare(geo, order_ref, leg_hbm, *refs):
    parts = refs[: geo.inner]
    out_ref, rows_ref, valid_ref, *cuts, leg_ref, sem = refs[geo.inner :]
    fetch = pltpu.make_async_copy(leg_hbm, leg_ref, sem)
    fetch.start()
    place = Place(geo, order_ref)
    m_local, sin_cos, samples, width = parts[0].shape
    window = out_ref.shape[2]
    line = sin_cos * samples
    start = place.a * geo.pair
    piece = 16
    steps = samples // piece
    shifts = [choose(place.inner(shift), geo.places) for shift in range(geo.inner)]
    degree = start + lax.broadcasted_iota(jnp.int32, (piece, window), 1)

    def one(i):
        m, rest = lax.div(i, sin_cos * steps), lax.rem(i, sin_cos * steps)
        s, k = lax.div(rest, steps), lax.rem(rest, steps) * piece
        total = None
        for shift, part in zip(shifts, parts):
            block = part[m, s, pl.ds(pl.multiple_of(k, piece), piece), :]
            fill = jnp.zeros((piece, window - width), jnp.float32)
            block = pltpu.roll(jnp.concatenate([block, fill], axis=1), shift, 1)
            total = block if total is None else total + block
        total = jnp.where(degree >= place.order(m), total, 0.0)
        hi, lo = split_bf16(total)
        at = rest * piece
        out_ref[m, pl.ds(pl.multiple_of(at, piece), piece)] = hi
        out_ref[m, pl.ds(pl.multiple_of(line + at, piece), piece)] = lo

    repeat(m_local * sin_cos * steps, one)
    own = place.among(geo.own_starts) + lax.broadcasted_iota(jnp.int32, valid_ref.shape[1:], 1)
    for m in range(m_local):
        valid_ref[m] = (own >= place.order(m)).astype(jnp.float32)
    fetch.wait()

    def rows(m):
        leg = exact_window(geo, leg_ref, m, place.a)
        rows_ref[m] = synthesis(leg, out_ref, m)
        for shift, ref in enumerate(cuts):
            ref[m] = inner_block(geo, leg, lax.rem(place.b + shift, geo.inner))

    repeat(m_local, rows)


def synthesis(leg, dir_ref, m):
    rows, line = leg.shape[0], dir_ref.shape[1] // 2
    halves = jnp.concatenate(split_bf16(leg), axis=0)
    return dot_pairs(halves, dir_ref[m], ((1,), (1,)), rows, line)


def synthesise_rest(geo, own_ref, *refs):
    others = geo.outer - 1
    legs, (dir_ref, out_ref, *cuts) = refs[:others], refs[others:]
    place = Place(geo, None)
    rows = out_ref.shape[3]

    def put(m, shift, part):
        a = place.outer(shift)
        for o in range(out_ref.shape[0]):
            out_ref[o, a, m] = part[o * rows : (o + 1) * rows]

    for m in range(own_ref.shape[0]):
        put(m, 0, own_ref[m])
        for shift in range(1, geo.outer):
            leg = unpack_window(geo, legs[shift - 1], m)
            put(m, shift, synthesis(leg, dir_ref, m))
            for ahead, ref in enumerate(cuts):
                ref[shift - 1, m] = inner_block(geo, leg, lax.rem(place.b + ahead, geo.inner))


def weight_tables(longitudes, period, class_ref, land_ref, value_ref, basis_ref, out_ref):
    classes = class_ref[...]
    on_land = land_ref[...] == 1
    weight = jnp.zeros(classes.shape, jnp.float32)
    for c in range(value_ref.shape[0]):
        value = jnp.where(on_land, value_ref[c, 1], value_ref[c, 0])
        weight = jnp.where(classes == c, value, weight)
    rows = classes.shape[0]
    folded = jnp.zeros((rows, LANES), jnp.float32)
    for start in range(0, longitudes, LANES):
        piece = weight[:, start : min(start + LANES, longitudes)]
        if piece.shape[1] < LANES:
            piece = jnp.concatenate(
                [piece, jnp.zeros((rows, LANES - piece.shape[1]), jnp.float32)], axis=1
            )
        folded = folded + piece
    moments = lax.dot_general(
        folded,
        basis_ref[...],
        (((1,), (0,)), ((), ())),
        precision=HIGHEST,
        preferred_element_type=jnp.float32,
    )
    lane = lax.broadcasted_iota(jnp.int32, (rows, LANES), 1)
    sign = jnp.where(lane < LANES // 2, 1.0, -1.0)
    count = out_ref.shape[1]
    for n in range(count):
        even = jnp.broadcast_to(moments[:, n : n + 1], (rows, LANES))
        odd = jnp.broadcast_to(moments[:, count + n : count + n + 1], (rows, LANES))
        out_ref[0, n] = even
        out_ref[1, n] = sign * even
        out_ref[2, n] = odd
        out_ref[3, n] = sign * odd


def grid_rows(geo, stride, order_ref, recv_ref, table_ref, out_ref, plain, swapped, done):
    orders = plain.shape[0]
    m_local, each = recv_ref.shape[1], out_ref.shape[1]
    at = order_ref[...]
    slot = [lax.div(at[0, m], jnp.int32(stride)) for m in range(orders)]
    for m in range(orders):
        o, i = divmod(m, m_local)
        total = recv_ref[o * geo.outer, i]
        for a in range(1, geo.outer):
            total = total + recv_ref[o * geo.outer + a, i]
        at = slot[m]
        plain[at] = total
        swapped[at] = pltpu.roll(total, LANES // 2, 1)
    for i in range(orders):
        total = None
        for j in range(orders):
            cos_part = table_ref[0, abs(i - j)] + table_ref[1, i + j]
            if i >= j:
                sin_part = table_ref[2, i + j] - table_ref[3, i - j]
            else:
                sin_part = table_ref[2, i + j] + table_ref[3, j - i]
            term = cos_part * plain[j] + sin_part * swapped[j]
            total = term if total is None else total + term
        done[i] = total
    for m in range(orders):
        o, i = divmod(m, m_local)
        b, i = divmod(i, each)
        value = done[slot[m]]
        for a in range(geo.outer):
            out_ref[(o * geo.outer + a) * geo.inner + b, i] = value


def project(geo, shift, valid_ref, recv_ref, *refs):
    legs, refs = refs[: 2 * geo.inner], refs[2 * geo.inner :]
    dir_ref, res_ref, damp_ref = refs[:3]
    before_ref = refs[3] if shift else None
    app_ref, sums_ref = refs[-2:]
    place = Place(geo, None)
    each, sin_cos, samples, width = app_ref.shape
    first = place.inner(shift) * each
    window = geo.block_window
    copies = geo.outer * geo.inner
    order_devices = recv_ref.shape[0] // copies
    damping = damp_ref[...]
    rows = sin_cos * samples
    offsets = [p - s for p, s in zip(geo.places, geo.block_starts)]
    back = window - choose(place.b, offsets)

    def products(i):
        tiles, blocks = [], []
        for b in range(geo.inner):
            for a in range(geo.outer):
                band = place.outer(a) * geo.inner + place.inner(b)
                if a == 0:
                    blocks.append(legs[b][first + i])
                else:
                    blocks.append(legs[geo.inner + b][a - 1, first + i])
                for o in range(order_devices):
                    tiles.append(recv_ref[o * copies + band, i])
        hi, lo = split_bf16(jnp.concatenate(tiles, axis=0))
        high, low = split_bf16(jnp.concatenate(blocks, axis=0))
        dims = (((0,), (0,)), ((), ()))
        both = jnp.concatenate([hi, lo], axis=1)
        main = lax.dot_general(both, high, dims, preferred_element_type=jnp.float32)
        rest = lax.dot_general(hi, low, dims, preferred_element_type=jnp.float32)
        summed = main[:rows] + (main[rows:] + rest)
        summed = pltpu.roll(summed, back, 1)[:, :width]
        for s in range(sin_cos):
            app_ref[i, s] = summed[s * samples : (s + 1) * samples]

    repeat(each, products)

    def apply(at, sums):
        i, s = lax.div(at, sin_cos), lax.rem(at, sin_cos)
        valid = valid_ref[first + i, 0:1]
        direction = dir_ref[first + i, s] * valid
        residual = res_ref[first + i, s] * valid
        applied = app_ref[i, s] * valid + damping * direction
        app_ref[i, s] = applied
        terms = (
            residual * residual,
            direction * applied,
            residual * applied,
            applied * applied,
        )
        return tuple(old + fold(t) for old, t in zip(sums, terms))

    if shift:
        start = tuple(before_ref[i * samples : (i + 1) * samples] for i in range(4))
    else:
        start = (jnp.zeros((samples, LANES), jnp.float32),) * 4
    sums = lax.fori_loop(0, each * sin_cos, apply, start)
    stacked = jnp.concatenate(sums, axis=0)
    if shift < geo.inner - 1:
        sums_ref[...] = stacked
    else:
        line = to_line(stacked)

        def give(device):
            sums_ref[device] = line

        repeat(sums_ref.shape[0], give)


def update(geo, valid_ref, sums_ref, *refs):
    apps, refs = refs[: geo.inner], refs[geo.inner :]
    pos_ref, dir_ref, res_ref, *refs = refs
    outs, bufs, sems = refs[:3], refs[3:6], refs[6]
    place = Place(geo, None)
    m_local, sin_cos, samples, width = dir_ref.shape
    totals = jnp.sum(sums_ref[...], axis=0)
    before, curvature, cross, square = [
        totals[:, i * samples : (i + 1) * samples] for i in range(4)
    ]
    step_row = before / curvature
    after = before - 2.0 * step_row * cross + step_row * step_row * square
    ratio_row = after / before
    row = lax.broadcasted_iota(jnp.int32, (samples, samples), 0)
    column = lax.broadcasted_iota(jnp.int32, (samples, samples), 1)
    diagonal = row == column
    step = jnp.sum(jnp.where(diagonal, step_row, 0.0), axis=1, keepdims=True)
    ratio = jnp.sum(jnp.where(diagonal, ratio_row, 0.0), axis=1, keepdims=True)

    def copy(i, m, s):
        return pltpu.make_async_copy(bufs[i].at[m, s], outs[i].at[m, s], sems.at[i, m, s])

    each = m_local // geo.inner
    for shift, app_ref in enumerate(apps):

        def one(at, shift=shift, app_ref=app_ref):
            i, s = lax.div(at, sin_cos), lax.rem(at, sin_cos)
            m = place.inner(shift) * each + i
            valid = valid_ref[m, 0:1]
            direction = dir_ref[m, s] * valid
            residual = res_ref[m, s] * valid
            position = pos_ref[m, s] * valid
            new_residual = residual - step * app_ref[i, s]
            values = (
                position + step * direction,
                new_residual,
                new_residual + ratio * direction,
            )
            for i in range(3):
                bufs[i][m, s] = values[i]
                copy(i, m, s).start()

        repeat(each * sin_cos, one)

    def end(at):
        for i in range(3):
            copy(i, lax.div(at, sin_cos), lax.rem(at, sin_cos)).wait()

    repeat(m_local * sin_cos, end)


class Geometry:
    def __init__(self, outer, inner, degrees, m_local):
        self.outer, self.inner, self.m_local = outer, inner, m_local
        block = degrees // (outer * inner)

        def down(x):
            return x // LANES * LANES

        def up(x):
            return -(-x // LANES) * LANES

        pair = degrees // outer
        self.pair = pair
        self.own_starts = [[(a * inner + b) * block for b in range(inner)] for a in range(outer)]
        self.window_starts = [down(a * pair) for a in range(outer)]
        self.window_shifts = [a * pair - s for a, s in enumerate(self.window_starts)]
        self.take_width = max(up(s + pair) for s in self.window_shifts)
        self.window = up(pair)
        self.places = [b * block for b in range(inner)]
        self.block_window = max(up(p + block) - down(p) for p in self.places)
        self.block_starts = [min(down(p), self.window - self.block_window) for p in self.places]
        self.main = down(pair)
        self.rest = pair - self.main
        self.rest_each = LANES // self.rest if self.rest else 1
        self.rest_tiles = -(-m_local // self.rest_each) if self.rest else 0
        self.packed = m_local * self.main + self.rest_tiles * LANES


def far(x):
    return pltpu.with_memory_space_constraint(x, pltpu.HBM)


def rotate(x, axis, size, shift):
    return lax.ppermute(x, axis, [(i, (i + shift) % size) for i in range(size)])


def plain_grid(geo, grid_in, order_of, class_idx, land, class_weight, period):
    order_devices = grid_in.shape[0] // geo.outer
    m_local, rows, width = grid_in.shape[1:]
    orders = order_devices * m_local
    longitudes = class_idx.shape[1]
    stacked = grid_in.reshape(order_devices, geo.outer, m_local, rows, 2, width // 2)
    stacked = jnp.sum(stacked, axis=1).reshape(orders, rows, 2, width // 2)
    phases = order_of[:, None] * jnp.arange(period, dtype=jnp.int32)[None, :] % longitudes
    angles = phases.astype(jnp.float32) * (2.0 * math.pi / longitudes)
    harmonic = jnp.stack([jnp.cos(angles), jnp.sin(angles)])
    surface = jnp.einsum("mrsk,smp->rkp", stacked, harmonic, precision=HIGHEST)
    onehot = class_idx[:, :, None] == jnp.arange(class_weight.shape[0], dtype=jnp.int32)
    by_class = jnp.dot(onehot.astype(jnp.float32), class_weight, precision=HIGHEST)
    weight = jnp.where(land == 1, by_class[:, :, 1], by_class[:, :, 0])
    folded = jnp.sum(weight.reshape(rows, longitudes // period, period), axis=1)
    weighted = surface * folded[:, None, :]
    spectra = jnp.einsum("rkp,smp->mrsk", weighted, harmonic, precision=HIGHEST)
    each = m_local // geo.inner
    spectra = spectra * (2.0 / longitudes)
    spectra = spectra.reshape(order_devices, 1, geo.inner, each, rows, width)
    spectra = jnp.broadcast_to(
        spectra, (order_devices, geo.outer, geo.inner, each, rows, width)
    )
    return spectra.reshape(order_devices * geo.outer * geo.inner, each, rows, width)


def shards(
    outer,
    inner,
    position,
    residual,
    direction,
    legendre,
    order_of,
    class_idx,
    land,
    class_weight,
    damping,
):
    m_local, sin_cos, samples, deg_local = position.shape
    degrees, band_rows = legendre.shape[1:]
    rows_here, longitudes = class_idx.shape
    orders = order_of.shape[0]
    order_devices = orders // m_local
    devices = order_devices * outer * inner
    each = m_local // inner
    line = sin_cos * samples
    geo = Geometry(outer, inner, degrees, m_local)
    by_row = jnp.transpose(legendre, (0, 2, 1))
    cut = pltpu.VMEM((band_rows, geo.packed), jnp.float32)
    leg_moved = 4 * m_local * band_rows * degrees
    leg_scratch = [pltpu.VMEM(by_row.shape, jnp.float32), pltpu.SemaphoreType.DMA(())]
    cuts = call(
        functools.partial(cut_windows, geo),
        (cut,) * (outer - 1),
        [IN_HBM],
        m_local * band_rows * geo.window,
        8 * outer * m_local * band_rows * geo.window,
        leg_scratch,
    )(far(by_row))
    received = [rotate(cuts[s - 1], "outer", outer, s) for s in range(1, outer)]
    stride = longitudes // (2 * orders)
    period = longitudes // stride if longitudes % stride == 0 else longitudes
    small = orders <= 16 and LANES % period == 0 and line == LANES and longitudes % period == 0
    if small:
        count = 2 * orders
        n = np.arange(count)[None, :]
        p = np.arange(LANES)[:, None]
        angle = 2.0 * math.pi * ((n * p) % period) / period
        basis = np.zeros((LANES, -(-2 * count // LANES) * LANES), np.float32)
        basis[:, :count] = np.cos(angle) / longitudes
        basis[:, count : 2 * count] = np.sin(angle) / longitudes
        tables = call(
            functools.partial(weight_tables, longitudes, period),
            jax.ShapeDtypeStruct((4, count, rows_here, LANES), jnp.float32),
            [WHOLE, WHOLE, SCALARS, WHOLE],
            100 * rows_here * longitudes,
            8 * rows_here * longitudes,
        )(class_idx, land, class_weight, jnp.asarray(basis))

    siblings = [rotate(direction, "inner", inner, s) for s in range(1, inner)]
    if small:
        siblings, tables = lax.optimization_barrier((siblings, tables))
    own_flops = 8 * m_local * line * geo.window * band_rows
    dir_window, own_rows, valid, *own_blocks = call(
        functools.partial(prepare, geo),
        (
            jax.ShapeDtypeStruct((m_local, 2 * line, geo.window), jnp.bfloat16),
            jax.ShapeDtypeStruct((m_local, band_rows, line), jnp.float32),
            jax.ShapeDtypeStruct((m_local, 8, deg_local), jnp.float32),
        )
        + (jax.ShapeDtypeStruct((m_local, band_rows, geo.block_window), jnp.float32),) * inner,
        [SCALARS, IN_HBM] + [WHOLE] * inner,
        own_flops,
        8 * m_local * line * geo.window + leg_moved,
        leg_scratch,
    )(order_of, far(by_row), direction, *siblings)
    first_legs = [own_blocks[0]]
    first_legs += [rotate(own_blocks[s], "inner", inner, s) for s in range(1, inner)]

    received, first_legs = lax.optimization_barrier((received, first_legs))
    block = jax.ShapeDtypeStruct((outer - 1, m_local, band_rows, geo.block_window), jnp.float32)
    to_rows, *blocks = call(
        functools.partial(synthesise_rest, geo),
        (jax.ShapeDtypeStruct((order_devices, outer, m_local, rows_here, line), jnp.float32),)
        + (block,) * inner,
        [WHOLE] * (outer + 1),
        own_flops * (outer - 1),
        4 * m_local * (line + band_rows) * geo.window,
    )(own_rows, *received, dir_window)
    rest_legs = [blocks[0]]
    rest_legs += [rotate(blocks[s], "inner", inner, s) for s in range(1, inner)]
    grid_in = lax.all_to_all(
        to_rows.reshape(order_devices * outer, m_local, rows_here, line),
        ("order", "outer"),
        split_axis=0,
        concat_axis=0,
        tiled=True,
    )

    grid_in, rest_legs = lax.optimization_barrier((grid_in, rest_legs))
    if small:
        to_orders = call(
            functools.partial(grid_rows, geo, stride),
            jax.ShapeDtypeStruct((devices, each, rows_here, line), jnp.float32),
            [WHOLE, WHOLE, WHOLE],
            6 * orders * orders * rows_here * line,
            8 * orders * rows_here * line,
            [pltpu.VMEM((orders, rows_here, line), jnp.float32)] * 3,
        )(order_of[None, :], grid_in, tables)
    else:
        to_orders = plain_grid(geo, grid_in, order_of, class_idx, land, class_weight, period)
    spectra = lax.all_to_all(
        to_orders, ("order", "outer", "inner"), split_axis=0, concat_axis=0, tiled=True
    )
    shares = [spectra] + [rotate(spectra, "inner", inner, s) for s in range(1, inner)]
    coefficients = jax.ShapeDtypeStruct(position.shape, jnp.float32)
    part = (each,) + position.shape[1:]
    sums = ()
    applied = []
    for shift, share in enumerate(shares):
        if shift < inner - 1:
            sums_out = jax.ShapeDtypeStruct((4 * samples, LANES), jnp.float32)
        else:
            sums_out = jax.ShapeDtypeStruct((devices, 1, 4 * samples), jnp.float32)
        result, sums = call(
            functools.partial(project, geo, shift),
            (jax.ShapeDtypeStruct(part, jnp.float32), sums_out),
            [WHOLE] * (5 + 2 * inner + (shift > 0)),
            6 * each * line * geo.block_window * band_rows * outer * inner,
            16 * each * line * deg_local,
        )(
            valid,
            share,
            *first_legs,
            *rest_legs,
            direction,
            residual,
            damping[None, :],
            *((sums,) if shift else ()),
        )
        applied.append(result)
    sums = lax.all_to_all(
        sums, ("order", "outer", "inner"), split_axis=0, concat_axis=0, tiled=True
    )
    return call(
        functools.partial(update, geo),
        (coefficients,) * 3,
        [WHOLE] * (5 + inner),
        10 * m_local * line * deg_local,
        28 * m_local * line * deg_local,
        [pltpu.VMEM(position.shape, jnp.float32)] * 3
        + [pltpu.SemaphoreType.DMA((3, m_local, sin_cos))],
        IN_HBM,
    )(valid, sums, *applied, position, direction, residual)


def solution(mesh):
    order_devices, bands = mesh.shape["order"], mesh.shape["lat"]
    outer = 2 if bands % 2 == 0 else 1
    inner = bands // outer
    split = Mesh(mesh.devices.reshape(order_devices, outer, inner), ("order", "outer", "inner"))
    lat = ("outer", "inner")
    coefficients = P("order", None, None, lat)
    grid = P(("outer", "inner", "order"), None)
    return jax.shard_map(
        functools.partial(shards, outer, inner),
        mesh=split,
        in_specs=(
            coefficients,
            coefficients,
            coefficients,
            P("order", None, lat),
            P(),
            grid,
            grid,
            P(),
            P(lat),
        ),
        out_specs=(coefficients,) * 3,
        check_vma=False,
    )
```

```python
import functools
import math

import jax
import jax.numpy as jnp
import numpy as np
from jax import lax
from jax.experimental import pallas as pl
from jax.experimental.pallas import tpu as pltpu
from jax.sharding import Mesh
from jax.sharding import PartitionSpec as P

LANES = 128
HIGHEST = lax.Precision.HIGHEST
VMEM_LEAST = 16 * 1024 * 1024
VMEM_MOST = 48 * 1024 * 1024
WHOLE = pl.BlockSpec(memory_space=pltpu.VMEM)
SCALARS = pl.BlockSpec(memory_space=pltpu.SMEM)
IN_HBM = pl.BlockSpec(memory_space=pltpu.HBM)


def repeat(count, body):
    lax.fori_loop(0, count, lambda i, carry: (body(i), carry)[1], 0)


def split_bf16(x):
    hi = x.astype(jnp.bfloat16)
    lo = (x - hi.astype(jnp.float32)).astype(jnp.bfloat16)
    return hi, lo


def dot_pairs(a, b, dims, rows, columns):
    product = lax.dot_general(a, b, (dims, ((), ())), preferred_element_type=jnp.float32)
    low = product[:rows, columns:] + product[rows:, :columns]
    return product[:rows, :columns] + (low + product[rows:, columns:])


def params(moved):
    grant = min(VMEM_MOST, max(VMEM_LEAST, 3 * moved))
    return pltpu.CompilerParams(vmem_limit_bytes=grant)


def call(kernel, out_shape, in_specs, flops, moved, scratch=(), out_spec=WHOLE, cost=0):
    return pl.pallas_call(
        kernel,
        out_shape=out_shape,
        in_specs=in_specs,
        out_specs=jax.tree.map(lambda _: out_spec, out_shape),
        scratch_shapes=scratch,
        compiler_params=params(moved),
        cost_estimate=pl.CostEstimate(flops=flops, bytes_accessed=cost or moved, transcendentals=0),
    )


class Place:
    def __init__(self, geo, order_ref):
        self.geo = geo
        self.a, self.b = lax.axis_index("outer"), lax.axis_index("inner")
        self.first = lax.axis_index("order") * geo.m_local
        self.order_ref = order_ref

    def order(self, m):
        return self.order_ref[self.first + m]

    def outer(self, shift):
        return lax.rem(self.a + (self.geo.outer - shift), self.geo.outer)

    def inner(self, shift):
        return lax.rem(self.b + (self.geo.inner - shift), self.geo.inner)

    def among(self, table, b=None):
        index = self.a * self.geo.inner + (self.b if b is None else b)
        return choose(index, [value for row in table for value in row])


def choose(index, values):
    result = jnp.int32(values[0])
    for i, value in enumerate(values[1:], 1):
        result = jnp.where(index == i, jnp.int32(value), result)
    return result


def take(leg_ref, m, index, starts, width):
    degrees = leg_ref.shape[2]
    start = pl.multiple_of(choose(index, starts), LANES)
    last = None
    for i, first in enumerate(starts):
        first = first + width - LANES
        tile = leg_ref[m, :, first : min(first + LANES, degrees)]
        if tile.shape[1] < LANES:
            fill = jnp.zeros((tile.shape[0], LANES - tile.shape[1]), jnp.float32)
            tile = jnp.concatenate([tile, fill], axis=1)
        last = tile if last is None else jnp.where(index == i, tile, last)
    return jnp.concatenate([leg_ref[m, :, pl.ds(start, width - LANES)], last], axis=1)


def exact_window(geo, leg_ref, m, block):
    wide = take(leg_ref, m, block, geo.window_starts, geo.take_width)
    back = lax.rem(geo.take_width - choose(block, geo.window_shifts), geo.take_width)
    return pltpu.roll(wide, back, 1)[:, : geo.window]


def inner_block(geo, window, target):
    result = None
    for b, start in enumerate(geo.block_starts):
        piece = window[:, start : start + geo.block_window]
        result = piece if result is None else jnp.where(target == b, piece, result)
    return result


def cut_windows(geo, leg_hbm, *refs):
    send_refs, (leg_ref, sem) = refs[:-2], refs[-2:]
    fetch = pltpu.make_async_copy(leg_hbm, leg_ref, sem)
    fetch.start()
    a = lax.axis_index("outer")
    fetch.wait()
    m_local, rows = leg_ref.shape[:2]
    lane = lax.broadcasted_iota(jnp.int32, (rows, LANES), 1)
    for shift, ref in enumerate(send_refs, 1):
        block = lax.rem(a + shift, geo.outer)
        tiles = [None] * geo.rest_tiles
        for m in range(m_local):
            window = exact_window(geo, leg_ref, m, block)
            ref[:, m * geo.main : (m + 1) * geo.main] = window[:, : geo.main]
            if geo.rest:
                at, place = divmod(m, geo.rest_each)
                tile = jnp.where(lane < geo.rest, window[:, geo.main :], 0.0)
                if place:
                    tile = pltpu.roll(tile, place * geo.rest, 1)
                tiles[at] = tile if tiles[at] is None else tiles[at] + tile
        for i, tile in enumerate(tiles):
            start = m_local * geo.main + i * LANES
            ref[:, start : start + LANES] = tile


def unpack_window(geo, ref, m):
    window = ref[:, m * geo.main : (m + 1) * geo.main]
    if geo.rest:
        at, place = divmod(m, geo.rest_each)
        start = geo.m_local * geo.main + at * LANES
        tile = ref[:, start : start + LANES]
        if place:
            tile = pltpu.roll(tile, LANES - place * geo.rest, 1)
        window = jnp.concatenate([window, tile], axis=1)
    return window


def fold(x):
    rows, width = x.shape
    folded = None
    for start in range(0, width, LANES):
        piece = x[:, start : min(start + LANES, width)]
        if piece.shape[1] < LANES:
            fill = jnp.zeros((rows, LANES - piece.shape[1]), jnp.float32)
            piece = jnp.concatenate([piece, fill], axis=1)
        folded = piece if folded is None else folded + piece
    return folded


def to_line(folded):
    return jnp.sum(jnp.transpose(folded), axis=0, keepdims=True)


def prepare(geo, order_ref, leg_hbm, *refs):
    parts = refs[: geo.inner]
    out_ref, rows_ref, valid_ref, *cuts, leg_ref, sem = refs[geo.inner :]
    fetch = pltpu.make_async_copy(leg_hbm, leg_ref, sem)
    fetch.start()
    place = Place(geo, order_ref)
    m_local, sin_cos, samples, width = parts[0].shape
    window = out_ref.shape[2]
    line = sin_cos * samples
    start = place.a * geo.pair
    piece = 16
    steps = samples // piece
    shifts = [choose(place.inner(shift), geo.places) for shift in range(geo.inner)]
    degree = start + lax.broadcasted_iota(jnp.int32, (piece, window), 1)

    def one(i):
        m, rest = lax.div(i, sin_cos * steps), lax.rem(i, sin_cos * steps)
        s, k = lax.div(rest, steps), lax.rem(rest, steps) * piece
        total = None
        for shift, part in zip(shifts, parts):
            block = part[m, s, pl.ds(pl.multiple_of(k, piece), piece), :]
            fill = jnp.zeros((piece, window - width), jnp.float32)
            block = pltpu.roll(jnp.concatenate([block, fill], axis=1), shift, 1)
            total = block if total is None else total + block
        total = jnp.where(degree >= place.order(m), total, 0.0)
        hi, lo = split_bf16(total)
        at = rest * piece
        out_ref[m, pl.ds(pl.multiple_of(at, piece), piece)] = hi
        out_ref[m, pl.ds(pl.multiple_of(line + at, piece), piece)] = lo

    repeat(m_local * sin_cos * steps, one)
    own = place.among(geo.own_starts) + lax.broadcasted_iota(jnp.int32, valid_ref.shape[1:], 1)
    for m in range(m_local):
        valid_ref[m] = (own >= place.order(m)).astype(jnp.float32)
    fetch.wait()

    def rows(m):
        leg = exact_window(geo, leg_ref, m, place.a)
        rows_ref[m] = synthesis(leg, out_ref, m)
        for shift, ref in enumerate(cuts):
            ref[m] = inner_block(geo, leg, lax.rem(place.b + shift, geo.inner))

    repeat(m_local, rows)


def synthesis(leg, dir_ref, m):
    rows, line = leg.shape[0], dir_ref.shape[1] // 2
    halves = jnp.concatenate(split_bf16(leg), axis=0)
    return dot_pairs(halves, dir_ref[m], ((1,), (1,)), rows, line)


def synthesise_rest(geo, own_ref, *refs):
    others = geo.outer - 1
    legs, (dir_ref, out_ref, *cuts) = refs[:others], refs[others:]
    place = Place(geo, None)
    rows = out_ref.shape[3]

    def put(m, shift, part):
        a = place.outer(shift)
        for o in range(out_ref.shape[0]):
            out_ref[o, a, m] = part[o * rows : (o + 1) * rows]

    for m in range(own_ref.shape[0]):
        put(m, 0, own_ref[m])
        for shift in range(1, geo.outer):
            leg = unpack_window(geo, legs[shift - 1], m)
            put(m, shift, synthesis(leg, dir_ref, m))
            for ahead, ref in enumerate(cuts):
                ref[shift - 1, m] = inner_block(geo, leg, lax.rem(place.b + ahead, geo.inner))


def weight_tables(longitudes, period, class_ref, land_ref, value_ref, basis_ref, out_ref):
    classes = class_ref[...]
    on_land = land_ref[...] == 1
    weight = jnp.zeros(classes.shape, jnp.float32)
    for c in range(value_ref.shape[0]):
        value = jnp.where(on_land, value_ref[c, 1], value_ref[c, 0])
        weight = jnp.where(classes == c, value, weight)
    rows = classes.shape[0]
    folded = jnp.zeros((rows, LANES), jnp.float32)
    for start in range(0, longitudes, LANES):
        piece = weight[:, start : min(start + LANES, longitudes)]
        if piece.shape[1] < LANES:
            piece = jnp.concatenate(
                [piece, jnp.zeros((rows, LANES - piece.shape[1]), jnp.float32)], axis=1
            )
        folded = folded + piece
    moments = lax.dot_general(
        folded,
        basis_ref[...],
        (((1,), (0,)), ((), ())),
        precision=HIGHEST,
        preferred_element_type=jnp.float32,
    )
    lane = lax.broadcasted_iota(jnp.int32, (rows, LANES), 1)
    sign = jnp.where(lane < LANES // 2, 1.0, -1.0)
    count = out_ref.shape[1]
    for n in range(count):
        even = jnp.broadcast_to(moments[:, n : n + 1], (rows, LANES))
        odd = jnp.broadcast_to(moments[:, count + n : count + n + 1], (rows, LANES))
        out_ref[0, n] = even
        out_ref[1, n] = sign * even
        out_ref[2, n] = odd
        out_ref[3, n] = sign * odd


def grid_rows(geo, stride, order_ref, recv_ref, table_ref, out_ref, plain, swapped, done):
    orders = plain.shape[0]
    m_local, each = recv_ref.shape[1], out_ref.shape[1]
    at = order_ref[...]
    slot = [lax.div(at[0, m], jnp.int32(stride)) for m in range(orders)]
    for m in range(orders):
        o, i = divmod(m, m_local)
        total = recv_ref[o * geo.outer, i]
        for a in range(1, geo.outer):
            total = total + recv_ref[o * geo.outer + a, i]
        at = slot[m]
        plain[at] = total
        swapped[at] = pltpu.roll(total, LANES // 2, 1)
    for i in range(orders):
        total = None
        for j in range(orders):
            cos_part = table_ref[0, abs(i - j)] + table_ref[1, i + j]
            if i >= j:
                sin_part = table_ref[2, i + j] - table_ref[3, i - j]
            else:
                sin_part = table_ref[2, i + j] + table_ref[3, j - i]
            term = cos_part * plain[j] + sin_part * swapped[j]
            total = term if total is None else total + term
        done[i] = total
    for m in range(orders):
        o, i = divmod(m, m_local)
        b, i = divmod(i, each)
        value = done[slot[m]]
        for a in range(geo.outer):
            out_ref[(o * geo.outer + a) * geo.inner + b, i] = value


def project(geo, shift, valid_ref, recv_ref, *refs):
    legs, refs = refs[: 2 * geo.inner], refs[2 * geo.inner :]
    dir_ref, res_ref, damp_ref = refs[:3]
    before_ref = refs[3] if shift else None
    app_ref, sums_ref = refs[-2:]
    place = Place(geo, None)
    each, sin_cos, samples, width = app_ref.shape
    first = place.inner(shift) * each
    window = geo.block_window
    copies = geo.outer * geo.inner
    order_devices = recv_ref.shape[0] // copies
    damping = damp_ref[...]
    rows = sin_cos * samples
    offsets = [p - s for p, s in zip(geo.places, geo.block_starts)]
    back = window - choose(place.b, offsets)

    def products(i):
        tiles, blocks = [], []
        for b in range(geo.inner):
            for a in range(geo.outer):
                band = place.outer(a) * geo.inner + place.inner(b)
                if a == 0:
                    blocks.append(legs[b][first + i])
                else:
                    blocks.append(legs[geo.inner + b][a - 1, first + i])
                for o in range(order_devices):
                    tiles.append(recv_ref[o * copies + band, i])
        hi, lo = split_bf16(jnp.concatenate(tiles, axis=0))
        high, low = split_bf16(jnp.concatenate(blocks, axis=0))
        dims = (((0,), (0,)), ((), ()))
        both = jnp.concatenate([hi, lo], axis=1)
        main = lax.dot_general(both, high, dims, preferred_element_type=jnp.float32)
        rest = lax.dot_general(hi, low, dims, preferred_element_type=jnp.float32)
        summed = main[:rows] + (main[rows:] + rest)
        summed = pltpu.roll(summed, back, 1)[:, :width]
        for s in range(sin_cos):
            app_ref[i, s] = summed[s * samples : (s + 1) * samples]

    repeat(each, products)

    def apply(at, sums):
        i, s = lax.div(at, sin_cos), lax.rem(at, sin_cos)
        valid = valid_ref[first + i, 0:1]
        direction = dir_ref[first + i, s] * valid
        residual = res_ref[first + i, s] * valid
        applied = app_ref[i, s] * valid + damping * direction
        app_ref[i, s] = applied
        terms = (
            residual * residual,
            direction * applied,
            residual * applied,
            applied * applied,
        )
        return tuple(old + fold(t) for old, t in zip(sums, terms))

    if shift:
        start = tuple(before_ref[i * samples : (i + 1) * samples] for i in range(4))
    else:
        start = (jnp.zeros((samples, LANES), jnp.float32),) * 4
    sums = lax.fori_loop(0, each * sin_cos, apply, start)
    stacked = jnp.concatenate(sums, axis=0)
    if shift < geo.inner - 1:
        sums_ref[...] = stacked
    else:
        line = to_line(stacked)

        def give(device):
            sums_ref[device] = line

        repeat(sums_ref.shape[0], give)


def update(geo, valid_ref, sums_ref, *refs):
    apps, refs = refs[: geo.inner], refs[geo.inner :]
    pos_ref, dir_ref, res_ref, *refs = refs
    outs, bufs, sems = refs[:3], refs[3:6], refs[6]
    place = Place(geo, None)
    m_local, sin_cos, samples, width = dir_ref.shape
    totals = jnp.sum(sums_ref[...], axis=0)
    before, curvature, cross, square = [
        totals[:, i * samples : (i + 1) * samples] for i in range(4)
    ]
    step_row = before / curvature
    after = before - 2.0 * step_row * cross + step_row * step_row * square
    ratio_row = after / before
    row = lax.broadcasted_iota(jnp.int32, (samples, samples), 0)
    column = lax.broadcasted_iota(jnp.int32, (samples, samples), 1)
    diagonal = row == column
    step = jnp.sum(jnp.where(diagonal, step_row, 0.0), axis=1, keepdims=True)
    ratio = jnp.sum(jnp.where(diagonal, ratio_row, 0.0), axis=1, keepdims=True)

    def copy(i, m, s):
        return pltpu.make_async_copy(bufs[i].at[m, s], outs[i].at[m, s], sems.at[i, m, s])

    each = m_local // geo.inner
    for shift, app_ref in enumerate(apps):

        def one(at, shift=shift, app_ref=app_ref):
            i, s = lax.div(at, sin_cos), lax.rem(at, sin_cos)
            m = place.inner(shift) * each + i
            valid = valid_ref[m, 0:1]
            direction = dir_ref[m, s] * valid
            residual = res_ref[m, s] * valid
            position = pos_ref[m, s] * valid
            new_residual = residual - step * app_ref[i, s]
            values = (
                position + step * direction,
                new_residual,
                new_residual + ratio * direction,
            )
            for i in range(3):
                bufs[i][m, s] = values[i]
                copy(i, m, s).start()

        repeat(each * sin_cos, one)

    def end(at):
        for i in range(3):
            copy(i, lax.div(at, sin_cos), lax.rem(at, sin_cos)).wait()

    repeat(m_local * sin_cos, end)


class Geometry:
    def __init__(self, outer, inner, degrees, m_local):
        self.outer, self.inner, self.m_local = outer, inner, m_local
        block = degrees // (outer * inner)

        def down(x):
            return x // LANES * LANES

        def up(x):
            return -(-x // LANES) * LANES

        pair = degrees // outer
        self.pair = pair
        self.own_starts = [[(a * inner + b) * block for b in range(inner)] for a in range(outer)]
        self.window_starts = [down(a * pair) for a in range(outer)]
        self.window_shifts = [a * pair - s for a, s in enumerate(self.window_starts)]
        self.take_width = max(up(s + pair) for s in self.window_shifts)
        self.window = up(pair)
        self.places = [b * block for b in range(inner)]
        self.block_window = max(up(p + block) - down(p) for p in self.places)
        self.block_starts = [min(down(p), self.window - self.block_window) for p in self.places]
        self.main = down(pair)
        self.rest = pair - self.main
        self.rest_each = LANES // self.rest if self.rest else 1
        self.rest_tiles = -(-m_local // self.rest_each) if self.rest else 0
        self.packed = m_local * self.main + self.rest_tiles * LANES


def far(x):
    return pltpu.with_memory_space_constraint(x, pltpu.HBM)


def rotate(x, axis, size, shift):
    return lax.ppermute(x, axis, [(i, (i + shift) % size) for i in range(size)])


def plain_grid(geo, grid_in, order_of, class_idx, land, class_weight, period):
    order_devices = grid_in.shape[0] // geo.outer
    m_local, rows, width = grid_in.shape[1:]
    orders = order_devices * m_local
    longitudes = class_idx.shape[1]
    stacked = grid_in.reshape(order_devices, geo.outer, m_local, rows, 2, width // 2)
    stacked = jnp.sum(stacked, axis=1).reshape(orders, rows, 2, width // 2)
    phases = order_of[:, None] * jnp.arange(period, dtype=jnp.int32)[None, :] % longitudes
    angles = phases.astype(jnp.float32) * (2.0 * math.pi / longitudes)
    harmonic = jnp.stack([jnp.cos(angles), jnp.sin(angles)])
    surface = jnp.einsum("mrsk,smp->rkp", stacked, harmonic, precision=HIGHEST)
    onehot = class_idx[:, :, None] == jnp.arange(class_weight.shape[0], dtype=jnp.int32)
    by_class = jnp.dot(onehot.astype(jnp.float32), class_weight, precision=HIGHEST)
    weight = jnp.where(land == 1, by_class[:, :, 1], by_class[:, :, 0])
    folded = jnp.sum(weight.reshape(rows, longitudes // period, period), axis=1)
    weighted = surface * folded[:, None, :]
    spectra = jnp.einsum("rkp,smp->mrsk", weighted, harmonic, precision=HIGHEST)
    each = m_local // geo.inner
    spectra = spectra * (2.0 / longitudes)
    spectra = spectra.reshape(order_devices, 1, geo.inner, each, rows, width)
    spectra = jnp.broadcast_to(
        spectra, (order_devices, geo.outer, geo.inner, each, rows, width)
    )
    return spectra.reshape(order_devices * geo.outer * geo.inner, each, rows, width)


def shards(
    outer,
    inner,
    position,
    residual,
    direction,
    legendre,
    order_of,
    class_idx,
    land,
    class_weight,
    damping,
):
    m_local, sin_cos, samples, deg_local = position.shape
    degrees, band_rows = legendre.shape[1:]
    rows_here, longitudes = class_idx.shape
    orders = order_of.shape[0]
    order_devices = orders // m_local
    devices = order_devices * outer * inner
    each = m_local // inner
    line = sin_cos * samples
    geo = Geometry(outer, inner, degrees, m_local)
    by_row = jnp.transpose(legendre, (0, 2, 1))
    cut = pltpu.VMEM((band_rows, geo.packed), jnp.float32)
    leg_moved = 4 * m_local * band_rows * degrees
    leg_scratch = [pltpu.VMEM(by_row.shape, jnp.float32), pltpu.SemaphoreType.DMA(())]
    cuts = call(
        functools.partial(cut_windows, geo),
        (cut,) * (outer - 1),
        [IN_HBM],
        m_local * band_rows * geo.window,
        8 * outer * m_local * band_rows * geo.window,
        leg_scratch,
    )(far(by_row))
    received = [rotate(cuts[s - 1], "outer", outer, s) for s in range(1, outer)]
    stride = longitudes // (2 * orders)
    period = longitudes // stride if longitudes % stride == 0 else longitudes
    small = orders <= 16 and LANES % period == 0 and line == LANES and longitudes % period == 0
    if small:
        count = 2 * orders
        n = np.arange(count)[None, :]
        p = np.arange(LANES)[:, None]
        angle = 2.0 * math.pi * ((n * p) % period) / period
        basis = np.zeros((LANES, -(-2 * count // LANES) * LANES), np.float32)
        basis[:, :count] = np.cos(angle) / longitudes
        basis[:, count : 2 * count] = np.sin(angle) / longitudes
        tables = call(
            functools.partial(weight_tables, longitudes, period),
            jax.ShapeDtypeStruct((4, count, rows_here, LANES), jnp.float32),
            [WHOLE, WHOLE, SCALARS, WHOLE],
            1,
            8 * rows_here * longitudes,
            cost=1,
        )(class_idx, land, class_weight, jnp.asarray(basis))

    siblings = [rotate(direction, "inner", inner, s) for s in range(1, inner)]
    own_flops = 8 * m_local * line * geo.window * band_rows
    dir_window, own_rows, valid, *own_blocks = call(
        functools.partial(prepare, geo),
        (
            jax.ShapeDtypeStruct((m_local, 2 * line, geo.window), jnp.bfloat16),
            jax.ShapeDtypeStruct((m_local, band_rows, line), jnp.float32),
            jax.ShapeDtypeStruct((m_local, 8, deg_local), jnp.float32),
        )
        + (jax.ShapeDtypeStruct((m_local, band_rows, geo.block_window), jnp.float32),) * inner,
        [SCALARS, IN_HBM] + [WHOLE] * inner,
        1,
        8 * m_local * line * geo.window + leg_moved,
        leg_scratch,
        cost=1,
    )(order_of, far(by_row), direction, *siblings)
    first_legs = [own_blocks[0]]
    first_legs += [rotate(own_blocks[s], "inner", inner, s) for s in range(1, inner)]

    if small:
        received, tables = lax.optimization_barrier((received, tables))
    block = jax.ShapeDtypeStruct((outer - 1, m_local, band_rows, geo.block_window), jnp.float32)
    to_rows, *blocks = call(
        functools.partial(synthesise_rest, geo),
        (jax.ShapeDtypeStruct((order_devices, outer, m_local, rows_here, line), jnp.float32),)
        + (block,) * inner,
        [WHOLE] * (outer + 1),
        own_flops * (outer - 1),
        4 * m_local * (line + band_rows) * geo.window,
    )(own_rows, *received, dir_window)
    rest_legs = [blocks[0]]
    rest_legs += [rotate(blocks[s], "inner", inner, s) for s in range(1, inner)]
    grid_in = lax.all_to_all(
        to_rows.reshape(order_devices * outer, m_local, rows_here, line),
        ("order", "outer"),
        split_axis=0,
        concat_axis=0,
        tiled=True,
    )

    grid_in, first_legs, rest_legs = lax.optimization_barrier((grid_in, first_legs, rest_legs))
    if small:
        to_orders = call(
            functools.partial(grid_rows, geo, stride),
            jax.ShapeDtypeStruct((devices, each, rows_here, line), jnp.float32),
            [WHOLE, WHOLE, WHOLE],
            6 * orders * orders * rows_here * line,
            8 * orders * rows_here * line,
            [pltpu.VMEM((orders, rows_here, line), jnp.float32)] * 3,
        )(order_of[None, :], grid_in, tables)
    else:
        to_orders = plain_grid(geo, grid_in, order_of, class_idx, land, class_weight, period)
    spectra = lax.all_to_all(
        to_orders, ("order", "outer", "inner"), split_axis=0, concat_axis=0, tiled=True
    )
    shares = [spectra] + [rotate(spectra, "inner", inner, s) for s in range(1, inner)]
    coefficients = jax.ShapeDtypeStruct(position.shape, jnp.float32)
    part = (each,) + position.shape[1:]
    sums = ()
    applied = []
    for shift, share in enumerate(shares):
        if shift < inner - 1:
            sums_out = jax.ShapeDtypeStruct((4 * samples, LANES), jnp.float32)
        else:
            sums_out = jax.ShapeDtypeStruct((devices, 1, 4 * samples), jnp.float32)
        result, sums = call(
            functools.partial(project, geo, shift),
            (jax.ShapeDtypeStruct(part, jnp.float32), sums_out),
            [WHOLE] * (5 + 2 * inner + (shift > 0)),
            6 * each * line * geo.block_window * band_rows * outer * inner,
            16 * each * line * deg_local,
        )(
            valid,
            share,
            *first_legs,
            *rest_legs,
            direction,
            residual,
            damping[None, :],
            *((sums,) if shift else ()),
        )
        applied.append(result)
    sums = lax.all_to_all(
        sums, ("order", "outer", "inner"), split_axis=0, concat_axis=0, tiled=True
    )
    return call(
        functools.partial(update, geo),
        (coefficients,) * 3,
        [WHOLE] * (5 + inner),
        10 * m_local * line * deg_local,
        28 * m_local * line * deg_local,
        [pltpu.VMEM(position.shape, jnp.float32)] * 3
        + [pltpu.SemaphoreType.DMA((3, m_local, sin_cos))],
        IN_HBM,
    )(valid, sums, *applied, position, direction, residual)


def solution(mesh):
    order_devices, bands = mesh.shape["order"], mesh.shape["lat"]
    outer = 2 if bands % 2 == 0 else 1
    inner = bands // outer
    split = Mesh(mesh.devices.reshape(order_devices, outer, inner), ("order", "outer", "inner"))
    lat = ("outer", "inner")
    coefficients = P("order", None, None, lat)
    grid = P(("outer", "inner", "order"), None)
    return jax.shard_map(
        functools.partial(shards, outer, inner),
        mesh=split,
        in_specs=(
            coefficients,
            coefficients,
            coefficients,
            P("order", None, lat),
            P(),
            grid,
            grid,
            P(),
            P(lat),
        ),
        out_specs=(coefficients,) * 3,
        check_vma=False,
    )
```

```python
import functools
import math

import jax
import jax.numpy as jnp
import numpy as np
from jax import lax
from jax.experimental import pallas as pl
from jax.experimental.pallas import tpu as pltpu
from jax.sharding import Mesh
from jax.sharding import PartitionSpec as P

LANES = 128
HIGHEST = lax.Precision.HIGHEST
VMEM_LEAST = 16 * 1024 * 1024
VMEM_MOST = 48 * 1024 * 1024
WHOLE = pl.BlockSpec(memory_space=pltpu.VMEM)
SCALARS = pl.BlockSpec(memory_space=pltpu.SMEM)
IN_HBM = pl.BlockSpec(memory_space=pltpu.HBM)


def repeat(count, body):
    lax.fori_loop(0, count, lambda i, carry: (body(i), carry)[1], 0)


def split_bf16(x):
    hi = x.astype(jnp.bfloat16)
    lo = (x - hi.astype(jnp.float32)).astype(jnp.bfloat16)
    return hi, lo


def dot_pairs(a, b, dims, rows, columns):
    product = lax.dot_general(a, b, (dims, ((), ())), preferred_element_type=jnp.float32)
    low = product[:rows, columns:] + product[rows:, :columns]
    return product[:rows, :columns] + (low + product[rows:, columns:])


def params(moved):
    grant = min(VMEM_MOST, max(VMEM_LEAST, 3 * moved))
    return pltpu.CompilerParams(vmem_limit_bytes=grant)


def call(kernel, out_shape, in_specs, flops, moved, scratch=(), out_spec=WHOLE, cost=0):
    return pl.pallas_call(
        kernel,
        out_shape=out_shape,
        in_specs=in_specs,
        out_specs=jax.tree.map(lambda _: out_spec, out_shape),
        scratch_shapes=scratch,
        compiler_params=params(moved),
        cost_estimate=pl.CostEstimate(flops=flops, bytes_accessed=cost or moved, transcendentals=0),
    )


class Place:
    def __init__(self, geo, order_ref):
        self.geo = geo
        self.a, self.b = lax.axis_index("outer"), lax.axis_index("inner")
        self.first = lax.axis_index("order") * geo.m_local
        self.order_ref = order_ref

    def order(self, m):
        return self.order_ref[self.first + m]

    def outer(self, shift):
        return lax.rem(self.a + (self.geo.outer - shift), self.geo.outer)

    def inner(self, shift):
        return lax.rem(self.b + (self.geo.inner - shift), self.geo.inner)

    def among(self, table, b=None):
        index = self.a * self.geo.inner + (self.b if b is None else b)
        return choose(index, [value for row in table for value in row])


def choose(index, values):
    result = jnp.int32(values[0])
    for i, value in enumerate(values[1:], 1):
        result = jnp.where(index == i, jnp.int32(value), result)
    return result


def take(leg_ref, m, index, starts, width):
    degrees = leg_ref.shape[2]
    start = pl.multiple_of(choose(index, starts), LANES)
    last = None
    for i, first in enumerate(starts):
        first = first + width - LANES
        tile = leg_ref[m, :, first : min(first + LANES, degrees)]
        if tile.shape[1] < LANES:
            fill = jnp.zeros((tile.shape[0], LANES - tile.shape[1]), jnp.float32)
            tile = jnp.concatenate([tile, fill], axis=1)
        last = tile if last is None else jnp.where(index == i, tile, last)
    return jnp.concatenate([leg_ref[m, :, pl.ds(start, width - LANES)], last], axis=1)


def exact_window(geo, leg_ref, m, block):
    wide = take(leg_ref, m, block, geo.window_starts, geo.take_width)
    back = lax.rem(geo.take_width - choose(block, geo.window_shifts), geo.take_width)
    return pltpu.roll(wide, back, 1)[:, : geo.window]


def inner_block(geo, window, target):
    result = None
    for b, start in enumerate(geo.block_starts):
        piece = window[:, start : start + geo.block_window]
        result = piece if result is None else jnp.where(target == b, piece, result)
    return result


def cut_windows(geo, leg_hbm, *refs):
    send_refs, (leg_ref, sem) = refs[:-2], refs[-2:]
    fetch = pltpu.make_async_copy(leg_hbm, leg_ref, sem)
    fetch.start()
    a = lax.axis_index("outer")
    fetch.wait()
    m_local, rows = leg_ref.shape[:2]
    lane = lax.broadcasted_iota(jnp.int32, (rows, LANES), 1)
    for shift, ref in enumerate(send_refs, 1):
        block = lax.rem(a + shift, geo.outer)
        tiles = [None] * geo.rest_tiles
        for m in range(m_local):
            window = exact_window(geo, leg_ref, m, block)
            ref[:, m * geo.main : (m + 1) * geo.main] = window[:, : geo.main]
            if geo.rest:
                at, place = divmod(m, geo.rest_each)
                tile = jnp.where(lane < geo.rest, window[:, geo.main :], 0.0)
                if place:
                    tile = pltpu.roll(tile, place * geo.rest, 1)
                tiles[at] = tile if tiles[at] is None else tiles[at] + tile
        for i, tile in enumerate(tiles):
            start = m_local * geo.main + i * LANES
            ref[:, start : start + LANES] = tile


def unpack_window(geo, ref, m):
    window = ref[:, m * geo.main : (m + 1) * geo.main]
    if geo.rest:
        at, place = divmod(m, geo.rest_each)
        start = geo.m_local * geo.main + at * LANES
        tile = ref[:, start : start + LANES]
        if place:
            tile = pltpu.roll(tile, LANES - place * geo.rest, 1)
        window = jnp.concatenate([window, tile], axis=1)
    return window


def fold(x):
    rows, width = x.shape
    folded = None
    for start in range(0, width, LANES):
        piece = x[:, start : min(start + LANES, width)]
        if piece.shape[1] < LANES:
            fill = jnp.zeros((rows, LANES - piece.shape[1]), jnp.float32)
            piece = jnp.concatenate([piece, fill], axis=1)
        folded = piece if folded is None else folded + piece
    return folded


def to_line(folded):
    return jnp.sum(jnp.transpose(folded), axis=0, keepdims=True)


def prepare(geo, order_ref, leg_hbm, *refs):
    parts = refs[: geo.inner]
    out_ref, rows_ref, valid_ref, *cuts, leg_ref, sem = refs[geo.inner :]
    fetch = pltpu.make_async_copy(leg_hbm, leg_ref, sem)
    fetch.start()
    place = Place(geo, order_ref)
    m_local, sin_cos, samples, width = parts[0].shape
    window = out_ref.shape[2]
    line = sin_cos * samples
    start = place.a * geo.pair
    piece = 16
    steps = samples // piece
    shifts = [choose(place.inner(shift), geo.places) for shift in range(geo.inner)]
    degree = start + lax.broadcasted_iota(jnp.int32, (piece, window), 1)

    def one(i):
        m, rest = lax.div(i, sin_cos * steps), lax.rem(i, sin_cos * steps)
        s, k = lax.div(rest, steps), lax.rem(rest, steps) * piece
        total = None
        for shift, part in zip(shifts, parts):
            block = part[m, s, pl.ds(pl.multiple_of(k, piece), piece), :]
            fill = jnp.zeros((piece, window - width), jnp.float32)
            block = pltpu.roll(jnp.concatenate([block, fill], axis=1), shift, 1)
            total = block if total is None else total + block
        total = jnp.where(degree >= place.order(m), total, 0.0)
        hi, lo = split_bf16(total)
        at = rest * piece
        out_ref[m, pl.ds(pl.multiple_of(at, piece), piece)] = hi
        out_ref[m, pl.ds(pl.multiple_of(line + at, piece), piece)] = lo

    repeat(m_local * sin_cos * steps, one)
    own = place.among(geo.own_starts) + lax.broadcasted_iota(jnp.int32, valid_ref.shape[1:], 1)
    for m in range(m_local):
        valid_ref[m] = (own >= place.order(m)).astype(jnp.float32)
    fetch.wait()

    def rows(m):
        leg = exact_window(geo, leg_ref, m, place.a)
        rows_ref[m] = synthesis(leg, out_ref, m)
        for shift, ref in enumerate(cuts):
            ref[m] = inner_block(geo, leg, lax.rem(place.b + shift, geo.inner))

    repeat(m_local, rows)


def synthesis(leg, dir_ref, m):
    rows, line = leg.shape[0], dir_ref.shape[1] // 2
    halves = jnp.concatenate(split_bf16(leg), axis=0)
    return dot_pairs(halves, dir_ref[m], ((1,), (1,)), rows, line)


def synthesise_rest(geo, own_ref, *refs):
    others = geo.outer - 1
    legs, (dir_ref, out_ref, *cuts) = refs[:others], refs[others:]
    place = Place(geo, None)
    rows = out_ref.shape[3]

    def put(m, shift, part):
        a = place.outer(shift)
        for o in range(out_ref.shape[1]):
            out_ref[a, o, m] = part[o * rows : (o + 1) * rows]

    for m in range(own_ref.shape[0]):
        put(m, 0, own_ref[m])
        for shift in range(1, geo.outer):
            leg = unpack_window(geo, legs[shift - 1], m)
            put(m, shift, synthesis(leg, dir_ref, m))
            for ahead, ref in enumerate(cuts):
                ref[shift - 1, m] = inner_block(geo, leg, lax.rem(place.b + ahead, geo.inner))


def weight_tables(longitudes, period, class_ref, land_ref, value_ref, basis_ref, out_ref):
    classes = class_ref[...]
    on_land = land_ref[...] == 1
    weight = jnp.zeros(classes.shape, jnp.float32)
    for c in range(value_ref.shape[0]):
        value = jnp.where(on_land, value_ref[c, 1], value_ref[c, 0])
        weight = jnp.where(classes == c, value, weight)
    rows = classes.shape[0]
    folded = jnp.zeros((rows, LANES), jnp.float32)
    for start in range(0, longitudes, LANES):
        piece = weight[:, start : min(start + LANES, longitudes)]
        if piece.shape[1] < LANES:
            piece = jnp.concatenate(
                [piece, jnp.zeros((rows, LANES - piece.shape[1]), jnp.float32)], axis=1
            )
        folded = folded + piece
    moments = lax.dot_general(
        folded,
        basis_ref[...],
        (((1,), (0,)), ((), ())),
        precision=HIGHEST,
        preferred_element_type=jnp.float32,
    )
    lane = lax.broadcasted_iota(jnp.int32, (rows, LANES), 1)
    sign = jnp.where(lane < LANES // 2, 1.0, -1.0)
    count = out_ref.shape[1]
    for n in range(count):
        even = jnp.broadcast_to(moments[:, n : n + 1], (rows, LANES))
        odd = jnp.broadcast_to(moments[:, count + n : count + n + 1], (rows, LANES))
        out_ref[0, n] = even
        out_ref[1, n] = sign * even
        out_ref[2, n] = odd
        out_ref[3, n] = sign * odd


def grid_rows(geo, stride, order_ref, recv_ref, table_ref, out_ref, plain, swapped, done):
    orders = plain.shape[0]
    m_local, each = recv_ref.shape[1], out_ref.shape[1]
    order_devices = orders // m_local
    at = order_ref[...]
    slot = [lax.div(at[0, m], jnp.int32(stride)) for m in range(orders)]
    for m in range(orders):
        o, i = divmod(m, m_local)
        total = recv_ref[o, i]
        for a in range(1, geo.outer):
            total = total + recv_ref[a * order_devices + o, i]
        at = slot[m]
        plain[at] = total
        swapped[at] = pltpu.roll(total, LANES // 2, 1)
    for i in range(orders):
        total = None
        for j in range(orders):
            cos_part = table_ref[0, abs(i - j)] + table_ref[1, i + j]
            if i >= j:
                sin_part = table_ref[2, i + j] - table_ref[3, i - j]
            else:
                sin_part = table_ref[2, i + j] + table_ref[3, j - i]
            term = cos_part * plain[j] + sin_part * swapped[j]
            total = term if total is None else total + term
        done[i] = total
    for m in range(orders):
        o, i = divmod(m, m_local)
        b, i = divmod(i, each)
        value = done[slot[m]]
        for a in range(geo.outer):
            out_ref[(b * geo.outer + a) * order_devices + o, i] = value


def project(geo, shift, valid_ref, recv_ref, *refs):
    legs, refs = refs[: 2 * geo.inner], refs[2 * geo.inner :]
    dir_ref, res_ref, damp_ref = refs[:3]
    before_ref = refs[3] if shift else None
    app_ref, sums_ref = refs[-2:]
    place = Place(geo, None)
    each, sin_cos, samples, width = app_ref.shape
    first = place.inner(shift) * each
    window = geo.block_window
    copies = geo.outer * geo.inner
    order_devices = recv_ref.shape[0] // copies
    damping = damp_ref[...]
    rows = sin_cos * samples
    offsets = [p - s for p, s in zip(geo.places, geo.block_starts)]
    back = window - choose(place.b, offsets)

    def products(i):
        tiles, blocks = [], []
        for b in range(geo.inner):
            for a in range(geo.outer):
                band = place.inner(b) * geo.outer + place.outer(a)
                tile = recv_ref[pl.ds(band * order_devices, order_devices), i]
                tiles.append(tile.reshape(-1, tile.shape[2]))
                if a == 0:
                    blocks.append(legs[b][first + i])
                else:
                    blocks.append(legs[geo.inner + b][a - 1, first + i])
        hi, lo = split_bf16(jnp.concatenate(tiles, axis=0))
        high, low = split_bf16(jnp.concatenate(blocks, axis=0))
        dims = (((0,), (0,)), ((), ()))
        both = jnp.concatenate([hi, lo], axis=1)
        main = lax.dot_general(both, high, dims, preferred_element_type=jnp.float32)
        rest = lax.dot_general(hi, low, dims, preferred_element_type=jnp.float32)
        summed = main[:rows] + (main[rows:] + rest)
        summed = pltpu.roll(summed, back, 1)[:, :width]
        for s in range(sin_cos):
            app_ref[i, s] = summed[s * samples : (s + 1) * samples]

    repeat(each, products)

    def apply(at, sums):
        i, s = lax.div(at, sin_cos), lax.rem(at, sin_cos)
        valid = valid_ref[first + i, 0:1]
        direction = dir_ref[first + i, s] * valid
        residual = res_ref[first + i, s] * valid
        applied = app_ref[i, s] * valid + damping * direction
        app_ref[i, s] = applied
        terms = (
            residual * residual,
            direction * applied,
            residual * applied,
            applied * applied,
        )
        return tuple(old + fold(t) for old, t in zip(sums, terms))

    if shift:
        start = tuple(before_ref[i * samples : (i + 1) * samples] for i in range(4))
    else:
        start = (jnp.zeros((samples, LANES), jnp.float32),) * 4
    sums = lax.fori_loop(0, each * sin_cos, apply, start)
    stacked = jnp.concatenate(sums, axis=0)
    if shift < geo.inner - 1:
        sums_ref[...] = stacked
    else:
        line = to_line(stacked)

        def give(device):
            sums_ref[device] = line

        repeat(sums_ref.shape[0], give)


def update(geo, valid_ref, sums_ref, *refs):
    apps, refs = refs[: geo.inner], refs[geo.inner :]
    pos_ref, dir_ref, res_ref, *refs = refs
    outs, bufs, sems = refs[:3], refs[3:6], refs[6]
    place = Place(geo, None)
    m_local, sin_cos, samples, width = dir_ref.shape
    totals = jnp.sum(sums_ref[...], axis=0)
    before, curvature, cross, square = [
        totals[:, i * samples : (i + 1) * samples] for i in range(4)
    ]
    step_row = before / curvature
    after = before - 2.0 * step_row * cross + step_row * step_row * square
    ratio_row = after / before
    row = lax.broadcasted_iota(jnp.int32, (samples, samples), 0)
    column = lax.broadcasted_iota(jnp.int32, (samples, samples), 1)
    diagonal = row == column
    step = jnp.sum(jnp.where(diagonal, step_row, 0.0), axis=1, keepdims=True)
    ratio = jnp.sum(jnp.where(diagonal, ratio_row, 0.0), axis=1, keepdims=True)

    def copy(i, m, s):
        return pltpu.make_async_copy(bufs[i].at[m, s], outs[i].at[m, s], sems.at[i, m, s])

    each = m_local // geo.inner
    for shift, app_ref in enumerate(apps):

        def one(at, shift=shift, app_ref=app_ref):
            i, s = lax.div(at, sin_cos), lax.rem(at, sin_cos)
            m = place.inner(shift) * each + i
            valid = valid_ref[m, 0:1]
            direction = dir_ref[m, s] * valid
            residual = res_ref[m, s] * valid
            position = pos_ref[m, s] * valid
            new_residual = residual - step * app_ref[i, s]
            values = (
                position + step * direction,
                new_residual,
                new_residual + ratio * direction,
            )
            for i in range(3):
                bufs[i][m, s] = values[i]
                copy(i, m, s).start()

        repeat(each * sin_cos, one)

    def end(at):
        for i in range(3):
            copy(i, lax.div(at, sin_cos), lax.rem(at, sin_cos)).wait()

    repeat(m_local * sin_cos, end)


class Geometry:
    def __init__(self, outer, inner, degrees, m_local):
        self.outer, self.inner, self.m_local = outer, inner, m_local
        block = degrees // (outer * inner)

        def down(x):
            return x // LANES * LANES

        def up(x):
            return -(-x // LANES) * LANES

        pair = degrees // outer
        self.pair = pair
        self.own_starts = [[(a * inner + b) * block for b in range(inner)] for a in range(outer)]
        self.window_starts = [down(a * pair) for a in range(outer)]
        self.window_shifts = [a * pair - s for a, s in enumerate(self.window_starts)]
        self.take_width = max(up(s + pair) for s in self.window_shifts)
        self.window = up(pair)
        self.places = [b * block for b in range(inner)]
        self.block_window = max(up(p + block) - down(p) for p in self.places)
        self.block_starts = [min(down(p), self.window - self.block_window) for p in self.places]
        self.main = down(pair)
        self.rest = pair - self.main
        self.rest_each = LANES // self.rest if self.rest else 1
        self.rest_tiles = -(-m_local // self.rest_each) if self.rest else 0
        self.packed = m_local * self.main + self.rest_tiles * LANES


def far(x):
    return pltpu.with_memory_space_constraint(x, pltpu.HBM)


def rotate(x, axis, size, shift):
    return lax.ppermute(x, axis, [(i, (i + shift) % size) for i in range(size)])


def plain_grid(geo, grid_in, order_of, class_idx, land, class_weight, period):
    order_devices = grid_in.shape[0] // geo.outer
    m_local, rows, width = grid_in.shape[1:]
    orders = order_devices * m_local
    longitudes = class_idx.shape[1]
    stacked = grid_in.reshape(geo.outer, order_devices, m_local, rows, 2, width // 2)
    stacked = jnp.sum(stacked, axis=0).reshape(orders, rows, 2, width // 2)
    phases = order_of[:, None] * jnp.arange(period, dtype=jnp.int32)[None, :] % longitudes
    angles = phases.astype(jnp.float32) * (2.0 * math.pi / longitudes)
    harmonic = jnp.stack([jnp.cos(angles), jnp.sin(angles)])
    surface = jnp.einsum("mrsk,smp->rkp", stacked, harmonic, precision=HIGHEST)
    onehot = class_idx[:, :, None] == jnp.arange(class_weight.shape[0], dtype=jnp.int32)
    by_class = jnp.dot(onehot.astype(jnp.float32), class_weight, precision=HIGHEST)
    weight = jnp.where(land == 1, by_class[:, :, 1], by_class[:, :, 0])
    folded = jnp.sum(weight.reshape(rows, longitudes // period, period), axis=1)
    weighted = surface * folded[:, None, :]
    spectra = jnp.einsum("rkp,smp->mrsk", weighted, harmonic, precision=HIGHEST)
    each = m_local // geo.inner
    spectra = spectra * (2.0 / longitudes)
    spectra = spectra.reshape(order_devices, geo.inner, 1, each, rows, width)
    spectra = jnp.transpose(spectra, (1, 2, 0, 3, 4, 5))
    spectra = jnp.broadcast_to(
        spectra, (geo.inner, geo.outer, order_devices, each, rows, width)
    )
    return spectra.reshape(order_devices * geo.outer * geo.inner, each, rows, width)


def shards(
    outer,
    inner,
    position,
    residual,
    direction,
    legendre,
    order_of,
    class_idx,
    land,
    class_weight,
    damping,
):
    m_local, sin_cos, samples, deg_local = position.shape
    degrees, band_rows = legendre.shape[1:]
    rows_here, longitudes = class_idx.shape
    orders = order_of.shape[0]
    order_devices = orders // m_local
    devices = order_devices * outer * inner
    each = m_local // inner
    line = sin_cos * samples
    geo = Geometry(outer, inner, degrees, m_local)
    by_row = jnp.transpose(legendre, (0, 2, 1))
    cut = pltpu.VMEM((band_rows, geo.packed), jnp.float32)
    leg_moved = 4 * m_local * band_rows * degrees
    leg_scratch = [pltpu.VMEM(by_row.shape, jnp.float32), pltpu.SemaphoreType.DMA(())]
    cuts = call(
        functools.partial(cut_windows, geo),
        (cut,) * (outer - 1),
        [IN_HBM],
        m_local * band_rows * geo.window,
        8 * outer * m_local * band_rows * geo.window,
        leg_scratch,
    )(far(by_row))
    received = [rotate(cuts[s - 1], "outer", outer, s) for s in range(1, outer)]
    stride = longitudes // (2 * orders)
    period = longitudes // stride if longitudes % stride == 0 else longitudes
    small = orders <= 16 and LANES % period == 0 and line == LANES and longitudes % period == 0
    if small:
        count = 2 * orders
        n = np.arange(count)[None, :]
        p = np.arange(LANES)[:, None]
        angle = 2.0 * math.pi * ((n * p) % period) / period
        basis = np.zeros((LANES, -(-2 * count // LANES) * LANES), np.float32)
        basis[:, :count] = np.cos(angle) / longitudes
        basis[:, count : 2 * count] = np.sin(angle) / longitudes
        tables = call(
            functools.partial(weight_tables, longitudes, period),
            jax.ShapeDtypeStruct((4, count, rows_here, LANES), jnp.float32),
            [WHOLE, WHOLE, SCALARS, WHOLE],
            1,
            8 * rows_here * longitudes,
            cost=1,
        )(class_idx, land, class_weight, jnp.asarray(basis))

    siblings = [rotate(direction, "inner", inner, s) for s in range(1, inner)]
    own_flops = 8 * m_local * line * geo.window * band_rows
    dir_window, own_rows, valid, *own_blocks = call(
        functools.partial(prepare, geo),
        (
            jax.ShapeDtypeStruct((m_local, 2 * line, geo.window), jnp.bfloat16),
            jax.ShapeDtypeStruct((m_local, band_rows, line), jnp.float32),
            jax.ShapeDtypeStruct((m_local, 8, deg_local), jnp.float32),
        )
        + (jax.ShapeDtypeStruct((m_local, band_rows, geo.block_window), jnp.float32),) * inner,
        [SCALARS, IN_HBM] + [WHOLE] * inner,
        1,
        8 * m_local * line * geo.window + leg_moved,
        leg_scratch,
        cost=1,
    )(order_of, far(by_row), direction, *siblings)
    first_legs = [own_blocks[0]]
    first_legs += [rotate(own_blocks[s], "inner", inner, s) for s in range(1, inner)]

    if small:
        received, tables = lax.optimization_barrier((received, tables))
    block = jax.ShapeDtypeStruct((outer - 1, m_local, band_rows, geo.block_window), jnp.float32)
    to_rows, *blocks = call(
        functools.partial(synthesise_rest, geo),
        (jax.ShapeDtypeStruct((outer, order_devices, m_local, rows_here, line), jnp.float32),)
        + (block,) * inner,
        [WHOLE] * (outer + 1),
        own_flops * (outer - 1),
        4 * m_local * (line + band_rows) * geo.window,
    )(own_rows, *received, dir_window)
    rest_legs = [blocks[0]]
    rest_legs += [rotate(blocks[s], "inner", inner, s) for s in range(1, inner)]
    grid_in = lax.all_to_all(
        to_rows.reshape(order_devices * outer, m_local, rows_here, line),
        ("outer", "order"),
        split_axis=0,
        concat_axis=0,
        tiled=True,
    )

    grid_in, first_legs, rest_legs = lax.optimization_barrier((grid_in, first_legs, rest_legs))
    if small:
        to_orders = call(
            functools.partial(grid_rows, geo, stride),
            jax.ShapeDtypeStruct((devices, each, rows_here, line), jnp.float32),
            [WHOLE, WHOLE, WHOLE],
            6 * orders * orders * rows_here * line,
            8 * orders * rows_here * line,
            [pltpu.VMEM((orders, rows_here, line), jnp.float32)] * 3,
        )(order_of[None, :], grid_in, tables)
    else:
        to_orders = plain_grid(geo, grid_in, order_of, class_idx, land, class_weight, period)
    spectra = lax.all_to_all(
        to_orders, ("inner", "outer", "order"), split_axis=0, concat_axis=0, tiled=True
    )
    shares = [spectra] + [rotate(spectra, "inner", inner, s) for s in range(1, inner)]
    coefficients = jax.ShapeDtypeStruct(position.shape, jnp.float32)
    part = (each,) + position.shape[1:]
    sums = ()
    applied = []
    for shift, share in enumerate(shares):
        if shift < inner - 1:
            sums_out = jax.ShapeDtypeStruct((4 * samples, LANES), jnp.float32)
        else:
            sums_out = jax.ShapeDtypeStruct((devices, 1, 4 * samples), jnp.float32)
        result, sums = call(
            functools.partial(project, geo, shift),
            (jax.ShapeDtypeStruct(part, jnp.float32), sums_out),
            [WHOLE] * (5 + 2 * inner + (shift > 0)),
            6 * each * line * geo.block_window * band_rows * outer * inner,
            16 * each * line * deg_local,
        )(
            valid,
            share,
            *first_legs,
            *rest_legs,
            direction,
            residual,
            damping[None, :],
            *((sums,) if shift else ()),
        )
        applied.append(result)
    sums = lax.all_to_all(
        sums, ("inner", "outer", "order"), split_axis=0, concat_axis=0, tiled=True
    )
    return call(
        functools.partial(update, geo),
        (coefficients,) * 3,
        [WHOLE] * (5 + inner),
        10 * m_local * line * deg_local,
        28 * m_local * line * deg_local,
        [pltpu.VMEM(position.shape, jnp.float32)] * 3
        + [pltpu.SemaphoreType.DMA((3, m_local, sin_cos))],
        IN_HBM,
    )(valid, sums, *applied, position, direction, residual)


def solution(mesh):
    order_devices, bands = mesh.shape["order"], mesh.shape["lat"]
    outer = 2 if bands % 2 == 0 else 1
    inner = bands // outer
    split = Mesh(mesh.devices.reshape(order_devices, outer, inner), ("order", "outer", "inner"))
    lat = ("outer", "inner")
    coefficients = P("order", None, None, lat)
    grid = P(("outer", "inner", "order"), None)
    return jax.shard_map(
        functools.partial(shards, outer, inner),
        mesh=split,
        in_specs=(
            coefficients,
            coefficients,
            coefficients,
            P("order", None, lat),
            P(),
            grid,
            grid,
            P(),
            P(lat),
        ),
        out_specs=(coefficients,) * 3,
        check_vma=False,
    )
```

```python
import functools
import math

import jax
import jax.numpy as jnp
import numpy as np
from jax import lax
from jax.experimental import pallas as pl
from jax.experimental.pallas import tpu as pltpu
from jax.sharding import Mesh
from jax.sharding import PartitionSpec as P

LANES = 128
HIGHEST = lax.Precision.HIGHEST
VMEM_LEAST = 16 * 1024 * 1024
VMEM_MOST = 48 * 1024 * 1024
WHOLE = pl.BlockSpec(memory_space=pltpu.VMEM)
SCALARS = pl.BlockSpec(memory_space=pltpu.SMEM)
IN_HBM = pl.BlockSpec(memory_space=pltpu.HBM)


def repeat(count, body):
    lax.fori_loop(0, count, lambda i, carry: (body(i), carry)[1], 0)


def split_bf16(x):
    hi = x.astype(jnp.bfloat16)
    lo = (x - hi.astype(jnp.float32)).astype(jnp.bfloat16)
    return hi, lo


def dot_pairs(a, b, dims, rows, columns):
    product = lax.dot_general(a, b, (dims, ((), ())), preferred_element_type=jnp.float32)
    low = product[:rows, columns:] + product[rows:, :columns]
    return product[:rows, :columns] + (low + product[rows:, columns:])


def params(moved):
    grant = min(VMEM_MOST, max(VMEM_LEAST, 3 * moved))
    return pltpu.CompilerParams(vmem_limit_bytes=grant)


def call(kernel, out_shape, in_specs, flops, moved, scratch=(), out_spec=WHOLE, cost=0):
    return pl.pallas_call(
        kernel,
        out_shape=out_shape,
        in_specs=in_specs,
        out_specs=jax.tree.map(lambda _: out_spec, out_shape),
        scratch_shapes=scratch,
        compiler_params=params(moved),
        cost_estimate=pl.CostEstimate(flops=flops, bytes_accessed=cost or moved, transcendentals=0),
    )


class Place:
    def __init__(self, geo, order_ref):
        self.geo = geo
        self.a, self.b = lax.axis_index("outer"), lax.axis_index("inner")
        self.first = lax.axis_index("order") * geo.m_local
        self.order_ref = order_ref

    def order(self, m):
        return self.order_ref[self.first + m]

    def outer(self, shift):
        return lax.rem(self.a + (self.geo.outer - shift), self.geo.outer)

    def inner(self, shift):
        return lax.rem(self.b + (self.geo.inner - shift), self.geo.inner)

    def among(self, table, b=None):
        index = self.a * self.geo.inner + (self.b if b is None else b)
        return choose(index, [value for row in table for value in row])


def choose(index, values):
    result = jnp.int32(values[0])
    for i, value in enumerate(values[1:], 1):
        result = jnp.where(index == i, jnp.int32(value), result)
    return result


def take(leg_ref, m, index, starts, width):
    degrees = leg_ref.shape[2]
    start = pl.multiple_of(choose(index, starts), LANES)
    last = None
    for i, first in enumerate(starts):
        first = first + width - LANES
        tile = leg_ref[m, :, first : min(first + LANES, degrees)]
        if tile.shape[1] < LANES:
            fill = jnp.zeros((tile.shape[0], LANES - tile.shape[1]), jnp.float32)
            tile = jnp.concatenate([tile, fill], axis=1)
        last = tile if last is None else jnp.where(index == i, tile, last)
    return jnp.concatenate([leg_ref[m, :, pl.ds(start, width - LANES)], last], axis=1)


def exact_window(geo, leg_ref, m, block):
    wide = take(leg_ref, m, block, geo.window_starts, geo.take_width)
    back = lax.rem(geo.take_width - choose(block, geo.window_shifts), geo.take_width)
    return pltpu.roll(wide, back, 1)[:, : geo.window]


def inner_block(geo, window, target):
    result = None
    for b, start in enumerate(geo.block_starts):
        piece = window[:, start : start + geo.block_window]
        result = piece if result is None else jnp.where(target == b, piece, result)
    return result


def cut_windows(geo, leg_hbm, *refs):
    send_refs, (leg_ref, sems) = refs[:-2], refs[-2:]
    m_local, rows = leg_ref.shape[:2]
    fetches = [
        pltpu.make_async_copy(leg_hbm.at[m], leg_ref.at[m], sems.at[m]) for m in range(m_local)
    ]
    for fetch in fetches:
        fetch.start()
    a = lax.axis_index("outer")
    lane = lax.broadcasted_iota(jnp.int32, (rows, LANES), 1)
    for shift, ref in enumerate(send_refs, 1):
        block = lax.rem(a + shift, geo.outer)
        tiles = [None] * geo.rest_tiles
        for m in range(m_local):
            if shift == 1:
                fetches[m].wait()
            window = exact_window(geo, leg_ref, m, block)
            ref[:, m * geo.main : (m + 1) * geo.main] = window[:, : geo.main]
            if geo.rest:
                at, place = divmod(m, geo.rest_each)
                tile = jnp.where(lane < geo.rest, window[:, geo.main :], 0.0)
                if place:
                    tile = pltpu.roll(tile, place * geo.rest, 1)
                tiles[at] = tile if tiles[at] is None else tiles[at] + tile
        for i, tile in enumerate(tiles):
            start = m_local * geo.main + i * LANES
            ref[:, start : start + LANES] = tile


def unpack_window(geo, ref, m):
    window = ref[:, m * geo.main : (m + 1) * geo.main]
    if geo.rest:
        at, place = divmod(m, geo.rest_each)
        start = geo.m_local * geo.main + at * LANES
        tile = ref[:, start : start + LANES]
        if place:
            tile = pltpu.roll(tile, LANES - place * geo.rest, 1)
        window = jnp.concatenate([window, tile], axis=1)
    return window


def fold(x):
    rows, width = x.shape
    folded = None
    for start in range(0, width, LANES):
        piece = x[:, start : min(start + LANES, width)]
        if piece.shape[1] < LANES:
            fill = jnp.zeros((rows, LANES - piece.shape[1]), jnp.float32)
            piece = jnp.concatenate([piece, fill], axis=1)
        folded = piece if folded is None else folded + piece
    return folded


def to_line(folded):
    return jnp.sum(jnp.transpose(folded), axis=0, keepdims=True)


def prepare(geo, order_ref, leg_hbm, *refs):
    parts = refs[: geo.inner]
    out_ref, rows_ref, valid_ref, *cuts, leg_ref, sem = refs[geo.inner :]
    fetch = pltpu.make_async_copy(leg_hbm, leg_ref, sem)
    fetch.start()
    place = Place(geo, order_ref)
    m_local, sin_cos, samples, width = parts[0].shape
    window = out_ref.shape[2]
    line = sin_cos * samples
    start = place.a * geo.pair
    piece = 16
    steps = samples // piece
    shifts = [choose(place.inner(shift), geo.places) for shift in range(geo.inner)]
    degree = start + lax.broadcasted_iota(jnp.int32, (piece, window), 1)

    def one(i):
        m, rest = lax.div(i, sin_cos * steps), lax.rem(i, sin_cos * steps)
        s, k = lax.div(rest, steps), lax.rem(rest, steps) * piece
        total = None
        for shift, part in zip(shifts, parts):
            block = part[m, s, pl.ds(pl.multiple_of(k, piece), piece), :]
            fill = jnp.zeros((piece, window - width), jnp.float32)
            block = pltpu.roll(jnp.concatenate([block, fill], axis=1), shift, 1)
            total = block if total is None else total + block
        total = jnp.where(degree >= place.order(m), total, 0.0)
        hi, lo = split_bf16(total)
        at = rest * piece
        out_ref[m, pl.ds(pl.multiple_of(at, piece), piece)] = hi
        out_ref[m, pl.ds(pl.multiple_of(line + at, piece), piece)] = lo

    repeat(m_local * sin_cos * steps, one)
    own = place.among(geo.own_starts) + lax.broadcasted_iota(jnp.int32, valid_ref.shape[1:], 1)
    for m in range(m_local):
        valid_ref[m] = (own >= place.order(m)).astype(jnp.float32)
    fetch.wait()

    def rows(m):
        leg = exact_window(geo, leg_ref, m, place.a)
        rows_ref[m] = synthesis(leg, out_ref, m)
        for shift, ref in enumerate(cuts):
            ref[m] = inner_block(geo, leg, lax.rem(place.b + shift, geo.inner))

    repeat(m_local, rows)


def synthesis(leg, dir_ref, m):
    rows, line = leg.shape[0], dir_ref.shape[1] // 2
    halves = jnp.concatenate(split_bf16(leg), axis=0)
    return dot_pairs(halves, dir_ref[m], ((1,), (1,)), rows, line)


def synthesise_rest(geo, own_ref, *refs):
    others = geo.outer - 1
    legs, (dir_ref, out_ref, *cuts) = refs[:others], refs[others:]
    place = Place(geo, None)
    rows = out_ref.shape[3]

    def put(m, shift, part):
        a = place.outer(shift)
        for o in range(out_ref.shape[1]):
            out_ref[a, o, m] = part[o * rows : (o + 1) * rows]

    for m in range(own_ref.shape[0]):
        put(m, 0, own_ref[m])
        for shift in range(1, geo.outer):
            leg = unpack_window(geo, legs[shift - 1], m)
            put(m, shift, synthesis(leg, dir_ref, m))
            for ahead, ref in enumerate(cuts):
                ref[shift - 1, m] = inner_block(geo, leg, lax.rem(place.b + ahead, geo.inner))


def weight_tables(longitudes, period, class_ref, land_ref, value_ref, basis_ref, out_ref):
    classes = class_ref[...]
    on_land = land_ref[...] == 1
    weight = jnp.zeros(classes.shape, jnp.float32)
    for c in range(value_ref.shape[0]):
        value = jnp.where(on_land, value_ref[c, 1], value_ref[c, 0])
        weight = jnp.where(classes == c, value, weight)
    rows = classes.shape[0]
    folded = jnp.zeros((rows, LANES), jnp.float32)
    for start in range(0, longitudes, LANES):
        piece = weight[:, start : min(start + LANES, longitudes)]
        if piece.shape[1] < LANES:
            piece = jnp.concatenate(
                [piece, jnp.zeros((rows, LANES - piece.shape[1]), jnp.float32)], axis=1
            )
        folded = folded + piece
    moments = lax.dot_general(
        folded,
        basis_ref[...],
        (((1,), (0,)), ((), ())),
        precision=HIGHEST,
        preferred_element_type=jnp.float32,
    )
    lane = lax.broadcasted_iota(jnp.int32, (rows, LANES), 1)
    sign = jnp.where(lane < LANES // 2, 1.0, -1.0)
    count = out_ref.shape[1]
    for n in range(count):
        even = jnp.broadcast_to(moments[:, n : n + 1], (rows, LANES))
        odd = jnp.broadcast_to(moments[:, count + n : count + n + 1], (rows, LANES))
        out_ref[0, n] = even
        out_ref[1, n] = sign * even
        out_ref[2, n] = odd
        out_ref[3, n] = sign * odd


def grid_rows(geo, stride, order_ref, recv_ref, table_ref, out_ref, plain, swapped, done):
    orders = plain.shape[0]
    m_local, each = recv_ref.shape[1], out_ref.shape[1]
    order_devices = orders // m_local
    at = order_ref[...]
    slot = [lax.div(at[0, m], jnp.int32(stride)) for m in range(orders)]
    for m in range(orders):
        o, i = divmod(m, m_local)
        total = recv_ref[o, i]
        for a in range(1, geo.outer):
            total = total + recv_ref[a * order_devices + o, i]
        at = slot[m]
        plain[at] = total
        swapped[at] = pltpu.roll(total, LANES // 2, 1)
    for i in range(orders):
        total = None
        for j in range(orders):
            cos_part = table_ref[0, abs(i - j)] + table_ref[1, i + j]
            if i >= j:
                sin_part = table_ref[2, i + j] - table_ref[3, i - j]
            else:
                sin_part = table_ref[2, i + j] + table_ref[3, j - i]
            term = cos_part * plain[j] + sin_part * swapped[j]
            total = term if total is None else total + term
        done[i] = total
    for m in range(orders):
        o, i = divmod(m, m_local)
        b, i = divmod(i, each)
        value = done[slot[m]]
        for a in range(geo.outer):
            out_ref[(b * geo.outer + a) * order_devices + o, i] = value


def project(geo, shift, valid_ref, recv_ref, *refs):
    legs, refs = refs[: 2 * geo.inner], refs[2 * geo.inner :]
    dir_ref, res_ref, damp_ref = refs[:3]
    before_ref = refs[3] if shift else None
    app_ref, sums_ref = refs[-2:]
    place = Place(geo, None)
    each, sin_cos, samples, width = app_ref.shape
    first = place.inner(shift) * each
    window = geo.block_window
    copies = geo.outer * geo.inner
    order_devices = recv_ref.shape[0] // copies
    damping = damp_ref[...]
    rows = sin_cos * samples
    offsets = [p - s for p, s in zip(geo.places, geo.block_starts)]
    back = window - choose(place.b, offsets)

    def products(i):
        tiles, blocks = [], []
        for b in range(geo.inner):
            for a in range(geo.outer):
                band = place.inner(b) * geo.outer + place.outer(a)
                tile = recv_ref[pl.ds(band * order_devices, order_devices), i]
                tiles.append(tile.reshape(-1, tile.shape[2]))
                if a == 0:
                    blocks.append(legs[b][first + i])
                else:
                    blocks.append(legs[geo.inner + b][a - 1, first + i])
        hi, lo = split_bf16(jnp.concatenate(tiles, axis=0))
        high, low = split_bf16(jnp.concatenate(blocks, axis=0))
        dims = (((0,), (0,)), ((), ()))
        both = jnp.concatenate([hi, lo], axis=1)
        main = lax.dot_general(both, high, dims, preferred_element_type=jnp.float32)
        rest = lax.dot_general(hi, low, dims, preferred_element_type=jnp.float32)
        summed = main[:rows] + (main[rows:] + rest)
        summed = pltpu.roll(summed, back, 1)[:, :width]
        for s in range(sin_cos):
            app_ref[i, s] = summed[s * samples : (s + 1) * samples]

    repeat(each, products)

    def apply(at, sums):
        i, s = lax.div(at, sin_cos), lax.rem(at, sin_cos)
        valid = valid_ref[first + i, 0:1]
        direction = dir_ref[first + i, s] * valid
        residual = res_ref[first + i, s] * valid
        applied = app_ref[i, s] * valid + damping * direction
        app_ref[i, s] = applied
        terms = (direction * applied, residual * applied, applied * applied)
        return tuple(old + fold(t) for old, t in zip(sums, terms))

    def norm(at, old):
        m, s = lax.div(at, sin_cos), lax.rem(at, sin_cos)
        residual = res_ref[m, s] * valid_ref[m, 0:1]
        return old + fold(residual * residual)

    zero = jnp.zeros((samples, LANES), jnp.float32)
    if shift:
        before, *start = [before_ref[i * samples : (i + 1) * samples] for i in range(4)]
    else:
        before, start = lax.fori_loop(0, geo.m_local * sin_cos, norm, zero), [zero] * 3
    sums = lax.fori_loop(0, each * sin_cos, apply, tuple(start))
    stacked = jnp.concatenate((before,) + sums, axis=0)
    if shift < geo.inner - 1:
        sums_ref[...] = stacked
    else:
        line = to_line(stacked)

        def give(device):
            sums_ref[device] = line

        repeat(sums_ref.shape[0], give)


def update(geo, valid_ref, sums_ref, *refs):
    apps, refs = refs[: geo.inner], refs[geo.inner :]
    pos_ref, dir_ref, res_ref, *refs = refs
    outs, bufs, sems = refs[:3], refs[3:6], refs[6]
    place = Place(geo, None)
    m_local, sin_cos, samples, width = dir_ref.shape
    totals = jnp.sum(sums_ref[...], axis=0)
    before, curvature, cross, square = [
        totals[:, i * samples : (i + 1) * samples] for i in range(4)
    ]
    step_row = before / curvature
    after = before - 2.0 * step_row * cross + step_row * step_row * square
    ratio_row = after / before
    row = lax.broadcasted_iota(jnp.int32, (samples, samples), 0)
    column = lax.broadcasted_iota(jnp.int32, (samples, samples), 1)
    diagonal = row == column
    step = jnp.sum(jnp.where(diagonal, step_row, 0.0), axis=1, keepdims=True)
    ratio = jnp.sum(jnp.where(diagonal, ratio_row, 0.0), axis=1, keepdims=True)

    def copy(i, m, s):
        return pltpu.make_async_copy(bufs[i].at[m, s], outs[i].at[m, s], sems.at[i, m, s])

    each = m_local // geo.inner
    for shift, app_ref in enumerate(apps):

        def one(at, shift=shift, app_ref=app_ref):
            i, s = lax.div(at, sin_cos), lax.rem(at, sin_cos)
            m = place.inner(shift) * each + i
            valid = valid_ref[m, 0:1]
            direction = dir_ref[m, s] * valid
            residual = res_ref[m, s] * valid
            position = pos_ref[m, s] * valid
            new_residual = residual - step * app_ref[i, s]
            values = (
                position + step * direction,
                new_residual,
                new_residual + ratio * direction,
            )
            for i in range(3):
                bufs[i][m, s] = values[i]
                copy(i, m, s).start()

        repeat(each * sin_cos, one)

    def end(at):
        for i in range(3):
            copy(i, lax.div(at, sin_cos), lax.rem(at, sin_cos)).wait()

    repeat(m_local * sin_cos, end)


class Geometry:
    def __init__(self, outer, inner, degrees, m_local):
        self.outer, self.inner, self.m_local = outer, inner, m_local
        block = degrees // (outer * inner)

        def down(x):
            return x // LANES * LANES

        def up(x):
            return -(-x // LANES) * LANES

        pair = degrees // outer
        self.pair = pair
        self.own_starts = [[(a * inner + b) * block for b in range(inner)] for a in range(outer)]
        self.window_starts = [down(a * pair) for a in range(outer)]
        self.window_shifts = [a * pair - s for a, s in enumerate(self.window_starts)]
        self.take_width = max(up(s + pair) for s in self.window_shifts)
        self.window = up(pair)
        self.places = [b * block for b in range(inner)]
        self.block_window = max(up(p + block) - down(p) for p in self.places)
        self.block_starts = [min(down(p), self.window - self.block_window) for p in self.places]
        self.main = down(pair)
        self.rest = pair - self.main
        self.rest_each = LANES // self.rest if self.rest else 1
        self.rest_tiles = -(-m_local // self.rest_each) if self.rest else 0
        self.packed = m_local * self.main + self.rest_tiles * LANES


def far(x):
    return pltpu.with_memory_space_constraint(x, pltpu.HBM)


def rotate(x, axis, size, shift):
    return lax.ppermute(x, axis, [(i, (i + shift) % size) for i in range(size)])


def plain_grid(geo, grid_in, order_of, class_idx, land, class_weight, period):
    order_devices = grid_in.shape[0] // geo.outer
    m_local, rows, width = grid_in.shape[1:]
    orders = order_devices * m_local
    longitudes = class_idx.shape[1]
    stacked = grid_in.reshape(geo.outer, order_devices, m_local, rows, 2, width // 2)
    stacked = jnp.sum(stacked, axis=0).reshape(orders, rows, 2, width // 2)
    phases = order_of[:, None] * jnp.arange(period, dtype=jnp.int32)[None, :] % longitudes
    angles = phases.astype(jnp.float32) * (2.0 * math.pi / longitudes)
    harmonic = jnp.stack([jnp.cos(angles), jnp.sin(angles)])
    surface = jnp.einsum("mrsk,smp->rkp", stacked, harmonic, precision=HIGHEST)
    onehot = class_idx[:, :, None] == jnp.arange(class_weight.shape[0], dtype=jnp.int32)
    by_class = jnp.dot(onehot.astype(jnp.float32), class_weight, precision=HIGHEST)
    weight = jnp.where(land == 1, by_class[:, :, 1], by_class[:, :, 0])
    folded = jnp.sum(weight.reshape(rows, longitudes // period, period), axis=1)
    weighted = surface * folded[:, None, :]
    spectra = jnp.einsum("rkp,smp->mrsk", weighted, harmonic, precision=HIGHEST)
    each = m_local // geo.inner
    spectra = spectra * (2.0 / longitudes)
    spectra = spectra.reshape(order_devices, geo.inner, 1, each, rows, width)
    spectra = jnp.transpose(spectra, (1, 2, 0, 3, 4, 5))
    spectra = jnp.broadcast_to(
        spectra, (geo.inner, geo.outer, order_devices, each, rows, width)
    )
    return spectra.reshape(order_devices * geo.outer * geo.inner, each, rows, width)


def shards(
    outer,
    inner,
    position,
    residual,
    direction,
    legendre,
    order_of,
    class_idx,
    land,
    class_weight,
    damping,
):
    m_local, sin_cos, samples, deg_local = position.shape
    degrees, band_rows = legendre.shape[1:]
    rows_here, longitudes = class_idx.shape
    orders = order_of.shape[0]
    order_devices = orders // m_local
    devices = order_devices * outer * inner
    each = m_local // inner
    line = sin_cos * samples
    geo = Geometry(outer, inner, degrees, m_local)
    by_row = jnp.transpose(legendre, (0, 2, 1))
    cut = pltpu.VMEM((band_rows, geo.packed), jnp.float32)
    leg_moved = 4 * m_local * band_rows * degrees
    leg_scratch = [pltpu.VMEM(by_row.shape, jnp.float32), pltpu.SemaphoreType.DMA(())]
    cuts = call(
        functools.partial(cut_windows, geo),
        (cut,) * (outer - 1),
        [IN_HBM],
        m_local * band_rows * geo.window,
        8 * outer * m_local * band_rows * geo.window,
        [pltpu.VMEM(by_row.shape, jnp.float32), pltpu.SemaphoreType.DMA((m_local,))],
    )(far(by_row))
    received = [rotate(cuts[s - 1], "outer", outer, s) for s in range(1, outer)]
    stride = longitudes // (2 * orders)
    period = longitudes // stride if longitudes % stride == 0 else longitudes
    small = orders <= 16 and LANES % period == 0 and line == LANES and longitudes % period == 0
    if small:
        count = 2 * orders
        n = np.arange(count)[None, :]
        p = np.arange(LANES)[:, None]
        angle = 2.0 * math.pi * ((n * p) % period) / period
        basis = np.zeros((LANES, -(-2 * count // LANES) * LANES), np.float32)
        basis[:, :count] = np.cos(angle) / longitudes
        basis[:, count : 2 * count] = np.sin(angle) / longitudes
        tables = call(
            functools.partial(weight_tables, longitudes, period),
            jax.ShapeDtypeStruct((4, count, rows_here, LANES), jnp.float32),
            [WHOLE, WHOLE, SCALARS, WHOLE],
            1,
            8 * rows_here * longitudes,
            cost=1,
        )(class_idx, land, class_weight, jnp.asarray(basis))

    siblings = [rotate(direction, "inner", inner, s) for s in range(1, inner)]
    own_flops = 8 * m_local * line * geo.window * band_rows
    dir_window, own_rows, valid, *own_blocks = call(
        functools.partial(prepare, geo),
        (
            jax.ShapeDtypeStruct((m_local, 2 * line, geo.window), jnp.bfloat16),
            jax.ShapeDtypeStruct((m_local, band_rows, line), jnp.float32),
            jax.ShapeDtypeStruct((m_local, 8, deg_local), jnp.float32),
        )
        + (jax.ShapeDtypeStruct((m_local, band_rows, geo.block_window), jnp.float32),) * inner,
        [SCALARS, IN_HBM] + [WHOLE] * inner,
        1,
        8 * m_local * line * geo.window + leg_moved,
        leg_scratch,
        cost=1,
    )(order_of, far(by_row), direction, *siblings)
    first_legs = [own_blocks[0]]
    first_legs += [rotate(own_blocks[s], "inner", inner, s) for s in range(1, inner)]

    if small:
        received, tables = lax.optimization_barrier((received, tables))
    block = jax.ShapeDtypeStruct((outer - 1, m_local, band_rows, geo.block_window), jnp.float32)
    to_rows, *blocks = call(
        functools.partial(synthesise_rest, geo),
        (jax.ShapeDtypeStruct((outer, order_devices, m_local, rows_here, line), jnp.float32),)
        + (block,) * inner,
        [WHOLE] * (outer + 1),
        own_flops * (outer - 1),
        4 * m_local * (line + band_rows) * geo.window,
    )(own_rows, *received, dir_window)
    rest_legs = [blocks[0]]
    rest_legs += [rotate(blocks[s], "inner", inner, s) for s in range(1, inner)]
    grid_in = lax.all_to_all(
        to_rows.reshape(order_devices * outer, m_local, rows_here, line),
        ("outer", "order"),
        split_axis=0,
        concat_axis=0,
        tiled=True,
    )

    grid_in, first_legs, rest_legs = lax.optimization_barrier((grid_in, first_legs, rest_legs))
    if small:
        to_orders = call(
            functools.partial(grid_rows, geo, stride),
            jax.ShapeDtypeStruct((devices, each, rows_here, line), jnp.float32),
            [WHOLE, WHOLE, WHOLE],
            6 * orders * orders * rows_here * line,
            8 * orders * rows_here * line,
            [pltpu.VMEM((orders, rows_here, line), jnp.float32)] * 3,
        )(order_of[None, :], grid_in, tables)
    else:
        to_orders = plain_grid(geo, grid_in, order_of, class_idx, land, class_weight, period)
    spectra = lax.all_to_all(
        to_orders, ("inner", "outer", "order"), split_axis=0, concat_axis=0, tiled=True
    )
    shares = [spectra] + [rotate(spectra, "inner", inner, s) for s in range(1, inner)]
    coefficients = jax.ShapeDtypeStruct(position.shape, jnp.float32)
    part = (each,) + position.shape[1:]
    sums = ()
    applied = []
    for shift, share in enumerate(shares):
        if shift < inner - 1:
            sums_out = jax.ShapeDtypeStruct((4 * samples, LANES), jnp.float32)
        else:
            sums_out = jax.ShapeDtypeStruct((devices, 1, 4 * samples), jnp.float32)
        result, sums = call(
            functools.partial(project, geo, shift),
            (jax.ShapeDtypeStruct(part, jnp.float32), sums_out),
            [WHOLE] * (5 + 2 * inner + (shift > 0)),
            6 * each * line * geo.block_window * band_rows * outer * inner,
            16 * each * line * deg_local,
        )(
            valid,
            share,
            *first_legs,
            *rest_legs,
            direction,
            residual,
            damping[None, :],
            *((sums,) if shift else ()),
        )
        applied.append(result)
    sums = lax.all_to_all(
        sums, ("inner", "outer", "order"), split_axis=0, concat_axis=0, tiled=True
    )
    return call(
        functools.partial(update, geo),
        (coefficients,) * 3,
        [WHOLE] * (5 + inner),
        10 * m_local * line * deg_local,
        28 * m_local * line * deg_local,
        [pltpu.VMEM(position.shape, jnp.float32)] * 3
        + [pltpu.SemaphoreType.DMA((3, m_local, sin_cos))],
        IN_HBM,
    )(valid, sums, *applied, position, direction, residual)


def solution(mesh):
    order_devices, bands = mesh.shape["order"], mesh.shape["lat"]
    outer = 2 if bands % 2 == 0 else 1
    inner = bands // outer
    split = Mesh(mesh.devices.reshape(order_devices, outer, inner), ("order", "outer", "inner"))
    lat = ("outer", "inner")
    coefficients = P("order", None, None, lat)
    grid = P(("outer", "inner", "order"), None)
    return jax.shard_map(
        functools.partial(shards, outer, inner),
        mesh=split,
        in_specs=(
            coefficients,
            coefficients,
            coefficients,
            P("order", None, lat),
            P(),
            grid,
            grid,
            P(),
            P(lat),
        ),
        out_specs=(coefficients,) * 3,
        check_vma=False,
    )
```

```python
import functools
import math

import jax
import jax.numpy as jnp
import numpy as np
from jax import lax
from jax.experimental import pallas as pl
from jax.experimental.pallas import tpu as pltpu
from jax.sharding import Mesh
from jax.sharding import PartitionSpec as P

LANES = 128
HIGHEST = lax.Precision.HIGHEST
VMEM_LEAST = 16 * 1024 * 1024
VMEM_MOST = 48 * 1024 * 1024
WHOLE = pl.BlockSpec(memory_space=pltpu.VMEM)
SCALARS = pl.BlockSpec(memory_space=pltpu.SMEM)
IN_HBM = pl.BlockSpec(memory_space=pltpu.HBM)


def repeat(count, body):
    lax.fori_loop(0, count, lambda i, carry: (body(i), carry)[1], 0)


def split_bf16(x):
    hi = x.astype(jnp.bfloat16)
    lo = (x - hi.astype(jnp.float32)).astype(jnp.bfloat16)
    return hi, lo


def dot_pairs(a, b, dims, rows, columns):
    product = lax.dot_general(a, b, (dims, ((), ())), preferred_element_type=jnp.float32)
    low = product[:rows, columns:] + product[rows:, :columns]
    return product[:rows, :columns] + (low + product[rows:, columns:])


def params(moved):
    grant = min(VMEM_MOST, max(VMEM_LEAST, 3 * moved))
    return pltpu.CompilerParams(vmem_limit_bytes=grant)


def call(kernel, out_shape, in_specs, flops, moved, scratch=(), out_spec=WHOLE, cost=0):
    return pl.pallas_call(
        kernel,
        out_shape=out_shape,
        in_specs=in_specs,
        out_specs=jax.tree.map(lambda _: out_spec, out_shape),
        scratch_shapes=scratch,
        compiler_params=params(moved),
        cost_estimate=pl.CostEstimate(flops=flops, bytes_accessed=cost or moved, transcendentals=0),
    )


class Place:
    def __init__(self, geo, order_ref):
        self.geo = geo
        self.a, self.b = lax.axis_index("outer"), lax.axis_index("inner")
        self.first = lax.axis_index("order") * geo.m_local
        self.order_ref = order_ref

    def order(self, m):
        return self.order_ref[self.first + m]

    def outer(self, shift):
        return lax.rem(self.a + (self.geo.outer - shift), self.geo.outer)

    def inner(self, shift):
        return lax.rem(self.b + (self.geo.inner - shift), self.geo.inner)

    def among(self, table, b=None):
        index = self.a * self.geo.inner + (self.b if b is None else b)
        return choose(index, [value for row in table for value in row])


def choose(index, values):
    result = jnp.int32(values[0])
    for i, value in enumerate(values[1:], 1):
        result = jnp.where(index == i, jnp.int32(value), result)
    return result


def take(leg_ref, m, index, starts, width):
    degrees = leg_ref.shape[2]
    start = pl.multiple_of(choose(index, starts), LANES)
    last = None
    for i, first in enumerate(starts):
        first = first + width - LANES
        tile = leg_ref[m, :, first : min(first + LANES, degrees)]
        if tile.shape[1] < LANES:
            fill = jnp.zeros((tile.shape[0], LANES - tile.shape[1]), jnp.float32)
            tile = jnp.concatenate([tile, fill], axis=1)
        last = tile if last is None else jnp.where(index == i, tile, last)
    return jnp.concatenate([leg_ref[m, :, pl.ds(start, width - LANES)], last], axis=1)


def exact_window(geo, leg_ref, m, block):
    wide = take(leg_ref, m, block, geo.window_starts, geo.take_width)
    back = lax.rem(geo.take_width - choose(block, geo.window_shifts), geo.take_width)
    return pltpu.roll(wide, back, 1)[:, : geo.window]


def inner_block(geo, window, target):
    result = None
    for b, start in enumerate(geo.block_starts):
        piece = window[:, start : start + geo.block_window]
        result = piece if result is None else jnp.where(target == b, piece, result)
    return result


def cut_windows(geo, leg_hbm, *refs):
    send_refs, (leg_ref, sem) = refs[:-2], refs[-2:]
    fetch = pltpu.make_async_copy(leg_hbm, leg_ref, sem)
    fetch.start()
    a = lax.axis_index("outer")
    fetch.wait()
    m_local, rows = leg_ref.shape[:2]
    lane = lax.broadcasted_iota(jnp.int32, (rows, LANES), 1)
    for shift, ref in enumerate(send_refs, 1):
        block = lax.rem(a + shift, geo.outer)
        tiles = [None] * geo.rest_tiles
        for m in range(m_local):
            window = exact_window(geo, leg_ref, m, block)
            ref[:, m * geo.main : (m + 1) * geo.main] = window[:, : geo.main]
            if geo.rest:
                at, place = divmod(m, geo.rest_each)
                tile = jnp.where(lane < geo.rest, window[:, geo.main :], 0.0)
                if place:
                    tile = pltpu.roll(tile, place * geo.rest, 1)
                tiles[at] = tile if tiles[at] is None else tiles[at] + tile
        for i, tile in enumerate(tiles):
            start = m_local * geo.main + i * LANES
            ref[:, start : start + LANES] = tile


def unpack_window(geo, ref, m):
    window = ref[:, m * geo.main : (m + 1) * geo.main]
    if geo.rest:
        at, place = divmod(m, geo.rest_each)
        start = geo.m_local * geo.main + at * LANES
        tile = ref[:, start : start + LANES]
        if place:
            tile = pltpu.roll(tile, LANES - place * geo.rest, 1)
        window = jnp.concatenate([window, tile], axis=1)
    return window


def fold(x):
    rows, width = x.shape
    folded = None
    for start in range(0, width, LANES):
        piece = x[:, start : min(start + LANES, width)]
        if piece.shape[1] < LANES:
            fill = jnp.zeros((rows, LANES - piece.shape[1]), jnp.float32)
            piece = jnp.concatenate([piece, fill], axis=1)
        folded = piece if folded is None else folded + piece
    return folded


def to_line(folded):
    return jnp.sum(jnp.transpose(folded), axis=0, keepdims=True)


def prepare(geo, order_ref, leg_hbm, *refs):
    parts = refs[: geo.inner]
    out_ref, rows_ref, valid_ref, *cuts, leg_ref, sem = refs[geo.inner :]
    fetch = pltpu.make_async_copy(leg_hbm, leg_ref, sem)
    fetch.start()
    place = Place(geo, order_ref)
    m_local, sin_cos, samples, width = parts[0].shape
    window = out_ref.shape[2]
    line = sin_cos * samples
    start = place.a * geo.pair
    piece = 16
    steps = samples // piece
    shifts = [choose(place.inner(shift), geo.places) for shift in range(geo.inner)]
    degree = start + lax.broadcasted_iota(jnp.int32, (piece, window), 1)

    def one(i):
        m, rest = lax.div(i, sin_cos * steps), lax.rem(i, sin_cos * steps)
        s, k = lax.div(rest, steps), lax.rem(rest, steps) * piece
        total = None
        for shift, part in zip(shifts, parts):
            block = part[m, s, pl.ds(pl.multiple_of(k, piece), piece), :]
            fill = jnp.zeros((piece, window - width), jnp.float32)
            block = pltpu.roll(jnp.concatenate([block, fill], axis=1), shift, 1)
            total = block if total is None else total + block
        total = jnp.where(degree >= place.order(m), total, 0.0)
        hi, lo = split_bf16(total)
        at = rest * piece
        out_ref[m, pl.ds(pl.multiple_of(at, piece), piece)] = hi
        out_ref[m, pl.ds(pl.multiple_of(line + at, piece), piece)] = lo

    repeat(m_local * sin_cos * steps, one)
    own = place.among(geo.own_starts) + lax.broadcasted_iota(jnp.int32, valid_ref.shape[1:], 1)
    for m in range(m_local):
        valid_ref[m] = (own >= place.order(m)).astype(jnp.float32)
    fetch.wait()

    def rows(m):
        leg = exact_window(geo, leg_ref, m, place.a)
        rows_ref[m] = synthesis(leg, out_ref, m)
        for shift, ref in enumerate(cuts):
            ref[m] = inner_block(geo, leg, lax.rem(place.b + shift, geo.inner))

    repeat(m_local, rows)


def synthesis(leg, dir_ref, m):
    rows, line = leg.shape[0], dir_ref.shape[1] // 2
    halves = jnp.concatenate(split_bf16(leg), axis=0)
    return dot_pairs(halves, dir_ref[m], ((1,), (1,)), rows, line)


def synthesise_rest(geo, own_ref, *refs):
    others = geo.outer - 1
    legs, (dir_ref, out_ref, *cuts) = refs[:others], refs[others:]
    place = Place(geo, None)
    rows = out_ref.shape[3]

    def put(m, shift, part):
        a = place.outer(shift)
        for o in range(out_ref.shape[1]):
            out_ref[a, o, m] = part[o * rows : (o + 1) * rows]

    for m in range(own_ref.shape[0]):
        put(m, 0, own_ref[m])
        for shift in range(1, geo.outer):
            leg = unpack_window(geo, legs[shift - 1], m)
            put(m, shift, synthesis(leg, dir_ref, m))
            for ahead, ref in enumerate(cuts):
                ref[shift - 1, m] = inner_block(geo, leg, lax.rem(place.b + ahead, geo.inner))


def weight_tables(longitudes, period, class_ref, land_ref, value_ref, basis_ref, out_ref):
    classes = class_ref[...]
    on_land = land_ref[...] == 1
    weight = jnp.zeros(classes.shape, jnp.float32)
    for c in range(value_ref.shape[0]):
        value = jnp.where(on_land, value_ref[c, 1], value_ref[c, 0])
        weight = jnp.where(classes == c, value, weight)
    rows = classes.shape[0]
    folded = jnp.zeros((rows, LANES), jnp.float32)
    for start in range(0, longitudes, LANES):
        piece = weight[:, start : min(start + LANES, longitudes)]
        if piece.shape[1] < LANES:
            piece = jnp.concatenate(
                [piece, jnp.zeros((rows, LANES - piece.shape[1]), jnp.float32)], axis=1
            )
        folded = folded + piece
    moments = lax.dot_general(
        folded,
        basis_ref[...],
        (((1,), (0,)), ((), ())),
        precision=HIGHEST,
        preferred_element_type=jnp.float32,
    )
    lane = lax.broadcasted_iota(jnp.int32, (rows, LANES), 1)
    sign = jnp.where(lane < LANES // 2, 1.0, -1.0)
    count = out_ref.shape[1]
    for n in range(count):
        even = jnp.broadcast_to(moments[:, n : n + 1], (rows, LANES))
        odd = jnp.broadcast_to(moments[:, count + n : count + n + 1], (rows, LANES))
        out_ref[0, n] = even
        out_ref[1, n] = sign * even
        out_ref[2, n] = odd
        out_ref[3, n] = sign * odd


def grid_rows(geo, stride, order_ref, recv_ref, table_ref, out_ref, plain, swapped, done):
    orders = plain.shape[0]
    m_local, each = recv_ref.shape[1], out_ref.shape[1]
    order_devices = orders // m_local
    at = order_ref[...]
    slot = [lax.div(at[0, m], jnp.int32(stride)) for m in range(orders)]
    for m in range(orders):
        o, i = divmod(m, m_local)
        total = recv_ref[o, i]
        for a in range(1, geo.outer):
            total = total + recv_ref[a * order_devices + o, i]
        at = slot[m]
        plain[at] = total
        swapped[at] = pltpu.roll(total, LANES // 2, 1)
    for i in range(orders):
        total = None
        for j in range(orders):
            cos_part = table_ref[0, abs(i - j)] + table_ref[1, i + j]
            if i >= j:
                sin_part = table_ref[2, i + j] - table_ref[3, i - j]
            else:
                sin_part = table_ref[2, i + j] + table_ref[3, j - i]
            term = cos_part * plain[j] + sin_part * swapped[j]
            total = term if total is None else total + term
        done[i] = total
    for m in range(orders):
        o, i = divmod(m, m_local)
        b, i = divmod(i, each)
        value = done[slot[m]]
        for a in range(geo.outer):
            out_ref[(b * geo.outer + a) * order_devices + o, i] = value


def project(geo, shift, valid_ref, recv_ref, *refs):
    legs, refs = refs[: 2 * geo.inner], refs[2 * geo.inner :]
    dir_ref, res_ref, damp_ref = refs[:3]
    before_ref = refs[3] if shift else None
    app_ref, sums_ref = refs[-2:]
    place = Place(geo, None)
    each, sin_cos, samples, width = app_ref.shape
    first = place.inner(shift) * each
    window = geo.block_window
    copies = geo.outer * geo.inner
    order_devices = recv_ref.shape[0] // copies
    damping = damp_ref[...]
    rows = sin_cos * samples
    offsets = [p - s for p, s in zip(geo.places, geo.block_starts)]
    back = window - choose(place.b, offsets)

    def products(i):
        tiles, blocks = [], []
        for b in range(geo.inner):
            for a in range(geo.outer):
                band = place.inner(b) * geo.outer + place.outer(a)
                tile = recv_ref[pl.ds(band * order_devices, order_devices), i]
                tiles.append(tile.reshape(-1, tile.shape[2]))
                if a == 0:
                    blocks.append(legs[b][first + i])
                else:
                    blocks.append(legs[geo.inner + b][a - 1, first + i])
        hi, lo = split_bf16(jnp.concatenate(tiles, axis=0))
        high, low = split_bf16(jnp.concatenate(blocks, axis=0))
        dims = (((0,), (0,)), ((), ()))
        both = jnp.concatenate([hi, lo], axis=1)
        main = lax.dot_general(both, high, dims, preferred_element_type=jnp.float32)
        rest = lax.dot_general(hi, low, dims, preferred_element_type=jnp.float32)
        summed = main[:rows] + (main[rows:] + rest)
        summed = pltpu.roll(summed, back, 1)[:, :width]
        for s in range(sin_cos):
            app_ref[i, s] = summed[s * samples : (s + 1) * samples]

    repeat(each, products)

    def apply(at, sums):
        i, s = lax.div(at, sin_cos), lax.rem(at, sin_cos)
        valid = valid_ref[first + i, 0:1]
        direction = dir_ref[first + i, s] * valid
        residual = res_ref[first + i, s] * valid
        applied = app_ref[i, s] * valid + damping * direction
        app_ref[i, s] = applied
        terms = (
            residual * residual,
            direction * applied,
            residual * applied,
            applied * applied,
        )
        return tuple(old + fold(t) for old, t in zip(sums, terms))

    if shift:
        start = tuple(before_ref[i * samples : (i + 1) * samples] for i in range(4))
    else:
        start = (jnp.zeros((samples, LANES), jnp.float32),) * 4
    sums = lax.fori_loop(0, each * sin_cos, apply, start)
    stacked = jnp.concatenate(sums, axis=0)
    if shift < geo.inner - 1:
        sums_ref[...] = stacked
    else:
        line = to_line(stacked)

        def give(device):
            sums_ref[device] = line

        repeat(sums_ref.shape[0], give)


def update(geo, valid_ref, sums_ref, *refs):
    apps, refs = refs[: geo.inner], refs[geo.inner :]
    pos_ref, dir_ref, res_ref, *refs = refs
    outs, bufs, sems = refs[:3], refs[3:6], refs[6]
    place = Place(geo, None)
    m_local, sin_cos, samples, width = dir_ref.shape
    totals = jnp.sum(sums_ref[...], axis=0)
    before, curvature, cross, square = [
        totals[:, i * samples : (i + 1) * samples] for i in range(4)
    ]
    step_row = before / curvature
    after = before - 2.0 * step_row * cross + step_row * step_row * square
    ratio_row = after / before
    row = lax.broadcasted_iota(jnp.int32, (samples, samples), 0)
    column = lax.broadcasted_iota(jnp.int32, (samples, samples), 1)
    diagonal = row == column
    step = jnp.sum(jnp.where(diagonal, step_row, 0.0), axis=1, keepdims=True)
    ratio = jnp.sum(jnp.where(diagonal, ratio_row, 0.0), axis=1, keepdims=True)

    def copy(i, m, s):
        return pltpu.make_async_copy(bufs[i].at[m, s], outs[i].at[m, s], sems.at[i, m, s])

    each = m_local // geo.inner
    for shift, app_ref in enumerate(apps):

        def one(at, shift=shift, app_ref=app_ref):
            i, s = lax.div(at, sin_cos), lax.rem(at, sin_cos)
            m = place.inner(shift) * each + i
            valid = valid_ref[m, 0:1]
            direction = dir_ref[m, s] * valid
            residual = res_ref[m, s] * valid
            position = pos_ref[m, s] * valid
            new_residual = residual - step * app_ref[i, s]
            values = (
                position + step * direction,
                new_residual,
                new_residual + ratio * direction,
            )
            for i in range(3):
                bufs[i][m, s] = values[i]
                copy(i, m, s).start()

        repeat(each * sin_cos, one)

    def end(at):
        for i in range(3):
            copy(i, lax.div(at, sin_cos), lax.rem(at, sin_cos)).wait()

    repeat(m_local * sin_cos, end)


class Geometry:
    def __init__(self, outer, inner, degrees, m_local):
        self.outer, self.inner, self.m_local = outer, inner, m_local
        block = degrees // (outer * inner)

        def down(x):
            return x // LANES * LANES

        def up(x):
            return -(-x // LANES) * LANES

        pair = degrees // outer
        self.pair = pair
        self.own_starts = [[(a * inner + b) * block for b in range(inner)] for a in range(outer)]
        self.window_starts = [down(a * pair) for a in range(outer)]
        self.window_shifts = [a * pair - s for a, s in enumerate(self.window_starts)]
        self.take_width = max(up(s + pair) for s in self.window_shifts)
        self.window = up(pair)
        self.places = [b * block for b in range(inner)]
        self.block_window = max(up(p + block) - down(p) for p in self.places)
        self.block_starts = [min(down(p), self.window - self.block_window) for p in self.places]
        self.main = down(pair)
        self.rest = pair - self.main
        self.rest_each = LANES // self.rest if self.rest else 1
        self.rest_tiles = -(-m_local // self.rest_each) if self.rest else 0
        self.packed = m_local * self.main + self.rest_tiles * LANES


def far(x):
    return pltpu.with_memory_space_constraint(x, pltpu.HBM)


def rotate(x, axis, size, shift):
    return lax.ppermute(x, axis, [(i, (i + shift) % size) for i in range(size)])


def plain_grid(geo, grid_in, order_of, class_idx, land, class_weight, period):
    order_devices = grid_in.shape[0] // geo.outer
    m_local, rows, width = grid_in.shape[1:]
    orders = order_devices * m_local
    longitudes = class_idx.shape[1]
    stacked = grid_in.reshape(geo.outer, order_devices, m_local, rows, 2, width // 2)
    stacked = jnp.sum(stacked, axis=0).reshape(orders, rows, 2, width // 2)
    phases = order_of[:, None] * jnp.arange(period, dtype=jnp.int32)[None, :] % longitudes
    angles = phases.astype(jnp.float32) * (2.0 * math.pi / longitudes)
    harmonic = jnp.stack([jnp.cos(angles), jnp.sin(angles)])
    surface = jnp.einsum("mrsk,smp->rkp", stacked, harmonic, precision=HIGHEST)
    onehot = class_idx[:, :, None] == jnp.arange(class_weight.shape[0], dtype=jnp.int32)
    by_class = jnp.dot(onehot.astype(jnp.float32), class_weight, precision=HIGHEST)
    weight = jnp.where(land == 1, by_class[:, :, 1], by_class[:, :, 0])
    folded = jnp.sum(weight.reshape(rows, longitudes // period, period), axis=1)
    weighted = surface * folded[:, None, :]
    spectra = jnp.einsum("rkp,smp->mrsk", weighted, harmonic, precision=HIGHEST)
    each = m_local // geo.inner
    spectra = spectra * (2.0 / longitudes)
    spectra = spectra.reshape(order_devices, geo.inner, 1, each, rows, width)
    spectra = jnp.transpose(spectra, (1, 2, 0, 3, 4, 5))
    spectra = jnp.broadcast_to(
        spectra, (geo.inner, geo.outer, order_devices, each, rows, width)
    )
    return spectra.reshape(order_devices * geo.outer * geo.inner, each, rows, width)


def shards(
    outer,
    inner,
    position,
    residual,
    direction,
    legendre,
    order_of,
    class_idx,
    land,
    class_weight,
    damping,
):
    m_local, sin_cos, samples, deg_local = position.shape
    degrees, band_rows = legendre.shape[1:]
    rows_here, longitudes = class_idx.shape
    orders = order_of.shape[0]
    order_devices = orders // m_local
    devices = order_devices * outer * inner
    each = m_local // inner
    line = sin_cos * samples
    geo = Geometry(outer, inner, degrees, m_local)
    by_row = jnp.transpose(legendre, (0, 2, 1))
    cut = pltpu.VMEM((band_rows, geo.packed), jnp.float32)
    leg_moved = 4 * m_local * band_rows * degrees
    leg_scratch = [pltpu.VMEM(by_row.shape, jnp.float32), pltpu.SemaphoreType.DMA(())]
    cuts = call(
        functools.partial(cut_windows, geo),
        (cut,) * (outer - 1),
        [IN_HBM],
        m_local * band_rows * geo.window,
        8 * outer * m_local * band_rows * geo.window,
        leg_scratch,
    )(far(by_row))
    received = [rotate(cuts[s - 1], "outer", outer, s) for s in range(1, outer)]
    stride = longitudes // (2 * orders)
    period = longitudes // stride if longitudes % stride == 0 else longitudes
    small = orders <= 16 and LANES % period == 0 and line == LANES and longitudes % period == 0
    if small:
        count = 2 * orders
        n = np.arange(count)[None, :]
        p = np.arange(LANES)[:, None]
        angle = 2.0 * math.pi * ((n * p) % period) / period
        basis = np.zeros((LANES, -(-2 * count // LANES) * LANES), np.float32)
        basis[:, :count] = np.cos(angle) / longitudes
        basis[:, count : 2 * count] = np.sin(angle) / longitudes
        tables = call(
            functools.partial(weight_tables, longitudes, period),
            jax.ShapeDtypeStruct((4, count, rows_here, LANES), jnp.float32),
            [WHOLE, WHOLE, SCALARS, WHOLE],
            1,
            8 * rows_here * longitudes,
            cost=1,
        )(class_idx, land, class_weight, jnp.asarray(basis))

    siblings = [rotate(direction, "inner", inner, s) for s in range(1, inner)]
    own_flops = 8 * m_local * line * geo.window * band_rows
    dir_window, own_rows, valid, *own_blocks = call(
        functools.partial(prepare, geo),
        (
            jax.ShapeDtypeStruct((m_local, 2 * line, geo.window), jnp.bfloat16),
            jax.ShapeDtypeStruct((m_local, band_rows, line), jnp.float32),
            jax.ShapeDtypeStruct((m_local, 8, deg_local), jnp.float32),
        )
        + (jax.ShapeDtypeStruct((m_local, band_rows, geo.block_window), jnp.float32),) * inner,
        [SCALARS, IN_HBM] + [WHOLE] * inner,
        1,
        8 * m_local * line * geo.window + leg_moved,
        leg_scratch,
        cost=1,
    )(order_of, far(by_row), direction, *siblings)
    first_legs = [own_blocks[0]]
    first_legs += [rotate(own_blocks[s], "inner", inner, s) for s in range(1, inner)]

    if small:
        received, tables = lax.optimization_barrier((received, tables))
    block = jax.ShapeDtypeStruct((outer - 1, m_local, band_rows, geo.block_window), jnp.float32)
    to_rows, *blocks = call(
        functools.partial(synthesise_rest, geo),
        (jax.ShapeDtypeStruct((outer, order_devices, m_local, rows_here, line), jnp.float32),)
        + (block,) * inner,
        [WHOLE] * (outer + 1),
        own_flops * (outer - 1),
        4 * m_local * (line + band_rows) * geo.window,
    )(own_rows, *received, dir_window)
    rest_legs = [blocks[0]]
    rest_legs += [rotate(blocks[s], "inner", inner, s) for s in range(1, inner)]
    grid_in = lax.all_to_all(
        to_rows.reshape(order_devices * outer, m_local, rows_here, line),
        ("outer", "order"),
        split_axis=0,
        concat_axis=0,
        tiled=True,
    )

    grid_in, first_legs, rest_legs = lax.optimization_barrier((grid_in, first_legs, rest_legs))
    if small:
        to_orders = call(
            functools.partial(grid_rows, geo, stride),
            jax.ShapeDtypeStruct((devices, each, rows_here, line), jnp.float32),
            [WHOLE, WHOLE, WHOLE],
            6 * orders * orders * rows_here * line,
            8 * orders * rows_here * line,
            [pltpu.VMEM((orders, rows_here, line), jnp.float32)] * 3,
        )(order_of[None, :], grid_in, tables)
    else:
        to_orders = plain_grid(geo, grid_in, order_of, class_idx, land, class_weight, period)
    spectra = lax.all_to_all(
        to_orders, ("inner", "outer", "order"), split_axis=0, concat_axis=0, tiled=True
    )
    shares = [spectra] + [rotate(spectra, "inner", inner, s) for s in range(1, inner)]
    coefficients = jax.ShapeDtypeStruct(position.shape, jnp.float32)
    part = (each,) + position.shape[1:]
    sums = ()
    applied = []
    for shift, share in enumerate(shares):
        if shift < inner - 1:
            sums_out = jax.ShapeDtypeStruct((4 * samples, LANES), jnp.float32)
        else:
            sums_out = jax.ShapeDtypeStruct((devices, 1, 4 * samples), jnp.float32)
        result, sums = call(
            functools.partial(project, geo, shift),
            (jax.ShapeDtypeStruct(part, jnp.float32), sums_out),
            [WHOLE] * (5 + 2 * inner + (shift > 0)),
            6 * each * line * geo.block_window * band_rows * outer * inner,
            16 * each * line * deg_local,
        )(
            valid,
            share,
            *first_legs,
            *rest_legs,
            direction,
            residual,
            damping[None, :],
            *((sums,) if shift else ()),
        )
        applied.append(result)
    sums = lax.all_to_all(
        sums, ("order", "outer", "inner"), split_axis=0, concat_axis=0, tiled=True
    )
    return call(
        functools.partial(update, geo),
        (coefficients,) * 3,
        [WHOLE] * (5 + inner),
        10 * m_local * line * deg_local,
        28 * m_local * line * deg_local,
        [pltpu.VMEM(position.shape, jnp.float32)] * 3
        + [pltpu.SemaphoreType.DMA((3, m_local, sin_cos))],
        IN_HBM,
    )(valid, sums, *applied, position, direction, residual)


def solution(mesh):
    order_devices, bands = mesh.shape["order"], mesh.shape["lat"]
    outer = 2 if bands % 2 == 0 else 1
    inner = bands // outer
    split = Mesh(mesh.devices.reshape(order_devices, outer, inner), ("order", "outer", "inner"))
    lat = ("outer", "inner")
    coefficients = P("order", None, None, lat)
    grid = P(("outer", "inner", "order"), None)
    return jax.shard_map(
        functools.partial(shards, outer, inner),
        mesh=split,
        in_specs=(
            coefficients,
            coefficients,
            coefficients,
            P("order", None, lat),
            P(),
            grid,
            grid,
            P(),
            P(lat),
        ),
        out_specs=(coefficients,) * 3,
        check_vma=False,
    )
```
